32 devices in a mesh: dp: 8 (over z, y), mp: 4 (over x, core).
Axes of the slice: x: 2, y: 2, z: 4, core: 2. Of those that a mesh axis runs over, the one named last changes fastest.
Arguments:
- stream_in: bfloat16 [8192, 768], P('dp'), may hold values from -12 to 12
- features: bfloat16 [128, 257, 1408], P('dp'), may hold values from -6 to 6
- image_index: int32 [8, 16], P('dp'), may hold values from 0 to 15, each once within a row
- text_segment: int32 [32, 128], P('dp'), may hold values from 0 to 3, never falling along the last dimension, each value on 1 to 64 neighbouring positions
- text_valid: int32 [32, 128], P('dp'), may hold values 0 or 1
- self_qkv: bfloat16 [3, 768, 768], P(None, 'dp', 'mp'), may hold values from -0.21875 to 0.21875
- self_out: bfloat16 [768, 768], P('mp', 'dp'), may hold values from -1.25 to 1.25
- cross_q: bfloat16 [768, 768], P('dp', 'mp'), may hold values from -0.21875 to 0.21875
- cross_kv: bfloat16 [2, 1408, 768], P(None, 'dp', 'mp'), may hold values from -0.15625 to 0.15625
- cross_out: bfloat16 [768, 768], P('mp', 'dp'), may hold values from -1.75 to 1.75
- ffn_in: bfloat16 [2, 768, 3072], P(None, 'dp', 'mp'), may hold values from -0.21875 to 0.21875
- ffn_out: bfloat16 [2, 3072, 768], P(None, 'mp', 'dp'), may hold values from -0.109375 to 0.109375
- vectors: bfloat16 [10, 768], P(None, 'dp'), may hold values from -1.5 to 1.5
- head_bias: bfloat16 [4, 768], P(None, 'mp'), may hold values from -3 to 3
- ffn_bias: bfloat16 [2, 3072], P(None, 'mp'), may hold values from -3 to 3
- out_grad: bfloat16 [8192, 768], P('dp'), may hold values from -6 to 6
Outputs:
- out_stream: bfloat16 [8192, 768], P('dp')
- stream_grad: float32 [8192, 768], P('dp')
- grad_self_qkv: float32 [3, 768, 768], P(None, 'dp', 'mp')
- grad_self_out: float32 [768, 768], P('mp', 'dp')
- grad_cross_q: float32 [768, 768], P('dp', 'mp')
- grad_cross_kv: float32 [2, 1408, 768], P(None, 'dp', 'mp')
- grad_cross_out: float32 [768, 768], P('mp', 'dp')
- grad_ffn_in: float32 [2, 768, 3072], P(None, 'dp', 'mp')
- grad_ffn_out: float32 [2, 3072, 768], P(None, 'mp', 'dp')
- grad_vectors: float32 [10, 768], P(None, 'dp')
- grad_head_bias: float32 [4, 768], P(None, 'mp')
- grad_ffn_bias: float32 [2, 3072], P(None, 'mp')
- stream_rms: float32 [4], replicated
The draws below stay inside these ranges and needn't reach their ends.
Inputs may be any that keep to these rules, and one draw needn't show every extreme that they name: `image_index`: each dp shard's row names each of its 16 images once. `text_segment`: never falls along a row; every slot 0 to 3 appears in every row.
All inputs are finite; a program needn't handle non-finite values. No bound on the sum of `text_valid` on one device may be relied on, other than what follows from the above.
Results may differ from the reference program's by a relative error of at most 0.014.
Values may be sent and summed in bfloat16 or wider, within the bound.
A program may use at most 192 MiB of HBM per device.

```python
import math
import jax
import jax.numpy as jnp
import numpy as np
from jax import lax

D = 768
HEADS = 12
HEAD = 64
FF = 3072
DV = 1408
KEYS = 257
QUERIES = 32
SLOTS = 4
ROW_LEN = 256
ROWS_DEV = 4
ROWS = 32
TOKENS = 8192
TEXT = 128
IMG_DEV = 16
IMAGES = 128
N_DP = 8


def draw_stream_in(key, part):
    key = jax.random.fold_in(key, 11)
    position = jnp.arange(TOKENS, dtype=jnp.float32) / TOKENS
    base_draw = jnp.clip(jax.random.normal(key, (TOKENS, D), jnp.float32), -6.0, 6.0)
    row_scale = 0.6 * jnp.exp(jnp.log(10.0 / 3.0) * position)
    return (base_draw * row_scale[:, None]).astype(jnp.bfloat16)


def draw_vectors(key, part):
    key = jax.random.fold_in(key, 23)
    first_key, second_key = jax.random.split(key)
    gain_values = jax.random.uniform(first_key, (10, D), jnp.float32, 0.6, 1.4)
    shifts = 0.3 * jnp.clip(jax.random.normal(second_key, (10, D), jnp.float32), -5.0, 5.0)
    row_index = jnp.arange(10)[:, None]
    is_gain = (row_index < 6) & (row_index % 2 == 0)
    return jnp.where(is_gain, gain_values, shifts).astype(jnp.bfloat16)


def touch_ends(drawn, rng, smallest, largest):
    index_at = [jax.random.randint(jax.random.fold_in(rng, axis), (), 0, length) for axis, length in enumerate(drawn.shape)]
    widest = drawn.shape.index(max(drawn.shape))
    beside = index_at[:widest] + [(index_at[widest] + 1) % drawn.shape[widest]] + index_at[widest + 1:]
    return drawn.at[tuple(index_at)].set(smallest).at[tuple(beside)].set(largest)


def block_levels(rng, extent, cuts, smallest, largest):
    level = 1.0
    for axis_at, parts in cuts:
        heights = jax.random.uniform(jax.random.fold_in(jax.random.fold_in(rng, 6), axis_at), (parts,), jnp.float32, smallest / len(cuts), largest / len(cuts))
        level = level * jnp.repeat(jnp.exp(heights), extent[axis_at] // parts).reshape((-1,) + (1,) * (len(extent) - 1 - axis_at))
    return level


def length_profile(count, total, most, skew):
    weights = [(1 << 20) // math.isqrt(rank ** skew) + 1 for rank in range(2, count + 1)]
    spare, given = total - most - (count - 1), [1] * (count - 1)
    while spare > 0:
        movable = [i for i in range(count - 1) if given[i] < most]
        whole, left = sum([weights[i] for i in movable]), spare
        for i in movable:
            addition = min(most - given[i], max(1, left * weights[i] // whole), spare)
            given[i] = given[i] + addition
            spare = spare - addition
    return np.array([most] + given)


def ragged_sizes(rng, number_of, total, bound, skew):
    if number_of == 2:
        one = jax.random.randint(rng, (), max(1, total - bound), min(bound, total - 1) + 1)
        return jnp.stack([one, total - one])
    tallies = jnp.asarray(length_profile(number_of, total, bound, skew), jnp.int32)
    couples = (number_of - 1) // 2
    giver, receiver = tallies[1:1 + 2 * couples:2], tallies[2:2 + 2 * couples:2]
    room = jnp.minimum(giver - 1, bound - receiver)
    shifted = jax.random.randint(jax.random.fold_in(rng, 1), (couples,), 0, 1 << 20) % (room + 1)
    tallies = tallies.at[1:1 + 2 * couples:2].set(giver - shifted).at[2:2 + 2 * couples:2].set(receiver + shifted)
    return tallies[jax.random.permutation(jax.random.fold_in(rng, 2), number_of)]


def scatter_about(own_key, extent, width, bound, cuts=(), held_as=jnp.bfloat16):
    drawn = jax.random.normal(own_key, extent, jnp.float32) * width
    if len(cuts) > 0:
        drawn = block_levels(own_key, extent, cuts, -0.22, 0.18) * drawn
    return jnp.clip(drawn, min=-bound, max=bound).astype(held_as)


def setup_inputs(seed: int = 0) -> dict:
    key_list = jax.random.split(jax.random.key(seed), 17)
    return {
        "stream_in": draw_stream_in(jax.random.fold_in(key_list[16], 71), 0),
        "features": scatter_about(key_list[1], (IMAGES, KEYS, DV), 1.0, 6.0, ((0, 8),)),
        "image_index": jax.vmap(lambda own: jax.random.permutation(own, IMG_DEV))(jax.random.split(key_list[2], N_DP)).reshape((N_DP, IMG_DEV)).astype(jnp.int32),
        "text_segment": jax.vmap(lambda own: jnp.searchsorted(jnp.cumsum(ragged_sizes(own, SLOTS, TEXT, TEXT // 2, 0)), jnp.arange(TEXT), side="right"))(jax.random.split(key_list[3], ROWS)).reshape((ROWS, TEXT)).astype(jnp.int32),
        "text_valid": touch_ends((jax.random.randint(key_list[4], (ROWS, TEXT), 0, 8) < 7).astype(jnp.int32), jax.random.fold_in(key_list[4], 1), 0, 1),
        "self_qkv": scatter_about(key_list[5], (3, D, D), D ** -0.5, 0.21875, ((1, 8), (2, 4))),
        "self_out": scatter_about(key_list[6], (D, D), (D // 32) ** -0.5, 1.25, ((0, 4), (1, 8))),
        "cross_q": scatter_about(key_list[7], (D, D), D ** -0.5, 0.21875, ((0, 8), (1, 4))),
        "cross_kv": scatter_about(key_list[8], (2, DV, D), DV ** -0.5, 0.15625, ((1, 8), (2, 4))),
        "cross_out": scatter_about(key_list[9], (D, D), (D // 64) ** -0.5, 1.75, ((0, 4), (1, 8))),
        "ffn_in": scatter_about(key_list[10], (2, D, FF), D ** -0.5, 0.21875, ((1, 8), (2, 4))),
        "ffn_out": scatter_about(key_list[11], (2, FF, D), FF ** -0.5, 0.109375, ((1, 4), (2, 8))),
        "vectors": draw_vectors(jax.random.fold_in(key_list[16], 71), 0),
        "head_bias": scatter_about(key_list[13], (4, D), 0.5, 3.0, ((1, 4),)),
        "ffn_bias": scatter_about(key_list[14], (2, FF), 0.5, 3.0, ((1, 4),)),
        "out_grad": scatter_about(key_list[15], (TOKENS, D), 1.0, 6.0, ((0, 8),)),
    }


EPSILON = 1e-06
MASKED = -1e+30
PRECISE = lax.Precision.HIGHEST

@jax.custom_vjp
def low(v):
    return lax.optimization_barrier(v.astype(jnp.bfloat16)).astype(jnp.float32)

@jax.custom_vjp
def low_back(v):
    return v

def low_keep(v):
    return (low(v), None)

def low_pass(kept, grad):
    return (grad,)

def back_keep(v):
    return (v, None)

def back_low(kept, grad):
    return (low(grad),)
low.defvjp(low_keep, low_pass)
low_back.defvjp(back_keep, back_low)

def layer_norm(values, gain_row, shift_row):
    row_mean = lax.optimization_barrier(jnp.mean(values, axis=-1, keepdims=True))
    centred = values - row_mean
    row_var = lax.optimization_barrier(jnp.mean(centred * centred, axis=-1, keepdims=True))
    return centred * lax.rsqrt(row_var + EPSILON) * gain_row + shift_row

def dense(left_side, right_side):
    return jnp.matmul(left_side, right_side, precision=PRECISE)

def project(inputs, weight, bias_row):
    return low(low_back(dense(inputs, weight) + bias_row))

def softmax_rows(scores):
    row_max = lax.optimization_barrier(jnp.max(scores, axis=-1, keepdims=True))
    exponent = jnp.exp(scores - row_max)
    return exponent / lax.optimization_barrier(jnp.sum(exponent, axis=-1, keepdims=True))

def attention(queries, keys_in, values_in, key_mask):
    score_scale = queries.shape[-1] ** (-0.5)
    scores = jnp.einsum('bqhe,bkhe->bhqk', queries, keys_in, precision=PRECISE) * score_scale
    if key_mask is not None:
        scores = jnp.where(key_mask[:, None], scores, MASKED)
    attn_probs = low(softmax_rows(low_back(scores)))
    mixed_out = jnp.einsum('bhqk,bkhe->bqhe', attn_probs, values_in, precision=PRECISE)
    return low(low_back(mixed_out))

def feed_forward(normed, weight_in, bias_in, weight_out, bias_out):
    up_value = low_back(dense(normed, weight_in) + bias_in)
    hidden = low(jax.nn.gelu(up_value, approximate=False))
    return low_back(dense(hidden, weight_out) + bias_out)

def shard_layer(weights, stream, image_feats, image_perm, text_seg, text_ok):
    self_qkv, self_out, cross_q, cross_kv, cross_out, ffn_in, ffn_out, vectors, head_bias, ffn_bias = weights
    row_count = stream.shape[0] // ROW_LEN
    query_count = SLOTS * QUERIES
    query_segment = jnp.arange(query_count, dtype=jnp.int32) // QUERIES
    segment = jnp.concatenate([jnp.broadcast_to(query_segment, (row_count, query_count)), text_seg], axis=1)
    valid = jnp.concatenate([jnp.ones((row_count, query_count), jnp.int32), text_ok], axis=1) == 1
    key_mask = (segment[:, :, None] == segment[:, None, :]) & valid[:, None, :]
    heads_shape = (row_count, ROW_LEN, HEADS, HEAD)
    normed_low = low(layer_norm(stream, vectors[0], vectors[1]))
    self_query = project(normed_low, self_qkv[0], head_bias[0])
    self_key = low(low_back(dense(normed_low, self_qkv[1])))
    self_value = project(normed_low, self_qkv[2], head_bias[1])
    self_mixed = attention(self_query.reshape(heads_shape), self_key.reshape(heads_shape), self_value.reshape(heads_shape), key_mask).reshape(-1, D)
    after_self = stream + low_back(dense(self_mixed, self_out) + vectors[6])
    self_rows = after_self.reshape(row_count, ROW_LEN, D)
    query_part = self_rows[:, :query_count].reshape(-1, D)
    cross_normed = low(layer_norm(query_part, vectors[2], vectors[3]))
    cross_query = project(cross_normed, cross_q, head_bias[2])
    chosen = jnp.take(image_feats, image_perm, axis=0)
    cross_keys = low(low_back(jnp.einsum('nkf,fc->nkc', chosen, cross_kv[0], precision=PRECISE)))
    cross_values = low(low_back(jnp.einsum('nkf,fc->nkc', chosen, cross_kv[1], precision=PRECISE) + head_bias[3]))
    slot_count = row_count * SLOTS
    cross_mixed = attention(cross_query.reshape(slot_count, QUERIES, HEADS, HEAD), cross_keys.reshape(slot_count, KEYS, HEADS, HEAD), cross_values.reshape(slot_count, KEYS, HEADS, HEAD), None).reshape(-1, D)
    after_query = query_part + low_back(dense(cross_mixed, cross_out) + vectors[7])
    after_cross = jnp.concatenate([after_query.reshape(row_count, query_count, D), self_rows[:, query_count:]], axis=1).reshape(-1, D)
    ffn_normed = low(layer_norm(after_cross, vectors[4], vectors[5])).reshape(row_count, ROW_LEN, D)
    ffn_query = feed_forward(ffn_normed[:, :query_count].reshape(-1, D), ffn_in[0], ffn_bias[0], ffn_out[0], vectors[8])
    ffn_text = feed_forward(ffn_normed[:, query_count:].reshape(-1, D), ffn_in[1], ffn_bias[1], ffn_out[1], vectors[9])
    ffn_branch = jnp.concatenate([ffn_query.reshape(row_count, query_count, D), ffn_text.reshape(row_count, ROW_LEN - query_count, D)], axis=1).reshape(-1, D)
    after_ffn = after_cross + ffn_branch
    token_weight = valid.reshape(-1).astype(jnp.float32)
    stream_stats = jnp.stack([jnp.sum(token_weight * lax.optimization_barrier(jnp.sum(section * section, axis=1))) for section in (stream, after_self, after_cross, after_ffn)] + [jnp.sum(token_weight)])
    return (after_ffn, stream_stats)

def reference(stream_in, features, image_index, text_segment, text_valid, self_qkv, self_out, cross_q, cross_kv, cross_out, ffn_in, ffn_out, vectors, head_bias, ffn_bias, out_grad):
    weights = tuple((weight.astype(jnp.float32) for weight in (self_qkv, self_out, cross_q, cross_kv, cross_out, ffn_in, ffn_out, vectors, head_bias, ffn_bias)))
    shard_feats = features.reshape(N_DP, IMG_DEV, KEYS, DV)
    shard_seg = text_segment.reshape(N_DP, ROWS_DEV, TEXT)
    shard_valid = text_valid.reshape(N_DP, ROWS_DEV, TEXT)

    def forward(weights, stream):

        def one_shard(pieces):
            stream_part, feats_part, perm_part, seg_part, valid_part = pieces
            return shard_layer(weights, stream_part, feats_part.astype(jnp.float32), perm_part, seg_part, valid_part)
        outputs, stats = lax.map(jax.checkpoint(one_shard), (stream.reshape(N_DP, -1, D), shard_feats, image_index, shard_seg, shard_valid))
        return (outputs.reshape(-1, D), lax.optimization_barrier(jnp.sum(stats, axis=0)))
    after_ffn, pull_back, stats = jax.vjp(forward, weights, stream_in.astype(jnp.float32), has_aux=True)
    weight_grads, stream_grad = pull_back(out_grad.astype(jnp.float32))
    stream_rms = jnp.sqrt(stats[:4] / (stats[4] * D))
    return (after_ffn.astype(jnp.bfloat16), stream_grad, weight_grads[0], weight_grads[1], weight_grads[2], weight_grads[3], weight_grads[4], weight_grads[5], weight_grads[6], weight_grads[7], weight_grads[8], weight_grads[9], stream_rms)
```

```python
import functools

import jax
import jax.numpy as jnp
from jax import lax
from jax.experimental import pallas as pl
from jax.experimental.pallas import tpu as pltpu
from jax.sharding import PartitionSpec as P

HEAD = 64
KEYS = 257
QUERIES = 32
SLOTS = 4
ROW_LEN = 256


EPSILON = 1e-06
MASKED = -1e30
MESH = pl.DeviceIdType.MESH
VMEM_LIMIT = 56 * 2**20


def dp_place(count):
    index = lax.axis_index("dp")
    return index // 2, lax.rem(index, 2), lax.axis_index("mp"), count // 2


def dp_barrier(line, side, rank, lines):
    barrier = pltpu.get_barrier_semaphore()
    for step in range(1, lines):
        other = lax.rem(line + step, lines)
        pl.semaphore_signal(
            barrier, inc=1, device_id=(other * 2 + side, rank), device_id_type=MESH
        )
    pl.semaphore_signal(
        barrier, inc=1, device_id=(line * 2 + 1 - side, rank), device_id_type=MESH
    )
    pl.semaphore_wait(barrier, lines)


def gather_kernel(count, pieces, *refs):
    shards, wholes = refs[:pieces], refs[pieces : 2 * pieces]
    own_sem, line_send, line_recv, side_send, side_recv = refs[2 * pieces :]
    line, side, rank, lines = dp_place(count)
    index = line * 2 + side
    beside = (line * 2 + 1 - side, rank)
    dp_barrier(line, side, rank, lines)

    def to_side(piece, step, source, origin):
        return pltpu.make_async_remote_copy(
            src_ref=source,
            dst_ref=wholes[piece].at[origin],
            send_sem=side_send.at[piece, step],
            recv_sem=side_recv.at[piece, step],
            device_id=beside,
            device_id_type=MESH,
        )

    def along(piece, step):
        return pltpu.make_async_remote_copy(
            src_ref=shards[piece],
            dst_ref=wholes[piece].at[index],
            send_sem=line_send.at[piece, step],
            recv_sem=line_recv.at[piece, step],
            device_id=(lax.rem(line + step, lines) * 2 + side, rank),
            device_id_type=MESH,
        )

    for piece in range(pieces):
        pltpu.make_async_copy(shards[piece], wholes[piece].at[index], own_sem.at[piece]).start()
        for step in range(1, lines):
            along(piece, step).start()
        to_side(piece, 0, shards[piece], index).start()
    for piece in range(pieces):
        for step in range(1, lines):
            along(piece, step).wait_recv()
            origin = lax.rem(line - step + lines, lines) * 2 + side
            to_side(piece, step, wholes[piece].at[origin], origin).start()
    for piece in range(pieces):
        pltpu.make_async_copy(shards[piece], wholes[piece].at[index], own_sem.at[piece]).wait()
        for step in range(1, lines):
            along(piece, step).wait_send()
        for step in range(lines):
            to_side(piece, step, shards[piece], index).wait()


def gather_dp(shards, count):
    pieces = len(shards)
    lines = count // 2
    anywhere = pl.BlockSpec(memory_space=pl.ANY)
    return pl.pallas_call(
        functools.partial(gather_kernel, count, pieces),
        out_shape=[jax.ShapeDtypeStruct((count, *item.shape), item.dtype) for item in shards],
        in_specs=[anywhere] * pieces,
        out_specs=[anywhere] * pieces,
        scratch_shapes=[pltpu.SemaphoreType.DMA((pieces,))]
        + [pltpu.SemaphoreType.DMA((pieces, lines))] * 4,
        compiler_params=pltpu.CompilerParams(collective_id=0, has_side_effects=True),
    )(*shards)


def scatter_kernel(count, pieces, *refs):
    terms, owned = refs[:pieces], refs[pieces : 2 * pieces]
    side_in, pair, line_in = (
        refs[2 * pieces : 3 * pieces],
        refs[3 * pieces : 4 * pieces],
        refs[4 * pieces : 5 * pieces],
    )
    line_send, line_recv, side_send, side_recv = refs[5 * pieces :]
    line, side, rank, lines = dp_place(count)
    beside = (line * 2 + 1 - side, rank)
    dp_barrier(line, side, rank, lines)

    def to_side(piece, step):
        other = lax.rem(line + step, lines)
        return pltpu.make_async_remote_copy(
            src_ref=terms[piece].at[other * 2 + 1 - side],
            dst_ref=side_in[piece].at[step],
            send_sem=side_send.at[piece, step],
            recv_sem=side_recv.at[piece, step],
            device_id=beside,
            device_id_type=MESH,
        )

    def along(piece, step):
        return pltpu.make_async_remote_copy(
            src_ref=pair[piece].at[step],
            dst_ref=line_in[piece].at[step],
            send_sem=line_send.at[piece, step],
            recv_sem=line_recv.at[piece, step],
            device_id=(lax.rem(line + step, lines) * 2 + side, rank),
            device_id_type=MESH,
        )

    order = [*range(1, lines), 0]
    for piece in range(pieces):
        for step in order:
            to_side(piece, step).start()
    for piece in range(pieces):
        for step in order:
            to_side(piece, step).wait_recv()
            other = lax.rem(line + step, lines)
            total = terms[piece][other * 2 + side].astype(jnp.float32) + side_in[piece][
                step
            ].astype(jnp.float32)
            if step == 0:
                owned[piece][...] = total
            else:
                pair[piece][step] = total.astype(jnp.bfloat16)
                along(piece, step).start()
    for piece in range(pieces):
        for step in range(1, lines):
            along(piece, step).wait_recv()
            owned[piece][...] += line_in[piece][step].astype(jnp.float32)
    for piece in range(pieces):
        for step in range(1, lines):
            along(piece, step).wait_send()
        for step in range(lines):
            to_side(piece, step).wait_send()


def scatter_dp(terms, count):
    pieces = len(terms)
    lines = count // 2
    inside = pl.BlockSpec(memory_space=pltpu.VMEM)
    blocks = [item.shape[1:] for item in terms]
    slots = [pltpu.VMEM((lines, *block), jnp.bfloat16) for block in blocks]
    return pl.pallas_call(
        functools.partial(scatter_kernel, count, pieces),
        out_shape=[jax.ShapeDtypeStruct(block, jnp.float32) for block in blocks],
        in_specs=[inside] * pieces,
        out_specs=[inside] * pieces,
        scratch_shapes=slots * 3 + [pltpu.SemaphoreType.DMA((pieces, lines))] * 4,
        compiler_params=pltpu.CompilerParams(
            collective_id=1, has_side_effects=True, vmem_limit_bytes=VMEM_LIMIT
        ),
    )(*terms)


def total_kernel(part_ref, total_ref, pair_in, half, far_in, whole, send_sem, recv_sem):
    place, rank = lax.axis_index("dp"), lax.axis_index("mp")
    chip, core = rank // 2, lax.rem(rank, 2)
    beside, far = chip * 2 + 1 - core, (1 - chip) * 2 + core
    barrier = pltpu.get_barrier_semaphore()
    for other in (beside, far):
        pl.semaphore_signal(barrier, inc=1, device_id=(place, other), device_id_type=MESH)
    pl.semaphore_wait(barrier, 2)

    def copy(source, target, slot, other):
        return pltpu.make_async_remote_copy(
            src_ref=source,
            dst_ref=target,
            send_sem=send_sem.at[slot],
            recv_sem=recv_sem.at[slot],
            device_id=(place, other),
            device_id_type=MESH,
        )

    diagonal = (1 - chip) * 2 + 1 - core
    pair_far = copy(part_ref.at[diagonal], pair_in.at[1], 1, beside)
    pair_near = copy(part_ref.at[beside], pair_in.at[0], 0, beside)
    pair_far.start()
    pair_near.start()
    pair_far.wait_recv()
    half[...] = (
        part_ref[far].astype(jnp.float32) + pair_in[1].astype(jnp.float32)
    ).astype(jnp.bfloat16)
    across = copy(half, far_in, 2, far)
    across.start()
    pair_near.wait_recv()
    near_sum = part_ref[rank].astype(jnp.float32) + pair_in[0].astype(jnp.float32)
    across.wait_recv()
    whole[rank] = (near_sum + far_in[...].astype(jnp.float32)).astype(jnp.bfloat16)
    back_far = copy(whole.at[rank], whole.at[rank], 3, far)
    back_near = copy(whole.at[rank], whole.at[rank], 4, beside)
    back_far.start()
    back_near.start()
    total_ref[rank] = whole[rank].astype(jnp.float32)
    back_far.wait_recv()
    back_diagonal = copy(whole.at[far], whole.at[far], 5, beside)
    back_diagonal.start()
    total_ref[far] = whole[far].astype(jnp.float32)
    back_near.wait_recv()
    total_ref[beside] = whole[beside].astype(jnp.float32)
    back_diagonal.wait_recv()
    total_ref[diagonal] = whole[diagonal].astype(jnp.float32)
    for item in (pair_far, pair_near, across, back_far, back_near, back_diagonal):
        item.wait_send()


def total_mp(partial_terms, collective):
    ranks = lax.axis_size("mp")
    tokens, width = partial_terms.shape
    if ranks != 4 or tokens % 64:
        return lax.psum(partial_terms, "mp")
    block = (tokens // ranks, width)
    inside = pl.BlockSpec(memory_space=pltpu.VMEM)
    low = partial_terms.astype(jnp.bfloat16).reshape(ranks, *block)
    return pl.pallas_call(
        total_kernel,
        out_shape=jax.ShapeDtypeStruct((ranks, *block), jnp.float32),
        in_specs=[inside],
        out_specs=inside,
        scratch_shapes=[
            pltpu.VMEM((2, *block), jnp.bfloat16),
            pltpu.VMEM(block, jnp.bfloat16),
            pltpu.VMEM(block, jnp.bfloat16),
            pltpu.VMEM((ranks, *block), jnp.bfloat16),
            pltpu.SemaphoreType.DMA((6,)),
            pltpu.SemaphoreType.DMA((6,)),
        ],
        compiler_params=pltpu.CompilerParams(
            collective_id=2 + collective, has_side_effects=True, vmem_limit_bytes=VMEM_LIMIT
        ),
    )(low).reshape(tokens, width)


def pack_weights(self_qkv, self_out, cross_q, cross_kv, cross_out, ffn_in, ffn_out, vectors):
    fan, wide = ffn_in.shape[1], ffn_in.shape[2]
    return (
        jnp.pad(vectors, ((0, 6), (0, -vectors.shape[1] % 128))),
        jnp.concatenate([self_qkv[0], self_qkv[1], self_qkv[2], self_out.T], axis=1),
        jnp.concatenate([cross_kv[0], cross_kv[1]], axis=1),
        jnp.concatenate([cross_q, cross_out.T], axis=1),
        jnp.concatenate([ffn_in, ffn_out.transpose(0, 2, 1)], axis=0).reshape(4 * fan, wide),
    )


def gather_all(self_qkv, self_out, cross_q, cross_kv, cross_out, ffn_in, ffn_out, vectors):
    fan, own = ffn_in.shape[1], vectors.shape[1]
    shards = pack_weights(
        self_qkv, self_out, cross_q, cross_kv, cross_out, ffn_in, ffn_out, vectors
    )
    count = lax.axis_size("dp")
    if fan % 16 or count % 2:
        wholes = [lax.all_gather(item, "dp", axis=0) for item in shards]
    else:
        wholes = gather_dp(shards, count)
    vec_all, self_all, kv_all, cross_all, ffn_all = wholes
    return (
        vec_all[:, :10, :own].transpose(1, 0, 2).reshape(10, -1),
        self_all.reshape(-1, self_all.shape[-1]),
        kv_all.reshape(-1, kv_all.shape[-1]),
        cross_all.reshape(-1, cross_all.shape[-1]),
        ffn_all.reshape(count, 4, fan, -1).transpose(1, 0, 2, 3).reshape(4, count * fan, -1),
    )


def scatter_all(terms):
    count = lax.axis_size("dp")
    blocks = [item.astype(jnp.bfloat16).reshape(count, -1, item.shape[-1]) for item in terms]
    if any(item.shape[1] % 16 for item in blocks) or count % 2:
        return [lax.psum_scatter(item, "dp", scatter_dimension=0, tiled=True) for item in terms]
    return scatter_dp(blocks, count)


def layer_norm(values, gain_row, shift_row):
    row_mean = jnp.mean(values, axis=-1, keepdims=True)
    centred = values - row_mean
    row_var = jnp.mean(centred * centred, axis=-1, keepdims=True)
    return centred * lax.rsqrt(row_var + EPSILON) * gain_row + shift_row


def norm_back(values, gain_row, shift_row, grad_normed):
    pull_back = jax.vjp(layer_norm, values, gain_row, shift_row)[1]
    return pull_back(grad_normed)


def gelu_exact(values):
    return jax.nn.gelu(values, approximate=False)


def round_low(values):
    return values.astype(jnp.bfloat16)


def matmul(left_side, right_side):
    return jnp.dot(left_side, right_side, preferred_element_type=jnp.float32)


def matmul_left(left_side, right_side):
    return lax.dot_general(
        left_side, right_side, (((0,), (0,)), ((), ())), preferred_element_type=jnp.float32
    )


def matmul_right(left_side, right_side):
    return lax.dot_general(
        left_side, right_side, (((1,), (1,)), ((), ())), preferred_element_type=jnp.float32
    )


def column_sum(values):
    return jnp.sum(values.astype(jnp.float32), axis=0)


def attn_scores(queries, keys_in, key_mask):
    score_scale = queries.shape[-1] ** (-0.5)
    scores = (
        jnp.einsum("bqhe,bkhe->bhqk", queries, keys_in, preferred_element_type=jnp.float32)
        * score_scale
    )
    if key_mask is None:
        return scores
    return jnp.where(key_mask[:, None], scores, MASKED)


def attend(queries, keys_in, values_in, key_mask):
    scores = attn_scores(queries, keys_in, key_mask)
    row_max = jnp.max(scores, axis=-1, keepdims=True)
    exponent = jnp.exp(scores - row_max)
    row_total = jnp.sum(exponent, axis=-1, keepdims=True)
    attn_probs = round_low(exponent / row_total)
    mixed_out = jnp.einsum(
        "bhqk,bkhe->bqhe", attn_probs, values_in, preferred_element_type=jnp.float32
    )
    return (round_low(mixed_out), row_max + jnp.log(row_total))


def attend_back(queries, keys_in, values_in, key_mask, log_total, grad_mixed):
    score_scale = queries.shape[-1] ** (-0.5)
    attn_probs = jnp.exp(attn_scores(queries, keys_in, key_mask) - log_total)
    grad_values = jnp.einsum(
        "bhqk,bqhe->bkhe", round_low(attn_probs), grad_mixed, preferred_element_type=jnp.float32
    )
    grad_probs = jnp.einsum(
        "bqhe,bkhe->bhqk", grad_mixed, values_in, preferred_element_type=jnp.float32
    )
    row_delta = jnp.sum(attn_probs * grad_probs, axis=-1, keepdims=True)
    grad_scores = round_low(attn_probs * (grad_probs - row_delta))
    grad_queries = (
        jnp.einsum("bhqk,bkhe->bqhe", grad_scores, keys_in, preferred_element_type=jnp.float32)
        * score_scale
    )
    grad_keys = (
        jnp.einsum("bhqk,bqhe->bkhe", grad_scores, queries, preferred_element_type=jnp.float32)
        * score_scale
    )
    return (round_low(grad_queries), round_low(grad_keys), round_low(grad_values))


def ffn_forward(normed_low, weight_up, bias_up, weight_down):
    up_value = matmul(normed_low, weight_up) + bias_up
    hidden = round_low(gelu_exact(up_value))
    return (up_value, hidden, matmul_right(hidden, weight_down))


def ffn_back(normed_low, up_value, hidden, weight_up, weight_down, grad_low):
    grad_down = matmul_left(grad_low, hidden)
    grad_hidden = matmul(grad_low, weight_down)
    grad_up = round_low(jax.vjp(gelu_exact, up_value)[1](grad_hidden)[0])
    grad_in = matmul_left(normed_low, grad_up)
    return (grad_in, grad_down, column_sum(grad_up), matmul_right(grad_up, weight_up))


def body(
    stream_in,
    features,
    image_index,
    text_segment,
    text_valid,
    self_qkv,
    self_out,
    cross_q,
    cross_kv,
    cross_out,
    ffn_in,
    ffn_out,
    vectors,
    head_bias,
    ffn_bias,
    out_grad,
):
    vector_low, self_w, ckv_all, cross_w, ffn_w = gather_all(
        self_qkv, self_out, cross_q, cross_kv, cross_out, ffn_in, ffn_out, vectors
    )
    local = self_qkv.shape[2]
    qkv_w = [self_w[:, i * local : (i + 1) * local] for i in range(3)]
    proj_w = self_w[:, 3 * local :]
    cq_w, cproj_w = cross_w[:, :local], cross_w[:, local:]
    ckv_w = [ckv_all[:, :local], ckv_all[:, local:]]
    up_w, down_w = ffn_w[:2], ffn_w[2:]
    vecs = vector_low.astype(jnp.float32)
    bias_heads = head_bias.astype(jnp.float32)
    bias_hidden = ffn_bias.astype(jnp.float32)
    stream = stream_in.astype(jnp.float32)
    tokens, model_width = stream.shape
    row_count = tokens // ROW_LEN
    query_count = SLOTS * QUERIES
    text_len = ROW_LEN - query_count
    local_width = local
    local_heads = local_width // HEAD
    query_segment = jnp.arange(query_count, dtype=jnp.int32) // QUERIES
    segment = jnp.concatenate(
        [jnp.broadcast_to(query_segment, (row_count, query_count)), text_segment], axis=1
    )
    valid = (
        jnp.concatenate([jnp.ones((row_count, query_count), jnp.int32), text_valid], axis=1) == 1
    )
    key_mask = (segment[:, :, None] == segment[:, None, :]) & valid[:, None, :]
    heads_shape = (row_count, ROW_LEN, local_heads, HEAD)
    normed_low = round_low(layer_norm(stream, vecs[0], vecs[1]))
    self_query = round_low(matmul(normed_low, qkv_w[0]) + bias_heads[0]).reshape(heads_shape)
    self_key = round_low(matmul(normed_low, qkv_w[1])).reshape(heads_shape)
    self_value = round_low(matmul(normed_low, qkv_w[2]) + bias_heads[1]).reshape(heads_shape)
    self_mixed, self_total = attend(self_query, self_key, self_value, key_mask)
    self_mixed = self_mixed.reshape(tokens, local_width)
    self_term = matmul_right(self_mixed, proj_w).reshape(row_count, ROW_LEN, model_width)
    after_self = stream + total_mp(self_term.reshape(tokens, model_width), 0) + vecs[6]
    self_rows = after_self.reshape(row_count, ROW_LEN, model_width)
    query_part = self_rows[:, :query_count].reshape(-1, model_width)
    cross_normed = round_low(layer_norm(query_part, vecs[2], vecs[3]))
    slot_count = row_count * SLOTS
    cross_query = round_low(matmul(cross_normed, cq_w) + bias_heads[2]).reshape(
        slot_count, QUERIES, local_heads, HEAD
    )
    image_order = image_index.reshape(-1)
    pick_table = (image_order[:, None] == jnp.arange(image_order.shape[0])[None, :]).astype(
        jnp.bfloat16
    )
    keys_all = round_low(
        jnp.einsum("nkf,fc->nkc", features, ckv_w[0], preferred_element_type=jnp.float32)
    )
    values_all = round_low(
        jnp.einsum("nkf,fc->nkc", features, ckv_w[1], preferred_element_type=jnp.float32)
        + bias_heads[3]
    )
    cross_keys = round_low(
        jnp.einsum("ij,jkc->ikc", pick_table, keys_all, preferred_element_type=jnp.float32)
    )
    cross_values = round_low(
        jnp.einsum("ij,jkc->ikc", pick_table, values_all, preferred_element_type=jnp.float32)
    )
    cross_keys = cross_keys.reshape(slot_count, KEYS, local_heads, HEAD)
    cross_values = cross_values.reshape(slot_count, KEYS, local_heads, HEAD)
    cross_mixed, cross_total = attend(cross_query, cross_keys, cross_values, None)
    cross_mixed = cross_mixed.reshape(-1, local_width)
    cross_term = matmul_right(cross_mixed, cproj_w).reshape(row_count, query_count, model_width)
    after_query = query_part + total_mp(cross_term.reshape(-1, model_width), 1) + vecs[7]
    after_cross = jnp.concatenate(
        [after_query.reshape(row_count, query_count, model_width), self_rows[:, query_count:]],
        axis=1,
    ).reshape(tokens, model_width)
    ffn_normed = round_low(layer_norm(after_cross, vecs[4], vecs[5])).reshape(
        row_count, ROW_LEN, model_width
    )
    ffn_query = ffn_normed[:, :query_count].reshape(-1, model_width)
    ffn_text = ffn_normed[:, query_count:].reshape(-1, model_width)
    up_query, hidden_query, part_query = ffn_forward(ffn_query, up_w[0], bias_hidden[0], down_w[0])
    up_text, hidden_text, part_text = ffn_forward(ffn_text, up_w[1], bias_hidden[1], down_w[1])
    ffn_terms = jnp.concatenate(
        [
            part_query.reshape(row_count, query_count, model_width),
            part_text.reshape(row_count, text_len, model_width),
        ],
        axis=1,
    )
    query_flag = jnp.arange(ROW_LEN) < query_count
    bias_rows = jnp.where(query_flag[:, None], vecs[8], vecs[9])
    ffn_sum = total_mp(ffn_terms.reshape(tokens, model_width), 0).reshape(
        row_count, ROW_LEN, model_width
    )
    after_ffn = after_cross + (ffn_sum + bias_rows).reshape(tokens, model_width)
    token_weight = valid.reshape(-1).astype(jnp.float32)
    stream_stats = jnp.stack(
        [
            jnp.sum(token_weight * jnp.sum(section * section, axis=1))
            for section in (stream, after_self, after_cross, after_ffn)
        ]
        + [jnp.sum(token_weight)]
    )
    out_low = round_low(after_ffn)
    grad_out = out_grad.astype(jnp.float32)
    grad_out_rows = grad_out.reshape(row_count, ROW_LEN, model_width)
    grad_low = round_low(grad_out_rows)
    grad_low_query = grad_low[:, :query_count].reshape(-1, model_width)
    grad_low_text = grad_low[:, query_count:].reshape(-1, model_width)
    in_query, down_query, hidden_bias_query, normed_grad_query = ffn_back(
        ffn_query, up_query, hidden_query, up_w[0], down_w[0], grad_low_query
    )
    in_text, down_text, hidden_bias_text, normed_grad_text = ffn_back(
        ffn_text, up_text, hidden_text, up_w[1], down_w[1], grad_low_text
    )
    normed_grad_q = normed_grad_query.reshape(row_count, query_count, model_width)
    normed_grad_t = normed_grad_text.reshape(row_count, text_len, model_width)
    normed_grad = jnp.concatenate([normed_grad_q, normed_grad_t], axis=1)
    normed_grad = total_mp(normed_grad.reshape(tokens, model_width), 0)
    cross_back, gain_three, shift_three = norm_back(after_cross, vecs[4], vecs[5], normed_grad)
    grad_cross = grad_out + cross_back
    grad_cross_rows = grad_cross.reshape(row_count, ROW_LEN, model_width)
    grad_branch_cross = round_low(grad_cross_rows[:, :query_count].reshape(-1, model_width))
    grad_cproj = matmul_left(grad_branch_cross, cross_mixed)
    grad_cross_mixed = round_low(matmul(grad_branch_cross, cproj_w)).reshape(
        cross_query.shape
    )
    grad_cq_part, grad_ck_part, grad_cv_part = attend_back(
        cross_query, cross_keys, cross_values, None, cross_total, grad_cross_mixed
    )
    grad_cq_part = grad_cq_part.reshape(-1, local_width)
    grad_ck_all = round_low(
        jnp.einsum(
            "ij,ikc->jkc",
            pick_table,
            grad_ck_part.reshape(-1, KEYS, local_width),
            preferred_element_type=jnp.float32,
        )
    )
    grad_cv_all = round_low(
        jnp.einsum(
            "ij,ikc->jkc",
            pick_table,
            grad_cv_part.reshape(-1, KEYS, local_width),
            preferred_element_type=jnp.float32,
        )
    )
    grad_ckv = jnp.concatenate(
        [
            jnp.einsum("nkf,nkc->fc", features, grad_ck_all, preferred_element_type=jnp.float32),
            jnp.einsum("nkf,nkc->fc", features, grad_cv_all, preferred_element_type=jnp.float32),
        ],
        axis=1,
    )
    grad_cq = matmul_left(cross_normed, grad_cq_part)
    cross_grad_term = matmul_right(grad_cq_part, cq_w)
    cross_normed_grad = total_mp(cross_grad_term, 1)
    query_back, gain_two, shift_two = norm_back(query_part, vecs[2], vecs[3], cross_normed_grad)
    grad_self = jnp.concatenate(
        [
            grad_cross_rows[:, :query_count]
            + query_back.reshape(row_count, query_count, model_width),
            grad_cross_rows[:, query_count:],
        ],
        axis=1,
    ).reshape(tokens, model_width)
    grad_branch_self = round_low(grad_self)
    grad_proj = matmul_left(grad_branch_self, self_mixed)
    grad_self_mixed = round_low(matmul(grad_branch_self, proj_w)).reshape(heads_shape)
    grad_sq, grad_sk, grad_sv = attend_back(
        self_query, self_key, self_value, key_mask, self_total, grad_self_mixed
    )
    grad_sq = grad_sq.reshape(tokens, local_width)
    grad_sk = grad_sk.reshape(tokens, local_width)
    grad_sv = grad_sv.reshape(tokens, local_width)
    grad_self_w = jnp.concatenate(
        [
            matmul_left(normed_low, grad_sq),
            matmul_left(normed_low, grad_sk),
            matmul_left(normed_low, grad_sv),
            grad_proj,
        ],
        axis=1,
    )
    self_grad_term = (
        matmul_right(grad_sq, qkv_w[0])
        + matmul_right(grad_sk, qkv_w[1])
        + matmul_right(grad_sv, qkv_w[2])
    )
    normed_grad_self = total_mp(self_grad_term, 0)
    stream_back, gain_one, shift_one = norm_back(stream, vecs[0], vecs[1], normed_grad_self)
    stream_grad = grad_self + stream_back
    norm_rows = jnp.stack([gain_one, shift_one, gain_two, shift_two, gain_three, shift_three])
    grad_vectors = jnp.concatenate(
        [
            norm_rows,
            jnp.stack(
                [
                    column_sum(grad_branch_self),
                    column_sum(grad_branch_cross),
                    column_sum(grad_low_query),
                    column_sum(grad_low_text),
                ]
            ),
        ]
    )
    owned_self, owned_ckv, owned_cross, own_in, own_in_text, own_out, own_out_text = scatter_all(
        [
            grad_self_w,
            grad_ckv,
            jnp.concatenate([grad_cq, grad_cproj], axis=1),
            in_query,
            in_text,
            down_query,
            down_text,
        ]
    )
    owned = (
        jnp.stack([owned_self[:, i * local : (i + 1) * local] for i in range(3)]),
        owned_self[:, 3 * local :].T,
        owned_cross[:, :local],
        jnp.stack([owned_ckv[:, :local], owned_ckv[:, local:]]),
        owned_cross[:, local:].T,
        jnp.stack([own_in, own_in_text]),
        jnp.stack([own_out.T, own_out_text.T]),
        lax.psum_scatter(grad_vectors, "dp", scatter_dimension=1, tiled=True),
    )
    grad_heads = jnp.stack(
        [
            column_sum(grad_sq),
            column_sum(grad_sv),
            column_sum(grad_cq_part),
            jnp.sum(grad_cv_part.astype(jnp.float32), axis=(0, 1)).reshape(-1),
        ]
    )
    grad_hidden_bias = jnp.stack([hidden_bias_query, hidden_bias_text])
    grad_heads, grad_hidden_bias, stream_stats = lax.psum(
        (grad_heads, grad_hidden_bias, stream_stats), "dp"
    )
    stream_rms = jnp.sqrt(stream_stats[:4] / (stream_stats[4] * model_width))
    return (
        out_low,
        stream_grad,
        owned[0],
        owned[1],
        owned[2],
        owned[3],
        owned[4],
        owned[5],
        owned[6],
        owned[7],
        grad_heads,
        grad_hidden_bias,
        stream_rms,
    )


def solution(mesh):
    in_specs = (
        P("dp", None),
        P("dp", None, None),
        P("dp", None),
        P("dp", None),
        P("dp", None),
        P(None, "dp", "mp"),
        P("mp", "dp"),
        P("dp", "mp"),
        P(None, "dp", "mp"),
        P("mp", "dp"),
        P(None, "dp", "mp"),
        P(None, "mp", "dp"),
        P(None, "dp"),
        P(None, "mp"),
        P(None, "mp"),
        P("dp", None),
    )
    out_specs = (
        P("dp", None),
        P("dp", None),
        P(None, "dp", "mp"),
        P("mp", "dp"),
        P("dp", "mp"),
        P(None, "dp", "mp"),
        P("mp", "dp"),
        P(None, "dp", "mp"),
        P(None, "mp", "dp"),
        P(None, "dp"),
        P(None, "mp"),
        P(None, "mp"),
        P(),
    )
    return jax.shard_map(body, mesh=mesh, in_specs=in_specs, out_specs=out_specs, check_vma=False)
```

```python
import functools
import math
import types

import jax
import jax.numpy as jnp
from jax import lax
from jax.experimental import pallas as pl
from jax.experimental.pallas import tpu as pltpu
from jax.sharding import PartitionSpec as P

HEAD = 64
KEYS = 257
QUERIES = 32
SLOTS = 4
ROW_LEN = 256


EPSILON = 1e-06
MASKED = -1e30
MESH = pl.DeviceIdType.MESH
VMEM_LIMIT = 62 * 2**20
BF16 = jnp.bfloat16
F32 = jnp.float32
PIECES = ("vec", "self", "kv", "cross", "in1", "out1", "in0", "out0")
TERMS = ("in1", "out1", "in0", "out0", "cross", "kv", "self")
SUMS = ("self", "cross", "gft", "gfq", "out", "gc", "ga")
SHARES = ("c", "ft", "fq", "gca", "gsat", "gsaq", "out", "sg")
WIDE = 256
CHUNK = 256
CHUNKS_HELD = 3
PADDED_KEYS = 272


def dot(left, right):
    return jnp.dot(left, right, preferred_element_type=F32)


def dot_rows(left, right):
    return lax.dot_general(left, right, (((0,), (0,)), ((), ())), preferred_element_type=F32)


def dot_columns(left, right):
    return lax.dot_general(left, right, (((1,), (1,)), ((), ())), preferred_element_type=F32)


def norm_parts(values):
    centred = values - jnp.mean(values, axis=-1, keepdims=True)
    scale = lax.rsqrt(jnp.mean(centred * centred, axis=-1, keepdims=True) + EPSILON)
    return centred * scale, scale


def norm_grad(normed, scale, gain, grad):
    scaled = grad * gain
    return scale * (
        scaled
        - jnp.mean(scaled, axis=-1, keepdims=True)
        - normed * jnp.mean(scaled * normed, axis=-1, keepdims=True)
    )


def lanes(width):
    return lax.broadcasted_iota(jnp.int32, (1, width), 1)


def of_head(head):
    lane = lanes(WIDE)
    return (lane >= head * HEAD) & (lane < (head + 1) * HEAD)


def spread(values, heads):
    return jnp.concatenate(
        [jnp.where(of_head(head), values, jnp.zeros_like(values)) for head in range(heads)], axis=0
    )


def fold(values, heads, tokens):
    total = jnp.where(of_head(0), values[:tokens], 0.0)
    for head in range(1, heads):
        total = total + jnp.where(of_head(head), values[head * tokens : (head + 1) * tokens], 0.0)
    return total


def softmax(scores):
    exponent = jnp.exp(scores - jnp.max(scores, axis=-1, keepdims=True))
    return exponent * (1.0 / jnp.sum(exponent, axis=-1, keepdims=True))


def pack_columns(items, axis):
    cut = items[0].shape[axis] // 128 * 128
    first = [lax.slice_in_dim(item, 0, cut, axis=axis) for item in items]
    last = [lax.slice_in_dim(item, cut, item.shape[axis], axis=axis) for item in items]
    return jnp.concatenate(first + last, axis=axis)


def unpack_columns(packed, count, width):
    cut = width // 128 * 128
    rest = width - cut
    return [
        jnp.concatenate(
            [
                packed[:, i * cut : (i + 1) * cut],
                packed[:, count * cut + i * rest : count * cut + (i + 1) * rest],
            ],
            axis=1,
        )
        for i in range(count)
    ]


def widen(packed, wide, count):
    low = lanes(128) < HEAD
    for i in range(count):
        at = (count + i // 2) * 128
        tail = packed[:, at : at + 128]
        if i % 2:
            tail = pltpu.roll(tail, HEAD, 1)
        wide[:, i * WIDE : i * WIDE + 128] = packed[:, i * 128 : (i + 1) * 128]
        wide[:, i * WIDE + 128 : (i + 1) * WIDE] = jnp.where(low, tail, jnp.zeros_like(tail))


def layer_kernel(names, sizes, *refs):
    s = types.SimpleNamespace(**dict(zip(names, refs)))
    z = sizes
    count, lines, rows, length, query, width, heads = (
        z.count,
        z.count // 2,
        z.rows,
        ROW_LEN,
        SLOTS * QUERIES,
        z.width,
        z.heads,
    )
    text = length - query
    place, rank = lax.axis_index("dp"), lax.axis_index("mp")
    line, side = place // 2, lax.rem(place, 2)
    chip, core = rank // 2, lax.rem(rank, 2)
    beside = chip * 2 + 1 - core
    far = (1 - chip) * 2 + core
    diagonal = (1 - chip) * 2 + 1 - core

    def remote(source, target, sems, index, device):
        return pltpu.make_async_remote_copy(
            src_ref=source,
            dst_ref=target,
            send_sem=sems[0].at[index],
            recv_sem=sems[1].at[index],
            device_id=device,
            device_id_type=MESH,
        )

    def along(step):
        return (lax.rem(line + step, lines) * 2 + side, rank)

    across = (line * 2 + 1 - side, rank)

    def block(ref, index, size):
        return ref.at[pl.ds(pl.multiple_of(index * size, 16), size)]

    fan, feat_fan = z.fan, z.feat_fan
    shard = {
        "vec": s.vec_h,
        "self": s.self_h,
        "kv": s.kv_h,
        "cross": s.cross_h,
        "in0": s.ffn_h.at[pl.ds(0, fan)],
        "in1": s.ffn_h.at[pl.ds(fan, fan)],
        "out0": s.ffn_h.at[pl.ds(2 * fan, fan)],
        "out1": s.ffn_h.at[pl.ds(3 * fan, fan)],
    }
    whole = {
        "vec": s.w_vec,
        "self": s.m_self,
        "kv": s.m_kv,
        "cross": s.m_cross,
        "in0": s.m_in0,
        "in1": s.m_in1,
        "out0": s.m_out0,
        "out1": s.m_out1,
    }
    size = {name: fan for name in PIECES} | {"vec": 16, "kv": feat_fan}

    def gather_own(name):
        p = PIECES.index(name)
        return pltpu.make_async_copy(
            shard[name], block(whole[name], place, size[name]), s.own_sem.at[p]
        )

    def gather_line(name, step):
        return remote(
            shard[name],
            block(whole[name], place, size[name]),
            (s.gl_send, s.gl_recv),
            (PIECES.index(name), step),
            along(step),
        )

    def gather_side(name, step):
        origin = lax.rem(line - step + lines, lines) * 2 + side
        target = block(whole[name], origin, size[name])
        return remote(
            shard[name] if step == 0 else target,
            target,
            (s.gs_send, s.gs_recv),
            (PIECES.index(name), step),
            across,
        )

    def gather_start(name):
        gather_own(name).start()
        for step in range(1, lines):
            gather_line(name, step).start()
        gather_side(name, 0).start()

    def gather_forward(name):
        for step in range(1, lines):
            gather_line(name, step).wait_recv()
            gather_side(name, step).start()

    def gather_finish(name):
        gather_own(name).wait()
        for step in range(lines):
            gather_side(name, step).wait_recv()

    def gather_sent(name):
        for step in range(1, lines):
            gather_line(name, step).wait_send()
        for step in range(lines):
            gather_side(name, step).wait_send()

    side_in = {name: getattr(s, "y_" + name) for name in TERMS}
    line_in = {name: getattr(s, "z_" + name) for name in TERMS}
    owned = {
        "self": s.own_self,
        "kv": s.own_kv,
        "cross": s.own_cross,
        "in0": s.own_ffn.at[pl.ds(0, fan)],
        "in1": s.own_ffn.at[pl.ds(fan, fan)],
        "out0": s.own_ffn.at[pl.ds(2 * fan, fan)],
        "out1": s.own_ffn.at[pl.ds(3 * fan, fan)],
    }
    order = [*range(1, lines), 0]

    def scatter_side(name, step):
        other = lax.rem(line + step, lines)
        return remote(
            block(whole[name], other * 2 + 1 - side, size[name]),
            side_in[name].at[step],
            (s.ss_send, s.ss_recv),
            (TERMS.index(name), step),
            across,
        )

    def scatter_line(name, step):
        other = lax.rem(line + step, lines)
        return remote(
            block(whole[name], other * 2 + side, size[name]),
            line_in[name].at[step - 1],
            (s.sl_send, s.sl_recv),
            (TERMS.index(name), step),
            along(step),
        )

    def scatter_start(name):
        for step in order:
            scatter_side(name, step).start()

    def scatter_forward(name):
        for step in range(1, lines):
            other = lax.rem(line + step, lines)
            mine = block(whole[name], other * 2 + side, size[name])
            scatter_side(name, step).wait_recv()
            mine[...] = (mine[...].astype(F32) + side_in[name][step].astype(F32)).astype(BF16)
            scatter_line(name, step).start()

    def scatter_finish(name):
        scatter_side(name, 0).wait_recv()
        total = block(whole[name], place, size[name])[...].astype(F32)
        total = total + side_in[name][0].astype(F32)
        for step in range(1, lines):
            scatter_line(name, step).wait_recv()
            total = total + line_in[name][step - 1].astype(F32)
        owned[name][...] = total
        for step in range(1, lines):
            scatter_line(name, step).wait_send()
        for step in range(lines):
            scatter_side(name, step).wait_send()

    def sum_buffers(name):
        landed = {"ga": "self", "gc": "cross"}.get(name, name)
        half = {"gft": s.half_t, "self": s.half_row, "out": s.half_row, "ga": s.half_row}
        return getattr(s, "pin_" + landed), half.get(name, s.half_q), getattr(s, "fin_" + landed)

    def sum_copy(name, hop):
        part = parts[name]
        pair_in, half, far_in = sum_buffers(name)
        source, target, device = (
            (part.at[diagonal], pair_in.at[1], beside),
            (part.at[beside], pair_in.at[0], beside),
            (half, far_in, far),
        )[hop]
        return remote(
            source, target, (s.sum_send, s.sum_recv), (SUMS.index(name), hop), (place, device)
        )

    parts = {
        "self": s.part_row,
        "cross": s.part_q,
        "gft": s.part_t,
        "gfq": s.part_q,
        "out": s.part_row,
        "gc": s.part_q,
        "ga": s.part_row,
    }

    def sum_forward(name):
        sum_copy(name, 0).wait_recv()
        pair_in, half, _ = sum_buffers(name)
        half[...] = (parts[name][far].astype(F32) + pair_in[1].astype(F32)).astype(BF16)
        sum_copy(name, 2).start()

    def sum_finish(name):
        sum_copy(name, 1).wait_recv()
        sum_copy(name, 2).wait_recv()
        pair_in, _, far_in = sum_buffers(name)
        total = parts[name][rank].astype(F32) + pair_in[0].astype(F32)
        return total + far_in[...].astype(F32)

    def sum_sent(name):
        for hop in range(3):
            sum_copy(name, hop).wait_send()

    shared = {
        "c": s.c,
        "ft": s.f_t,
        "fq": s.f_q,
        "gca": s.f_t,
        "gsat": s.gsa_t,
        "gsaq": s.f_q,
        "out": s.gy,
        "sg": s.x,
    }

    def share_copy(name, hop):
        ref = shared[name]
        index, device = ((rank, far), (rank, beside), (far, beside))[hop]
        return remote(
            ref.at[index],
            ref.at[index],
            (s.share_send, s.share_recv),
            (SHARES.index(name), hop),
            (place, device),
        )

    def share_start(name):
        share_copy(name, 0).start()
        share_copy(name, 1).start()

    def share_forward(name):
        share_copy(name, 0).wait_recv()
        share_copy(name, 2).start()

    def share_finish(name):
        share_copy(name, 1).wait_recv()
        share_copy(name, 2).wait_recv()

    def share_sent(name):
        for hop in range(3):
            share_copy(name, hop).wait_send()

    def vec(index):
        return s.vecs[index : index + 1, :]

    def column_total(values):
        return jnp.sum(values.astype(F32), axis=0, keepdims=True)

    def row_at(row):
        return pl.ds(pl.multiple_of(row * length, length), length)

    def put_stat(index, values, weight):
        total = jnp.sum(
            jnp.sum(values * values, axis=1, keepdims=True) * weight, axis=0, keepdims=True
        )
        s.small[10:11, :] += jnp.where(lanes(z.model) == index, total, 0.0)

    load_x = pltpu.make_async_copy(s.x_h, s.x, s.load_sem.at[0])
    load_gy = pltpu.make_async_copy(s.gy_h, s.gy, s.load_sem.at[1])
    load_x.start()
    barrier = pltpu.get_barrier_semaphore()
    partners = [along(step) for step in range(1, lines)] + [
        across,
        (place, beside),
        (place, far),
    ]
    for partner in partners:
        pl.semaphore_signal(barrier, inc=1, device_id=partner, device_id_type=MESH)
    pl.semaphore_wait(barrier, len(partners))
    gather_start("vec")
    gather_start("self")
    gather_start("kv")
    load_gy.start()

    chunk_count = z.features // CHUNK
    tail = z.features - chunk_count * CHUNK

    def load_chunk(index):
        slot = lax.rem(index, CHUNKS_HELD)
        return pltpu.make_async_copy(
            s.feat_h.at[pl.ds(pl.multiple_of(index * CHUNK, CHUNK), CHUNK)],
            s.chunk.at[slot],
            s.chunk_sem.at[slot],
        )

    load_tail = pltpu.make_async_copy(
        s.feat_h.at[pl.ds(chunk_count * CHUNK, tail)], s.tail, s.load_sem.at[2]
    )
    for index in range(CHUNKS_HELD):
        load_chunk(index).start()
    load_tail.start()

    s.small[...] = jnp.zeros_like(s.small)
    gather_forward("vec")
    gather_finish("vec")
    own = z.model // count
    for index in range(count):
        s.vecs[:, index * own : (index + 1) * own] = s.w_vec[
            index * 16 : (index + 1) * 16, :own
        ].astype(F32)
    load_x.wait()

    @pl.loop(0, rows)
    def _(row):
        normed, _ = norm_parts(s.x[row].astype(F32))
        s.a[row_at(row), :] = (normed * vec(0) + vec(1)).astype(BF16)

    s.x_own[...] = s.x[rank]
    weight_own = s.weight[...]
    weight_query, weight_text = weight_own[:query], weight_own[query:]
    s.small[10:11, :] += jnp.where(
        lanes(z.model) == 4, jnp.sum(weight_own, axis=0, keepdims=True), 0.0
    )
    put_stat(0, s.x_own[...].astype(F32), weight_own)

    gather_forward("self")
    gather_start("cross")
    gather_finish("self")
    widen(s.m_self, s.w_self, 4)

    def self_mask(row):
        return s.query_code[row_at(row), :] == s.key_code[pl.ds(row, 1), :]

    def send_order(step):
        chip_at = chip + (1 - 2 * chip) * (1 - step // 2)
        core_at = core + (1 - 2 * core) * (1 - lax.rem(step, 2))
        return chip_at * 2 + core_at

    @pl.loop(0, rows)
    def _(step):
        row = send_order(step)
        at = row_at(row)
        qkv = dot(s.a[at, :], s.w_self[:, : 3 * WIDE]) + s.bias[0:1, :]
        low = qkv.astype(BF16)
        s.qkv[at, :] = low
        queries = spread(low[:, :WIDE] * jnp.asarray(z.scale, BF16), heads)
        scores = dot_columns(queries, low[:, WIDE : 2 * WIDE])
        mask = self_mask(row)
        scores = jnp.concatenate(
            [
                jnp.where(mask, scores[head * length : (head + 1) * length], MASKED)
                for head in range(heads)
            ],
            axis=0,
        )
        probs = softmax(scores).astype(BF16)
        s.p_self[row] = probs
        mixed = fold(dot(probs, low[:, 2 * WIDE :]), heads, length).astype(BF16)
        s.o[at, :] = mixed
        s.part_row[row] = dot_columns(mixed, s.w_self[:, 3 * WIDE :]).astype(BF16)

        @pl.when(step == 0)
        def _():
            sum_copy("self", 0).start()

        @pl.when(step == 2)
        def _():
            sum_copy("self", 1).start()

    sum_forward("self")
    gather_forward("kv")
    gather_start("in1")
    gather_start("out1")
    gather_finish("kv")
    widen(s.m_kv, s.w_kv, 2)

    def project(values):
        return dot(values, s.w_kv[...]) + s.bias[2:3, : 2 * WIDE]

    def project_chunk(index):
        load_chunk(index).wait()
        result = project(s.chunk[lax.rem(index, CHUNKS_HELD)])

        @pl.when(index + CHUNKS_HELD < chunk_count)
        def _():
            load_chunk(index + CHUNKS_HELD).start()

        for tile in range(2 * WIDE // 128):
            s.stage[tile // 2, (tile % 2) * CHUNK : (tile % 2 + 1) * CHUNK, :] = result[
                :, tile * 128 : (tile + 1) * 128
            ]
        keys = CHUNK // z.images
        key_at = pl.ds(pl.multiple_of(index * keys, keys), keys)
        for image in range(z.images):
            for tile in range(2 * WIDE // 128):
                s.kv[image, key_at, tile * 128 : (tile + 1) * 128] = s.stage.at[tile // 2][
                    pl.ds((tile % 2) * CHUNK + image, keys, stride=z.images), :
                ].astype(BF16)

    split = chunk_count // 2

    @pl.loop(0, split)
    def _(index):
        project_chunk(index)

    after_self = s.x_own[...].astype(F32) + sum_finish("self") + vec(6)
    s.after_self[...] = after_self
    normed, _ = norm_parts(after_self[:query])
    s.c[rank] = (normed * vec(2) + vec(3)).astype(BF16)
    share_start("c")
    normed, _ = norm_parts(after_self[query:])
    s.f_t[rank] = (normed * vec(4) + vec(5)).astype(BF16)
    share_start("ft")
    put_stat(1, after_self, weight_own)
    put_stat(2, after_self[query:], weight_text)
    gather_forward("cross")
    gather_start("in0")
    gather_start("out0")
    share_forward("c")

    @pl.loop(split, chunk_count)
    def _(index):
        project_chunk(index)

    load_tail.wait()
    last = project(s.tail[...])
    first_row = lax.broadcasted_iota(jnp.int32, (tail, 1), 0) == 0
    for image in range(z.images):
        s.kv[image, z.keys - 1 :, :] = jnp.where(
            first_row, jnp.broadcast_to(last[image : image + 1, :], last.shape), 0.0
        ).astype(BF16)
    for index in range(CHUNKS_HELD):
        load_chunk(index).start()
    gather_finish("cross")
    widen(s.m_cross, s.w_cross, 2)
    share_forward("ft")
    share_finish("c")
    queries_total = rows * query
    cross_query = dot(s.c[...].reshape(queries_total, z.model), s.w_cross[:, :WIDE])
    s.qc[...] = (cross_query + s.bias[1:2, :WIDE]).astype(BF16).reshape(s.qc.shape)
    is_key = lanes(PADDED_KEYS) < z.keys

    def all_slots(ref):
        return ref[...].reshape(queries_total, WIDE)

    def cross_queries(image):
        values = s.qc[s.slot_of[image]]
        return spread(values * jnp.asarray(z.scale, BF16), heads)

    unroll = 4

    @pl.loop(0, z.images // unroll)
    def _(group):
        for inner in range(unroll):
            image = group * unroll + inner
            scores = dot_columns(cross_queries(image), s.kv[image, :, :WIDE])
            probs = softmax(jnp.where(is_key, scores, MASKED)).astype(BF16)
            s.p_cross[image] = probs
            mixed = fold(dot(probs, s.kv[image, :, WIDE:]), heads, QUERIES)
            s.oc_image[image] = mixed.astype(BF16)

    @pl.loop(0, z.images)
    def _(slot):
        s.oc[slot] = s.oc_image[s.image_of[slot]]

    s.part_q[...] = (
        dot_columns(all_slots(s.oc), s.w_cross[:, WIDE:]).astype(BF16).reshape(s.part_q.shape)
    )
    sum_copy("cross", 0).start()
    sum_copy("cross", 1).start()
    sum_forward("cross")
    share_finish("ft")

    f_of = {0: s.f_q, 1: s.f_t}
    w_in = {0: s.m_in0, 1: s.m_in1}
    w_out = {0: s.m_out0, 1: s.m_out1}
    load_gy.wait()

    def grad_rows(kind, row):
        return s.gy[row, kind * query : (kind + 1) * query, :]

    def feed_forward(kind, part, send):
        for pair in (1 - chip, chip):
            values = f_of[kind][pl.ds(pair * 2, 2)].reshape(2 * query, z.model)
            grads = jnp.concatenate(
                [grad_rows(kind, pair * 2), grad_rows(kind, pair * 2 + 1)], axis=0
            )
            up = dot(values, w_in[kind][...]) + s.bias[3 + kind : 4 + kind, :]
            share = 0.5 * (1.0 + lax.erf(up * (0.5**0.5)))
            hidden = (up * share).astype(BF16)
            slope = share + up * (jnp.exp(-0.5 * up * up) * ((0.5 / math.pi) ** 0.5))
            grad_up = (dot(grads, w_out[kind][...]) * slope).astype(BF16)
            at = pl.ds(pl.multiple_of(pair * 2 * query, 2 * query), 2 * query)
            s.hid[at, :] = hidden
            s.gu[at, :] = grad_up
            s.small[20 + kind : 21 + kind, :] += column_total(grad_up)
            back = dot_columns(grad_up, w_in[kind][...]).astype(BF16)
            part[pl.ds(pair * 2, 2)] = back.reshape(2, query, z.model)
            send(pair)
            out = dot_columns(hidden, w_out[kind][...]).astype(BF16)
            out = out.reshape(2, query, z.model)
            s.part_row[pl.ds(pair * 2, 2), kind * query : (kind + 1) * query, :] = out

    def weight_terms(kind):
        values = f_of[kind][...].reshape(queries_total, z.model)
        grads = jnp.concatenate([grad_rows(kind, row) for row in range(rows)], axis=0)
        for name, left, right in (
            ("in%d" % kind, values, s.gu[...]),
            ("out%d" % kind, grads, s.hid[...]),
        ):
            gather_sent(name)
            for at in range(0, z.model, WIDE):
                whole[name][at : at + WIDE, :] = dot_rows(left[:, at : at + WIDE], right).astype(
                    BF16
                )

    gather_forward("in1")
    gather_forward("out1")
    gather_finish("in1")
    gather_finish("out1")
    sum_sent("self")
    hops = iter((0, 1))
    feed_forward(1, s.part_t, lambda pair: sum_copy("gft", next(hops)).start())
    after_query = s.after_self[:query, :] + sum_finish("cross") + vec(7)
    s.after_query[...] = after_query
    normed, _ = norm_parts(after_query)
    s.f_q[rank] = (normed * vec(4) + vec(5)).astype(BF16)
    share_start("fq")
    sum_forward("gft")
    put_stat(2, after_query, weight_query)
    weight_terms(1)
    share_sent("ft")
    share_forward("fq")
    gather_forward("in0")
    gather_forward("out0")

    def own_back(total, after, grads, slot):
        normed, scale = norm_parts(after)
        s.small[4:5, :] += column_total(total * normed)
        s.small[5:6, :] += column_total(total)
        s.small[slot : slot + 1, :] += column_total(grads)
        return grads.astype(F32) + norm_grad(normed, scale, vec(4), total)

    grad_text = own_back(
        sum_finish("gft"), s.after_self[query:, :], grad_rows(1, rank), 9
    )
    s.g_own[query:, :] = grad_text
    grad_text_low = grad_text.astype(BF16)
    s.gsa_t[rank] = grad_text_low
    s.small[6:7, :] += column_total(grad_text_low)
    share_start("gsat")
    gather_finish("in0")
    gather_finish("out0")
    scatter_start("in1")
    scatter_start("out1")
    sum_sent("cross")
    share_finish("fq")
    hops = iter((0, 1))
    feed_forward(0, s.part_q, lambda pair: sum_copy("gfq", next(hops)).start())
    sum_forward("gfq")
    share_forward("gsat")
    weight_terms(0)
    share_sent("fq")
    scatter_start("in0")
    scatter_start("out0")
    grad_query = own_back(sum_finish("gfq"), s.after_query[...], grad_rows(0, rank), 8)
    s.g_own[:query, :] = grad_query
    grad_query_low = grad_query.astype(BF16)
    s.f_t[rank] = grad_query_low
    s.small[7:8, :] += column_total(grad_query_low)
    share_start("gca")
    sum_copy("out", 0).start()
    sum_copy("out", 1).start()
    share_finish("gsat")
    scatter_forward("in1")
    share_forward("gca")
    sum_forward("out")
    share_finish("gca")

    grad_mixed = dot(s.f_t[...].reshape(queries_total, z.model), s.w_cross[:, WIDE:])
    s.goc[...] = grad_mixed.astype(BF16).reshape(s.goc.shape)

    def stage_put(image, values):
        for tile in range(WIDE // 128):
            s.stage.at[tile][pl.ds(image, PADDED_KEYS, stride=z.images), :] = values[
                :, tile * 128 : (tile + 1) * 128
            ]

    @pl.loop(0, z.images // unroll)
    def _(group):
        for inner in range(unroll):
            image = group * unroll + inner
            grads = spread(s.goc[s.slot_of[image]], heads)
            probs = s.p_cross[image]
            wide = probs.astype(F32)
            grad_probs = dot_columns(grads, s.kv[image, :, WIDE:])
            delta = jnp.sum(wide * grad_probs, axis=-1, keepdims=True)
            grad_scores = (wide * (grad_probs - delta)).astype(BF16)
            mixed = fold(dot(grad_scores, s.kv[image, :, :WIDE]), heads, QUERIES) * z.scale
            s.kv[image, : heads * QUERIES, :PADDED_KEYS] = grad_scores
            s.oc_image[image] = mixed.astype(BF16)

    @pl.loop(0, z.images)
    def _(slot):
        s.gqc[slot] = s.oc_image[s.image_of[slot]]

    sum_sent("gfq")
    s.part_q[...] = (
        dot_columns(all_slots(s.gqc), s.w_cross[:, :WIDE]).astype(BF16).reshape(s.part_q.shape)
    )
    sum_copy("gc", 0).start()
    sum_copy("gc", 1).start()
    s.small[18:19, :WIDE] += column_total(all_slots(s.gqc))
    sum_forward("gc")
    scatter_forward("out1")

    after_ffn_sum = sum_finish("out")
    after_query_out = s.after_query[...] + after_ffn_sum[:query] + vec(8)
    after_text_out = s.after_self[query:, :] + after_ffn_sum[query:] + vec(9)
    put_stat(3, after_query_out, weight_query)
    put_stat(3, after_text_out, weight_text)
    s.gy[rank, :query, :] = after_query_out.astype(BF16)
    s.gy[rank, query:, :] = after_text_out.astype(BF16)

    def key_grad(image):
        grad_scores = s.kv[image, : heads * QUERIES, :PADDED_KEYS]
        return dot_rows(grad_scores, cross_queries(image))

    def value_grad(image):
        grads = spread(s.goc[s.slot_of[image]], heads)
        return dot_rows(s.p_cross[image], grads)

    def features_pass(grad_of):
        @pl.loop(0, z.images // unroll)
        def _(group):
            for inner in range(unroll):
                image = group * unroll + inner
                stage_put(image, grad_of(image))

        def grads_at(at):
            return jnp.concatenate(
                [s.stage[tile, at, :].astype(BF16) for tile in range(WIDE // 128)], axis=1
            )

        s.turned[...] = dot_rows(grads_at(pl.ds(chunk_count * CHUNK, tail)), s.tail[...])
        s.col_sum[...] = column_total(grads_at(pl.ds(chunk_count * CHUNK, tail)))

        @pl.loop(0, chunk_count)
        def _(index):
            load_chunk(index).wait()
            grads = grads_at(pl.ds(pl.multiple_of(index * CHUNK, CHUNK), CHUNK))
            s.turned[...] += dot_rows(grads, s.chunk[lax.rem(index, CHUNKS_HELD)])
            s.col_sum[...] += column_total(grads)

            @pl.when(index + CHUNKS_HELD < chunk_count)
            def _():
                load_chunk(index + CHUNKS_HELD).start()

    gather_sent("kv")
    features_pass(key_grad)
    for index in range(CHUNKS_HELD):
        load_chunk(index).start()
    turned = s.turned[...].T
    s.m_kv[:, :128] = turned[:, :128].astype(BF16)
    s.m_kv[:, 256:] = turned[:, 128:].astype(BF16)

    cross_sum = sum_finish("gc")
    normed, scale = norm_parts(s.after_self[:query, :])
    s.small[2:3, :] += column_total(cross_sum * normed)
    s.small[3:4, :] += column_total(cross_sum)
    grad_query = s.g_own[:query, :] + norm_grad(normed, scale, vec(2), cross_sum)
    s.g_own[:query, :] = grad_query
    grad_query_low = grad_query.astype(BF16)
    s.f_q[rank] = grad_query_low
    s.small[6:7, :] += column_total(grad_query_low)
    share_start("gsaq")
    share_start("out")
    low_half = lanes(128) < HEAD
    gather_sent("cross")
    grad_cq = dot_rows(s.c[...].reshape(queries_total, z.model), all_slots(s.gqc))
    grad_co = dot_rows(s.f_t[...].reshape(queries_total, z.model), all_slots(s.oc))
    s.m_cross[:, :128] = grad_cq[:, :128].astype(BF16)
    s.m_cross[:, 128:256] = grad_co[:, :128].astype(BF16)
    s.m_cross[:, 256:] = jnp.where(
        low_half, grad_cq[:, 128:], pltpu.roll(grad_co[:, 128:], HEAD, 1)
    ).astype(BF16)
    scatter_start("cross")
    share_forward("gsaq")
    scatter_forward("in0")
    share_finish("gsaq")
    sum_sent("out")

    @pl.loop(0, rows)
    def _(step):
        row = send_order(step)
        at = row_at(row)
        grads = jnp.concatenate([s.f_q[row], s.gsa_t[row]], axis=0)
        low = s.qkv[at, :]
        queries = spread(low[:, :WIDE] * jnp.asarray(z.scale, BF16), heads)
        grad_mixed = dot(grads, s.w_self[:, 3 * WIDE :]).astype(BF16)
        grad_mixed = spread(grad_mixed, heads)
        probs = s.p_self[row]
        wide = probs.astype(F32)
        grad_probs = dot_columns(grad_mixed, low[:, 2 * WIDE :])
        delta = jnp.sum(wide * grad_probs, axis=-1, keepdims=True)
        grad_scores = (wide * (grad_probs - delta)).astype(BF16)
        grad_q = fold(dot(grad_scores, low[:, WIDE : 2 * WIDE]), heads, length) * z.scale
        grad_k = dot_rows(grad_scores, queries)
        grad_v = dot_rows(probs, grad_mixed)
        grad_low = jnp.concatenate([grad_q, grad_k, grad_v], axis=1).astype(BF16)
        s.qkv[at, :] = grad_low
        s.small[16:17, :WIDE] += column_total(grad_low[:, :WIDE])
        s.small[17:18, :WIDE] += column_total(grad_low[:, 2 * WIDE :])
        s.part_row[row] = dot_columns(grad_low, s.w_self[:, : 3 * WIDE]).astype(BF16)

        @pl.when(step == 0)
        def _():
            sum_copy("ga", 0).start()

        @pl.when(step == 2)
        def _():
            sum_copy("ga", 1).start()

    sum_forward("ga")
    share_forward("out")

    gather_sent("self")
    grads_all = [
        dot_rows(s.a[...], s.qkv[:, i * WIDE : (i + 1) * WIDE]) for i in range(3)
    ]
    grad_stream = jnp.concatenate(
        [ref[row] for row in range(rows) for ref in (s.f_q, s.gsa_t)], axis=0
    )
    grads_all.append(dot_rows(grad_stream, s.o[...]))
    for i, value in enumerate(grads_all):
        s.m_self[:, i * 128 : (i + 1) * 128] = value[:, :128].astype(BF16)
    for i in range(2):
        s.m_self[:, (4 + i) * 128 : (5 + i) * 128] = jnp.where(
            low_half, grads_all[2 * i][:, 128:], pltpu.roll(grads_all[2 * i + 1][:, 128:], HEAD, 1)
        ).astype(BF16)
    scatter_start("self")
    scatter_forward("out0")
    scatter_forward("cross")

    self_sum = sum_finish("ga")
    normed, scale = norm_parts(s.x_own[...].astype(F32))
    s.small[0:1, :] += column_total(self_sum * normed)
    s.small[1:2, :] += column_total(self_sum)
    s.x[rank] = (s.g_own[...] + norm_grad(normed, scale, vec(0), self_sum)).astype(BF16)
    share_start("sg")

    features_pass(value_grad)
    s.small[19:20, :WIDE] += s.col_sum[...]
    turned = s.turned[...].T
    s.m_kv[:, 128:256] = turned[:, :128].astype(BF16)
    s.m_kv[:, 256:] = jnp.where(
        low_half, s.m_kv[:, 256:].astype(F32), pltpu.roll(turned[:, 128:], HEAD, 1)
    ).astype(BF16)
    scatter_start("kv")
    share_forward("sg")

    def small_copy(source, hop, device):
        target = s.small_in.at[hop] if source is s.small else s.small_in.at[hop, pl.ds(0, 16)]
        return remote(source, target, (s.small_send, s.small_recv), (hop,), device)

    shared_rows = s.small.at[pl.ds(0, 16)]
    for hop, device in enumerate(((place, beside), (place, far))):
        item = small_copy(shared_rows, hop, device)
        item.start()
        item.wait()
        s.small[:16, :] += s.small_in[hop, :16, :]
    scatter_forward("self")
    item = small_copy(s.small, 2, across)
    item.start()
    item.wait()
    s.small[...] += s.small_in[2]
    items = [small_copy(s.small, 2 + step, along(step)) for step in range(1, lines)]
    for item in items:
        item.start()
    scatter_forward("kv")
    share_finish("out")
    store_out = pltpu.make_async_copy(s.gy, s.out_h, s.load_sem.at[3])
    store_out.start()
    share_finish("sg")
    store_sg = pltpu.make_async_copy(s.x, s.sg_h, s.load_sem.at[4])
    store_sg.start()
    total = s.small[...]
    for step in range(1, lines):
        items[step - 1].wait_recv()
        total = total + s.small_in[2 + step]
    s.small_out[...] = total
    for name in TERMS:
        scatter_finish(name)
    for item in items:
        item.wait_send()
    gather_sent("vec")
    for name in ("gft", "gc", "ga"):
        sum_sent(name)
    for name in SHARES:
        if name not in ("ft", "fq"):
            share_sent(name)
    store_out.wait()
    store_sg.wait()


def layer(
    stream_in,
    features,
    image_index,
    text_segment,
    text_valid,
    self_qkv,
    self_out,
    cross_q,
    cross_kv,
    cross_out,
    ffn_in,
    ffn_out,
    vectors,
    head_bias,
    ffn_bias,
    out_grad,
):
    count = lax.axis_size("dp")
    tokens, model = stream_in.shape
    width, hidden = self_qkv.shape[2], ffn_in.shape[2]
    fan, feat_fan = ffn_in.shape[1], cross_kv.shape[1]
    rows, text = text_segment.shape
    images, keys, feat = features.shape
    query = SLOTS * QUERIES
    z = types.SimpleNamespace(
        count=count,
        rows=rows,
        width=width,
        heads=width // HEAD,
        fan=fan,
        feat_fan=feat_fan,
        model=model,
        features=images * keys,
        images=images,
        keys=keys,
        scale=HEAD**-0.5,
    )
    lines = count // 2

    def wide(row):
        return jnp.pad(row.astype(F32), (0, WIDE - width))

    none = jnp.zeros((WIDE,), F32)
    bias = jnp.stack(
        [
            jnp.concatenate([wide(head_bias[0]), none, wide(head_bias[1])]),
            jnp.concatenate([wide(head_bias[2]), none, none]),
            jnp.concatenate([none, wide(head_bias[3]), none]),
            ffn_bias[0].astype(F32),
            ffn_bias[1].astype(F32),
        ]
    )
    query_segment = jnp.arange(query, dtype=jnp.int32) // QUERIES
    segment = jnp.concatenate(
        [jnp.broadcast_to(query_segment, (rows, query)), text_segment], axis=1
    )
    valid = jnp.concatenate([jnp.ones((rows, query), jnp.int32), text_valid], axis=1)
    key_code = jnp.where(valid == 1, segment, -1)
    image_of = image_index.reshape(-1)
    slot_of = jnp.argmax(image_of[None, :] == jnp.arange(images)[:, None], axis=1)
    operands = {
        "slot_of": slot_of.astype(jnp.int32),
        "image_of": image_of,
        "vec_h": jnp.pad(vectors, ((0, 6), (0, 128 - vectors.shape[1]))),
        "self_h": pack_columns([self_qkv[0], self_qkv[1], self_qkv[2], self_out.T], 1),
        "kv_h": pack_columns([cross_kv[0], cross_kv[1]], 1),
        "cross_h": pack_columns([cross_q, cross_out.T], 1),
        "ffn_h": jnp.concatenate([ffn_in, ffn_out.transpose(0, 2, 1)], axis=0).reshape(
            4 * fan, hidden
        ),
        "x_h": stream_in.reshape(rows, ROW_LEN, model),
        "gy_h": out_grad.reshape(rows, ROW_LEN, model),
        "feat_h": features.transpose(1, 0, 2).reshape(keys * images, feat),
        "bias": bias,
        "query_code": segment.reshape(-1, 1),
        "key_code": key_code,
        "weight": lax.dynamic_index_in_dim(valid, lax.axis_index("mp"), 0, False)
        .reshape(-1, 1)
        .astype(F32),
    }
    spaces = {name: pltpu.SMEM for name in ("slot_of", "image_of")}
    spaces |= {name: pltpu.VMEM for name in ("bias", "query_code", "key_code", "weight")}
    results = {
        "out_h": ((rows, ROW_LEN, model), BF16),
        "sg_h": ((rows, ROW_LEN, model), BF16),
        "own_self": ((fan, 4 * width), F32),
        "own_kv": ((feat_fan, 2 * width), F32),
        "own_cross": ((fan, 2 * width), F32),
        "own_ffn": ((4 * fan, hidden), F32),
        "small_out": ((24, model), F32),
    }
    chunk_rows = (keys + PADDED_KEYS - keys) * images
    buffers = {
        "w_vec": ((count * 16, 128), BF16),
        "vecs": ((16, model), F32),
        "m_self": ((model, 4 * width), BF16),
        "m_kv": ((feat, 2 * width), BF16),
        "m_cross": ((model, 2 * width), BF16),
        "w_self": ((model, 4 * WIDE), BF16),
        "w_kv": ((feat, 2 * WIDE), BF16),
        "w_cross": ((model, 2 * WIDE), BF16),
        "x": ((rows, ROW_LEN, model), BF16),
        "x_own": ((ROW_LEN, model), BF16),
        "gy": ((rows, ROW_LEN, model), BF16),
        "a": ((tokens, model), BF16),
        "qkv": ((tokens, 3 * WIDE), BF16),
        "o": ((tokens, WIDE), BF16),
        "p_self": ((rows, z.heads * ROW_LEN, ROW_LEN), BF16),
        "c": ((rows, query, model), BF16),
        "f_q": ((rows, query, model), BF16),
        "f_t": ((rows, query, model), BF16),
        "gsa_t": ((rows, query, model), BF16),
        "qc": ((images, QUERIES, WIDE), BF16),
        "gqc": ((images, QUERIES, WIDE), BF16),
        "goc": ((images, QUERIES, WIDE), BF16),
        "oc": ((images, QUERIES, WIDE), BF16),
        "oc_image": ((images, QUERIES, WIDE), BF16),
        "kv": ((images, PADDED_KEYS, 2 * WIDE), BF16),
        "p_cross": ((images, z.heads * QUERIES, PADDED_KEYS), BF16),
        "stage": ((WIDE // 128, PADDED_KEYS * images, 128), F32),
        "turned": ((WIDE, feat), F32),
        "col_sum": ((1, WIDE), F32),
        "chunk": ((CHUNKS_HELD, CHUNK, feat), BF16),
        "tail": ((images * keys % CHUNK, feat), BF16),
        "hid": ((rows * query, hidden), BF16),
        "gu": ((rows * query, hidden), BF16),
        "part_row": ((rows, ROW_LEN, model), BF16),
        "part_q": ((rows, query, model), BF16),
        "part_t": ((rows, query, model), BF16),
        "after_self": ((ROW_LEN, model), F32),
        "after_query": ((query, model), F32),
        "g_own": ((ROW_LEN, model), F32),
        "small": ((24, model), F32),
        "small_in": ((2 + lines, 24, model), F32),
    }
    for name in ("in0", "in1", "out0", "out1"):
        buffers["m_" + name] = ((model, hidden), BF16)
    for name in ("self", "out", "cross", "gft", "gfq"):
        block = (ROW_LEN if name in ("self", "out") else query, model)
        buffers["pin_" + name] = ((2, *block), BF16)
        buffers["fin_" + name] = (block, BF16)
    buffers["half_row"] = ((ROW_LEN, model), BF16)
    buffers["half_q"] = ((query, model), BF16)
    buffers["half_t"] = ((query, model), BF16)
    for name in TERMS:
        high = feat_fan if name == "kv" else fan
        across = {"self": 4 * width, "kv": 2 * width, "cross": 2 * width}.get(name, hidden)
        buffers["y_" + name] = ((lines, high, across), BF16)
        buffers["z_" + name] = ((lines - 1, high, across), BF16)
    semaphores = {
        "own_sem": (len(PIECES),),
        "load_sem": (5,),
        "chunk_sem": (CHUNKS_HELD,),
    }
    for name in ("gl_send", "gl_recv", "gs_send", "gs_recv"):
        semaphores[name] = (len(PIECES), lines)
    for name in ("ss_send", "ss_recv", "sl_send", "sl_recv"):
        semaphores[name] = (len(TERMS), lines)
    for kind in ("send", "recv"):
        semaphores["sum_" + kind] = (len(SUMS), 3)
        semaphores["share_" + kind] = (len(SHARES), 3)
        semaphores["small_" + kind] = (2 + lines,)
    names = (*operands, *results, *buffers, *semaphores)
    held = ("out_h", "sg_h")
    done = pl.pallas_call(
        functools.partial(layer_kernel, names, z),
        out_shape=[jax.ShapeDtypeStruct(*item) for item in results.values()],
        in_specs=[pl.BlockSpec(memory_space=spaces.get(name, pl.ANY)) for name in operands],
        out_specs=[
            pl.BlockSpec(memory_space=pl.ANY if name in held else pltpu.VMEM) for name in results
        ],
        scratch_shapes=[pltpu.VMEM(*item) for item in buffers.values()]
        + [pltpu.SemaphoreType.DMA(item) for item in semaphores.values()],
        compiler_params=pltpu.CompilerParams(
            collective_id=0, has_side_effects=True, vmem_limit_bytes=VMEM_LIMIT
        ),
    )(*operands.values())
    out_all, grad_all, own_self, own_kv, own_cross, own_ffn, small = done
    grad_q, grad_k, grad_v, grad_out = unpack_columns(own_self, 4, width)
    grad_cq, grad_co = unpack_columns(own_cross, 2, width)
    own_ffn = own_ffn.reshape(4, fan, hidden)
    stats = small[10, :5]
    return (
        out_all.reshape(tokens, model),
        grad_all.reshape(tokens, model).astype(F32),
        jnp.stack([grad_q, grad_k, grad_v]),
        grad_out.T,
        grad_cq,
        jnp.stack(unpack_columns(own_kv, 2, width)),
        grad_co.T,
        own_ffn[:2],
        own_ffn[2:].transpose(0, 2, 1),
        lax.dynamic_slice_in_dim(
            small[:10], lax.axis_index("dp") * vectors.shape[1], vectors.shape[1], axis=1
        ),
        small[16:20, :width],
        small[20:22, :hidden],
        jnp.sqrt(stats[:4] / (stats[4] * model)),
    )


def layer_norm(values, gain_row, shift_row):
    row_mean = jnp.mean(values, axis=-1, keepdims=True)
    centred = values - row_mean
    row_var = jnp.mean(centred * centred, axis=-1, keepdims=True)
    return centred * lax.rsqrt(row_var + EPSILON) * gain_row + shift_row


def norm_back(values, gain_row, shift_row, grad_normed):
    pull_back = jax.vjp(layer_norm, values, gain_row, shift_row)[1]
    return pull_back(grad_normed)


def gelu_exact(values):
    return jax.nn.gelu(values, approximate=False)


def round_low(values):
    return values.astype(jnp.bfloat16)


def matmul(left_side, right_side):
    return jnp.dot(left_side, right_side, preferred_element_type=jnp.float32)


def matmul_left(left_side, right_side):
    return lax.dot_general(
        left_side, right_side, (((0,), (0,)), ((), ())), preferred_element_type=jnp.float32
    )


def matmul_right(left_side, right_side):
    return lax.dot_general(
        left_side, right_side, (((1,), (1,)), ((), ())), preferred_element_type=jnp.float32
    )


def column_sum(values):
    return jnp.sum(values.astype(jnp.float32), axis=0)


def attn_scores(queries, keys_in, key_mask):
    score_scale = queries.shape[-1] ** (-0.5)
    scores = (
        jnp.einsum("bqhe,bkhe->bhqk", queries, keys_in, preferred_element_type=jnp.float32)
        * score_scale
    )
    if key_mask is None:
        return scores
    return jnp.where(key_mask[:, None], scores, MASKED)


def attend(queries, keys_in, values_in, key_mask):
    scores = attn_scores(queries, keys_in, key_mask)
    row_max = jnp.max(scores, axis=-1, keepdims=True)
    exponent = jnp.exp(scores - row_max)
    row_total = jnp.sum(exponent, axis=-1, keepdims=True)
    attn_probs = round_low(exponent / row_total)
    mixed_out = jnp.einsum(
        "bhqk,bkhe->bqhe", attn_probs, values_in, preferred_element_type=jnp.float32
    )
    return (round_low(mixed_out), row_max + jnp.log(row_total))


def attend_back(queries, keys_in, values_in, key_mask, log_total, grad_mixed):
    score_scale = queries.shape[-1] ** (-0.5)
    attn_probs = jnp.exp(attn_scores(queries, keys_in, key_mask) - log_total)
    grad_values = jnp.einsum(
        "bhqk,bqhe->bkhe", round_low(attn_probs), grad_mixed, preferred_element_type=jnp.float32
    )
    grad_probs = jnp.einsum(
        "bqhe,bkhe->bhqk", grad_mixed, values_in, preferred_element_type=jnp.float32
    )
    row_delta = jnp.sum(attn_probs * grad_probs, axis=-1, keepdims=True)
    grad_scores = round_low(attn_probs * (grad_probs - row_delta))
    grad_queries = (
        jnp.einsum("bhqk,bkhe->bqhe", grad_scores, keys_in, preferred_element_type=jnp.float32)
        * score_scale
    )
    grad_keys = (
        jnp.einsum("bhqk,bqhe->bkhe", grad_scores, queries, preferred_element_type=jnp.float32)
        * score_scale
    )
    return (round_low(grad_queries), round_low(grad_keys), round_low(grad_values))


def heads_total(partial_terms):
    return lax.psum(partial_terms, "mp")


def inputs_total(partial_terms):
    return lax.psum(partial_terms, "mp")


def ffn_forward(normed_low, weight_up, bias_up, weight_down):
    up_value = matmul(normed_low, weight_up) + bias_up
    hidden = round_low(gelu_exact(up_value))
    return (up_value, hidden, matmul(hidden, weight_down))


def ffn_back(normed_low, up_value, hidden, weight_up, weight_down, grad_low):
    grad_down = matmul_left(hidden, grad_low)
    grad_hidden = matmul_right(grad_low, weight_down)
    grad_up = round_low(jax.vjp(gelu_exact, up_value)[1](grad_hidden)[0])
    grad_in = matmul_left(normed_low, grad_up)
    return (grad_in, grad_down, column_sum(grad_up), matmul_right(grad_up, weight_up))


def body(
    stream_in,
    features,
    image_index,
    text_segment,
    text_valid,
    self_qkv,
    self_out,
    cross_q,
    cross_kv,
    cross_out,
    ffn_in,
    ffn_out,
    vectors,
    head_bias,
    ffn_bias,
    out_grad,
):
    gathered = (
        lax.all_gather(self_qkv, "dp", axis=1, tiled=True),
        lax.all_gather(self_out, "dp", axis=1, tiled=True),
        lax.all_gather(cross_q, "dp", axis=0, tiled=True),
        lax.all_gather(cross_kv, "dp", axis=1, tiled=True),
        lax.all_gather(cross_out, "dp", axis=1, tiled=True),
        lax.all_gather(ffn_in, "dp", axis=1, tiled=True),
        lax.all_gather(ffn_out, "dp", axis=2, tiled=True),
        lax.all_gather(vectors, "dp", axis=1, tiled=True),
    )
    qkv_w, proj_w, cq_w, ckv_w, cproj_w, up_w, down_w, vector_low = gathered
    vecs = vector_low.astype(jnp.float32)
    bias_heads = head_bias.astype(jnp.float32)
    bias_hidden = ffn_bias.astype(jnp.float32)
    stream = stream_in.astype(jnp.float32)
    tokens, model_width = stream.shape
    row_count = tokens // ROW_LEN
    query_count = SLOTS * QUERIES
    text_len = ROW_LEN - query_count
    local_width = qkv_w.shape[2]
    local_heads = local_width // HEAD
    query_segment = jnp.arange(query_count, dtype=jnp.int32) // QUERIES
    segment = jnp.concatenate(
        [jnp.broadcast_to(query_segment, (row_count, query_count)), text_segment], axis=1
    )
    valid = (
        jnp.concatenate([jnp.ones((row_count, query_count), jnp.int32), text_valid], axis=1) == 1
    )
    key_mask = (segment[:, :, None] == segment[:, None, :]) & valid[:, None, :]
    heads_shape = (row_count, ROW_LEN, local_heads, HEAD)
    normed_low = round_low(layer_norm(stream, vecs[0], vecs[1]))
    self_query = round_low(matmul(normed_low, qkv_w[0]) + bias_heads[0]).reshape(heads_shape)
    self_key = round_low(matmul(normed_low, qkv_w[1])).reshape(heads_shape)
    self_value = round_low(matmul(normed_low, qkv_w[2]) + bias_heads[1]).reshape(heads_shape)
    self_mixed, self_total = attend(self_query, self_key, self_value, key_mask)
    self_mixed = self_mixed.reshape(tokens, local_width)
    self_term = matmul(self_mixed, proj_w).reshape(row_count, ROW_LEN, model_width)
    after_self = stream + heads_total(self_term.reshape(tokens, model_width)) + vecs[6]
    self_rows = after_self.reshape(row_count, ROW_LEN, model_width)
    query_part = self_rows[:, :query_count].reshape(-1, model_width)
    cross_normed = round_low(layer_norm(query_part, vecs[2], vecs[3]))
    slot_count = row_count * SLOTS
    cross_query = round_low(matmul(cross_normed, cq_w) + bias_heads[2]).reshape(
        slot_count, QUERIES, local_heads, HEAD
    )
    image_order = image_index.reshape(-1)
    pick_table = (image_order[:, None] == jnp.arange(image_order.shape[0])[None, :]).astype(
        jnp.bfloat16
    )
    keys_all = round_low(
        jnp.einsum("nkf,fc->nkc", features, ckv_w[0], preferred_element_type=jnp.float32)
    )
    values_all = round_low(
        jnp.einsum("nkf,fc->nkc", features, ckv_w[1], preferred_element_type=jnp.float32)
        + bias_heads[3]
    )
    cross_keys = round_low(
        jnp.einsum("ij,jkc->ikc", pick_table, keys_all, preferred_element_type=jnp.float32)
    )
    cross_values = round_low(
        jnp.einsum("ij,jkc->ikc", pick_table, values_all, preferred_element_type=jnp.float32)
    )
    cross_keys = cross_keys.reshape(slot_count, KEYS, local_heads, HEAD)
    cross_values = cross_values.reshape(slot_count, KEYS, local_heads, HEAD)
    cross_mixed, cross_total = attend(cross_query, cross_keys, cross_values, None)
    cross_mixed = cross_mixed.reshape(-1, local_width)
    cross_term = matmul(cross_mixed, cproj_w).reshape(row_count, query_count, model_width)
    after_query = query_part + heads_total(cross_term.reshape(-1, model_width)) + vecs[7]
    after_cross = jnp.concatenate(
        [after_query.reshape(row_count, query_count, model_width), self_rows[:, query_count:]],
        axis=1,
    ).reshape(tokens, model_width)
    ffn_normed = round_low(layer_norm(after_cross, vecs[4], vecs[5])).reshape(
        row_count, ROW_LEN, model_width
    )
    ffn_query = ffn_normed[:, :query_count].reshape(-1, model_width)
    ffn_text = ffn_normed[:, query_count:].reshape(-1, model_width)
    up_query, hidden_query, part_query = ffn_forward(ffn_query, up_w[0], bias_hidden[0], down_w[0])
    up_text, hidden_text, part_text = ffn_forward(ffn_text, up_w[1], bias_hidden[1], down_w[1])
    ffn_terms = jnp.concatenate(
        [
            part_query.reshape(row_count, query_count, model_width),
            part_text.reshape(row_count, text_len, model_width),
        ],
        axis=1,
    )
    query_flag = jnp.arange(ROW_LEN) < query_count
    bias_rows = jnp.where(query_flag[:, None], vecs[8], vecs[9])
    ffn_sum = heads_total(ffn_terms.reshape(tokens, model_width)).reshape(
        row_count, ROW_LEN, model_width
    )
    after_ffn = after_cross + (ffn_sum + bias_rows).reshape(tokens, model_width)
    token_weight = valid.reshape(-1).astype(jnp.float32)
    stream_stats = jnp.stack(
        [
            jnp.sum(token_weight * jnp.sum(section * section, axis=1))
            for section in (stream, after_self, after_cross, after_ffn)
        ]
        + [jnp.sum(token_weight)]
    )
    out_low = round_low(after_ffn)
    regathered = (
        lax.all_gather(self_qkv, "dp", axis=1, tiled=True),
        lax.all_gather(self_out, "dp", axis=1, tiled=True),
        lax.all_gather(cross_q, "dp", axis=0, tiled=True),
        lax.all_gather(cross_kv, "dp", axis=1, tiled=True),
        lax.all_gather(cross_out, "dp", axis=1, tiled=True),
        lax.all_gather(ffn_in, "dp", axis=1, tiled=True),
        lax.all_gather(ffn_out, "dp", axis=2, tiled=True),
        lax.all_gather(vectors, "dp", axis=1, tiled=True),
    )
    qkv_w, proj_w, cq_w, ckv_w, cproj_w, up_w, down_w, vector_low = regathered
    vecs = vector_low.astype(jnp.float32)
    grad_out = out_grad.astype(jnp.float32)
    grad_out_rows = grad_out.reshape(row_count, ROW_LEN, model_width)
    grad_low = round_low(grad_out_rows)
    grad_low_query = grad_low[:, :query_count].reshape(-1, model_width)
    grad_low_text = grad_low[:, query_count:].reshape(-1, model_width)
    in_query, down_query, hidden_bias_query, normed_grad_query = ffn_back(
        ffn_query, up_query, hidden_query, up_w[0], down_w[0], grad_low_query
    )
    in_text, down_text, hidden_bias_text, normed_grad_text = ffn_back(
        ffn_text, up_text, hidden_text, up_w[1], down_w[1], grad_low_text
    )
    normed_grad_q = normed_grad_query.reshape(row_count, query_count, model_width)
    normed_grad_t = normed_grad_text.reshape(row_count, text_len, model_width)
    normed_grad = jnp.concatenate([normed_grad_q, normed_grad_t], axis=1)
    normed_grad = inputs_total(normed_grad.reshape(tokens, model_width))
    cross_back, gain_three, shift_three = norm_back(after_cross, vecs[4], vecs[5], normed_grad)
    grad_cross = grad_out + cross_back
    grad_cross_rows = grad_cross.reshape(row_count, ROW_LEN, model_width)
    grad_branch_cross = round_low(grad_cross_rows[:, :query_count].reshape(-1, model_width))
    grad_cproj = matmul_left(cross_mixed, grad_branch_cross)
    grad_cross_mixed = round_low(matmul_right(grad_branch_cross, cproj_w)).reshape(
        cross_query.shape
    )
    grad_cq_part, grad_ck_part, grad_cv_part = attend_back(
        cross_query, cross_keys, cross_values, None, cross_total, grad_cross_mixed
    )
    grad_cq_part = grad_cq_part.reshape(-1, local_width)
    grad_ck_all = round_low(
        jnp.einsum(
            "ij,ikc->jkc",
            pick_table,
            grad_ck_part.reshape(-1, KEYS, local_width),
            preferred_element_type=jnp.float32,
        )
    )
    grad_cv_all = round_low(
        jnp.einsum(
            "ij,ikc->jkc",
            pick_table,
            grad_cv_part.reshape(-1, KEYS, local_width),
            preferred_element_type=jnp.float32,
        )
    )
    grad_ckv = jnp.stack(
        [
            jnp.einsum("nkf,nkc->fc", features, grad_ck_all, preferred_element_type=jnp.float32),
            jnp.einsum("nkf,nkc->fc", features, grad_cv_all, preferred_element_type=jnp.float32),
        ]
    )
    grad_cq = matmul_left(cross_normed, grad_cq_part)
    cross_grad_term = matmul_right(grad_cq_part, cq_w)
    cross_normed_grad = inputs_total(cross_grad_term)
    query_back, gain_two, shift_two = norm_back(query_part, vecs[2], vecs[3], cross_normed_grad)
    grad_self = jnp.concatenate(
        [
            grad_cross_rows[:, :query_count]
            + query_back.reshape(row_count, query_count, model_width),
            grad_cross_rows[:, query_count:],
        ],
        axis=1,
    ).reshape(tokens, model_width)
    grad_branch_self = round_low(grad_self)
    grad_proj = matmul_left(self_mixed, grad_branch_self)
    grad_self_mixed = round_low(matmul_right(grad_branch_self, proj_w)).reshape(heads_shape)
    grad_sq, grad_sk, grad_sv = attend_back(
        self_query, self_key, self_value, key_mask, self_total, grad_self_mixed
    )
    grad_sq = grad_sq.reshape(tokens, local_width)
    grad_sk = grad_sk.reshape(tokens, local_width)
    grad_sv = grad_sv.reshape(tokens, local_width)
    grad_qkv = jnp.stack(
        [
            matmul_left(normed_low, grad_sq),
            matmul_left(normed_low, grad_sk),
            matmul_left(normed_low, grad_sv),
        ]
    )
    self_grad_term = (
        matmul_right(grad_sq, qkv_w[0])
        + matmul_right(grad_sk, qkv_w[1])
        + matmul_right(grad_sv, qkv_w[2])
    )
    normed_grad_self = inputs_total(self_grad_term)
    stream_back, gain_one, shift_one = norm_back(stream, vecs[0], vecs[1], normed_grad_self)
    stream_grad = grad_self + stream_back
    norm_rows = jnp.stack([gain_one, shift_one, gain_two, shift_two, gain_three, shift_three])
    grad_vectors = jnp.concatenate(
        [
            norm_rows,
            jnp.stack(
                [
                    column_sum(grad_branch_self),
                    column_sum(grad_branch_cross),
                    column_sum(grad_low_query),
                    column_sum(grad_low_text),
                ]
            ),
        ]
    )
    grad_up = jnp.stack([in_query, in_text])
    grad_down = jnp.stack([down_query, down_text])
    owned = (
        lax.psum_scatter(grad_qkv, "dp", scatter_dimension=1, tiled=True),
        lax.psum_scatter(grad_proj, "dp", scatter_dimension=1, tiled=True),
        lax.psum_scatter(grad_cq, "dp", scatter_dimension=0, tiled=True),
        lax.psum_scatter(grad_ckv, "dp", scatter_dimension=1, tiled=True),
        lax.psum_scatter(grad_cproj, "dp", scatter_dimension=1, tiled=True),
        lax.psum_scatter(grad_up, "dp", scatter_dimension=1, tiled=True),
        lax.psum_scatter(grad_down, "dp", scatter_dimension=2, tiled=True),
        lax.psum_scatter(grad_vectors, "dp", scatter_dimension=1, tiled=True),
    )
    grad_heads = jnp.stack(
        [
            column_sum(grad_sq),
            column_sum(grad_sv),
            column_sum(grad_cq_part),
            jnp.sum(grad_cv_part.astype(jnp.float32), axis=(0, 1)).reshape(-1),
        ]
    )
    grad_hidden_bias = jnp.stack([hidden_bias_query, hidden_bias_text])
    grad_heads, grad_hidden_bias, stream_stats = lax.psum(
        (grad_heads, grad_hidden_bias, stream_stats), "dp"
    )
    stream_rms = jnp.sqrt(stream_stats[:4] / (stream_stats[4] * model_width))
    return (
        out_low,
        stream_grad,
        owned[0],
        owned[1],
        owned[2],
        owned[3],
        owned[4],
        owned[5],
        owned[6],
        owned[7],
        grad_heads,
        grad_hidden_bias,
        stream_rms,
    )


def solution(mesh):
    in_specs = (
        P("dp", None),
        P("dp", None, None),
        P("dp", None),
        P("dp", None),
        P("dp", None),
        P(None, "dp", "mp"),
        P("mp", "dp"),
        P("dp", "mp"),
        P(None, "dp", "mp"),
        P("mp", "dp"),
        P(None, "dp", "mp"),
        P(None, "mp", "dp"),
        P(None, "dp"),
        P(None, "mp"),
        P(None, "mp"),
        P("dp", None),
    )
    out_specs = (
        P("dp", None),
        P("dp", None),
        P(None, "dp", "mp"),
        P("mp", "dp"),
        P("dp", "mp"),
        P(None, "dp", "mp"),
        P("mp", "dp"),
        P(None, "dp", "mp"),
        P(None, "mp", "dp"),
        P(None, "dp"),
        P(None, "mp"),
        P(None, "mp"),
        P(),
    )

    def apply(*args):
        fan = args[5].shape[1] // mesh.shape["dp"]
        whole_tiles = fan % 16 == 0 and fan <= 128 and mesh.shape["dp"] % 2 == 0
        run = layer if whole_tiles and mesh.shape["mp"] == 4 else body
        return jax.shard_map(
            run, mesh=mesh, in_specs=in_specs, out_specs=out_specs, check_vma=False
        )(*args)

    return apply
```

```python
import functools
import math
import types

import jax
import jax.numpy as jnp
from jax import lax
from jax.experimental import pallas as pl
from jax.experimental.pallas import tpu as pltpu
from jax.sharding import PartitionSpec as P

HEAD = 64
KEYS = 257
QUERIES = 32
SLOTS = 4
ROW_LEN = 256


EPSILON = 1e-06
MASKED = -1e30
MESH = pl.DeviceIdType.MESH
VMEM_LIMIT = 62 * 2**20
BF16 = jnp.bfloat16
F32 = jnp.float32
PIECES = ("vec", "self", "kv", "cross")
TERMS = ("cross", "kv", "self")
SUMS = ("selfq", "selft", "cross", "gft", "gfq", "out", "gc", "gaq", "gat")
SHARES = ("c", "ft", "fq", "gca", "gsat", "gsaq", "out", "sgq", "sgt")
RINGED = ("in1", "out1", "in0", "out0")
WIDE = 256
CHUNK = 256
CHUNKS_HELD = 3
PADDED_KEYS = 272


def dot(left, right):
    return jnp.dot(left, right, preferred_element_type=F32)


def dot_rows(left, right):
    return lax.dot_general(left, right, (((0,), (0,)), ((), ())), preferred_element_type=F32)


def dot_columns(left, right):
    return lax.dot_general(left, right, (((1,), (1,)), ((), ())), preferred_element_type=F32)


def norm_parts(values):
    centred = values - jnp.mean(values, axis=-1, keepdims=True)
    scale = lax.rsqrt(jnp.mean(centred * centred, axis=-1, keepdims=True) + EPSILON)
    return centred * scale, scale


def norm_grad(normed, scale, gain, grad):
    scaled = grad * gain
    return scale * (
        scaled
        - jnp.mean(scaled, axis=-1, keepdims=True)
        - normed * jnp.mean(scaled * normed, axis=-1, keepdims=True)
    )


def lanes(width):
    return lax.broadcasted_iota(jnp.int32, (1, width), 1)


def of_head(head):
    lane = lanes(WIDE)
    return (lane >= head * HEAD) & (lane < (head + 1) * HEAD)


def spread(values, heads):
    return jnp.concatenate(
        [jnp.where(of_head(head), values, jnp.zeros_like(values)) for head in range(heads)], axis=0
    )


def fold(values, heads, tokens):
    total = jnp.where(of_head(0), values[:tokens], 0.0)
    for head in range(1, heads):
        total = total + jnp.where(of_head(head), values[head * tokens : (head + 1) * tokens], 0.0)
    return total


def softmax(scores):
    exponent = jnp.exp(scores - jnp.max(scores, axis=-1, keepdims=True))
    return exponent * (1.0 / jnp.sum(exponent, axis=-1, keepdims=True))


def widen(packed, wide, count):
    low = lanes(128) < HEAD
    for i in range(count):
        at = (count + i // 2) * 128
        tail = packed[:, at : at + 128]
        if i % 2:
            tail = pltpu.roll(tail, HEAD, 1)
        wide[:, i * WIDE : i * WIDE + 128] = packed[:, i * 128 : (i + 1) * 128]
        wide[:, i * WIDE + 128 : (i + 1) * WIDE] = jnp.where(low, tail, jnp.zeros_like(tail))


def layer_kernel(names, sizes, *refs):
    s = types.SimpleNamespace(**dict(zip(names, refs)))
    z = sizes
    count, lines, rows, length, query, width, heads = (
        z.count,
        z.count // 2,
        z.rows,
        ROW_LEN,
        SLOTS * QUERIES,
        z.width,
        z.heads,
    )
    text = length - query
    place, rank = lax.axis_index("dp"), lax.axis_index("mp")
    line, side = place // 2, lax.rem(place, 2)
    chip, core = rank // 2, lax.rem(rank, 2)
    beside = chip * 2 + 1 - core
    far = (1 - chip) * 2 + core
    diagonal = (1 - chip) * 2 + 1 - core

    def remote(source, target, sems, index, device):
        return pltpu.make_async_remote_copy(
            src_ref=source,
            dst_ref=target,
            send_sem=sems[0].at[index],
            recv_sem=sems[1].at[index],
            device_id=device,
            device_id_type=MESH,
        )

    def other_line(step):
        at, weight = 0, 1
        while weight < lines:
            bit = lax.rem(line // weight, 2)
            at = at + weight * (1 - bit if step // weight % 2 else bit)
            weight *= 2
        return at

    def along(step):
        return (other_line(step) * 2 + side, rank)

    across = (line * 2 + 1 - side, rank)

    def block(ref, index, size):
        return ref.at[pl.ds(pl.multiple_of(index * size, 16), size)]

    fan, feat_fan = z.fan, z.feat_fan
    whole = {
        "vec": s.w_vec,
        "self": s.m_self,
        "kv": s.m_kv,
        "cross": s.m_cross,
        "in0": s.m_in0,
        "in1": s.m_in1,
        "out0": s.m_out0,
        "out1": s.m_out1,
    }
    size = {name: fan for name in PIECES + RINGED} | {"vec": 16, "kv": feat_fan}
    shard = {name: block(whole[name], place, size[name]) for name in PIECES + RINGED}
    own_in = [
        pltpu.make_async_copy(s.ffn_in.at[kind], shard["in%d" % kind], s.own_sem.at[kind])
        for kind in range(2)
    ]

    def pack(name, items):
        for i, item in enumerate(items):
            shard[name][:, i * 128 : (i + 1) * 128] = item[:, :128]
        for i in range(0, len(items), 2):
            at = (len(items) + i // 2) * 128
            shard[name][:, at : at + 128] = jnp.concatenate(
                [items[i][:, 128:], items[i + 1][:, 128:]], axis=1
            )

    def turn(values):
        return values.astype(F32).T.astype(BF16)

    def gather_line(name, step):
        return remote(
            shard[name],
            block(whole[name], place, size[name]),
            (s.gl_send, s.gl_recv),
            (PIECES.index(name), step),
            along(step),
        )

    def gather_side(name, step):
        origin = other_line(step) * 2 + side
        target = block(whole[name], origin, size[name])
        return remote(
            target,
            target,
            (s.gs_send, s.gs_recv),
            (PIECES.index(name), step),
            across,
        )

    def gather_start(name):
        for step in range(1, lines):
            gather_line(name, step).start()
        gather_side(name, 0).start()

    def gather_forward(name):
        for step in range(1, lines):
            gather_line(name, step).wait_recv()
            gather_side(name, step).start()

    def gather_finish(name):
        for step in range(lines):
            gather_side(name, step).wait_recv()

    def gather_sent(name):
        for step in range(1, lines):
            gather_line(name, step).wait_send()
        for step in range(lines):
            gather_side(name, step).wait_send()

    spot = line + side * (count - 1 - 2 * line)

    def ring_index(at):
        at = lax.rem(at + 2 * count, count)
        on = at // lines
        return (at + on * (count - 1 - 2 * at)) * 2 + on

    ring_to = ((ring_index(spot + 1), rank), (ring_index(spot - 1), rank))

    def ring_part(name, way):
        cut = -(-size[name] // 32) * 16
        return (0, cut) if way == 0 else (cut, size[name] - cut)

    def ring_block(name, at, way):
        first, high = ring_part(name, way)
        return whole[name].at[
            pl.ds(pl.multiple_of(ring_index(at) * size[name] + first, 16), high)
        ]

    def ring_gather(name, way, hop):
        target = ring_block(name, spot - hop if way == 0 else spot + hop, way)
        index = (RINGED.index(name), way, hop)
        return remote(target, target, (s.rg_send, s.rg_recv), index, ring_to[way])

    def ring_pass(names, hop):
        for name in names:
            for way in range(2):
                if hop > 0:
                    ring_gather(name, way, hop - 1).wait_recv()
                if hop < count - 1:
                    ring_gather(name, way, hop).start()

    first_pair, last_pair = RINGED[:2], RINGED[2:]

    def ring_gather_sent(name):
        for way in range(2):
            for hop in range(count - 1):
                ring_gather(name, way, hop).wait_send()

    def ring_scatter(name, way, hop):
        first, high = ring_part(name, way)
        return remote(
            ring_block(name, spot - 1 - hop if way == 0 else spot + 1 + hop, way),
            getattr(s, "r_" + name).at[hop, pl.ds(first, high)],
            (s.rs_send, s.rs_recv),
            (RINGED.index(name), way, hop),
            ring_to[way],
        )

    def scatter_pass(names, hop):
        for name in names:
            for way in range(2):
                first, high = ring_part(name, way)
                if hop > 0:
                    ring_scatter(name, way, hop - 1).wait_recv()
                    landed = getattr(s, "r_" + name)[hop - 1, first : first + high, :]
                    mine = ring_block(name, spot - 1 - hop if way == 0 else spot + 1 + hop, way)
                    total = mine[...].astype(F32) + landed.astype(F32)
                    if hop < count - 1:
                        mine[...] = total.astype(BF16)
                    else:
                        owned[name][first : first + high, :] = total
                if hop < count - 1:
                    ring_scatter(name, way, hop).start()

    def ring_scatter_sent(name):
        for way in range(2):
            for hop in range(count - 1):
                ring_scatter(name, way, hop).wait_send()

    side_in = {name: getattr(s, "y_" + name) for name in TERMS}
    line_in = {name: getattr(s, "z_" + name) for name in TERMS}
    owned = {
        "self": s.own_self,
        "kv": s.own_kv,
        "cross": s.own_cross,
        "in0": s.own_ffn.at[pl.ds(0, fan)],
        "in1": s.own_ffn.at[pl.ds(fan, fan)],
        "out0": s.own_ffn.at[pl.ds(2 * fan, fan)],
        "out1": s.own_ffn.at[pl.ds(3 * fan, fan)],
    }
    order = [*range(1, lines), 0]

    def scatter_side(name, step):
        other = other_line(step)
        return remote(
            block(whole[name], other * 2 + 1 - side, size[name]),
            side_in[name].at[step],
            (s.ss_send, s.ss_recv),
            (TERMS.index(name), step),
            across,
        )

    def scatter_line(name, step):
        other = other_line(step)
        return remote(
            block(whole[name], other * 2 + side, size[name]),
            line_in[name].at[step - 1],
            (s.sl_send, s.sl_recv),
            (TERMS.index(name), step),
            along(step),
        )

    def scatter_start(name):
        for step in order:
            scatter_side(name, step).start()

    def scatter_forward(name):
        for step in range(1, lines):
            other = other_line(step)
            mine = block(whole[name], other * 2 + side, size[name])
            scatter_side(name, step).wait_recv()
            mine[...] = (mine[...].astype(F32) + side_in[name][step].astype(F32)).astype(BF16)
            scatter_line(name, step).start()

    def scatter_finish(name):
        scatter_side(name, 0).wait_recv()
        total = block(whole[name], place, size[name])[...].astype(F32)
        total = total + side_in[name][0].astype(F32)
        for step in range(1, lines):
            scatter_line(name, step).wait_recv()
            total = total + line_in[name][step - 1].astype(F32)
        owned[name][...] = total
        for step in range(1, lines):
            scatter_line(name, step).wait_send()
        for step in range(lines):
            scatter_side(name, step).wait_send()

    halves = {"selfq": 0, "selft": 1, "cross": 0, "gft": 1, "gfq": 0, "gc": 1, "gaq": 0, "gat": 1}

    def sum_buffers(name):
        landed = {"gaq": "selfq", "gat": "selft", "gc": "cross"}.get(name, name)
        half = s.half_row if name == "out" else s.half.at[halves[name]]
        return getattr(s, "pin_" + landed), half, getattr(s, "fin_" + landed)

    def part(name, index):
        if name in ("selfq", "gaq"):
            return s.part_row.at[index, pl.ds(0, query)]
        if name in ("selft", "gat"):
            return s.part_row.at[index, pl.ds(query, text)]
        return {"out": s.part_row, "gft": s.part_t}.get(name, s.part_q).at[index]

    def sum_copy(name, hop):
        pair_in, half, far_in = sum_buffers(name)
        source, target, device = (
            (part(name, diagonal), pair_in.at[1], beside),
            (part(name, beside), pair_in.at[0], beside),
            (half, far_in, far),
        )[hop]
        index = (SUMS.index(name), hop)
        return remote(source, target, (s.sum_send, s.sum_recv), index, (place, device))

    def sum_forward(name):
        sum_copy(name, 0).wait_recv()
        pair_in, half, _ = sum_buffers(name)
        half[...] = (part(name, far)[...].astype(F32) + pair_in[1].astype(F32)).astype(BF16)
        sum_copy(name, 2).start()

    def sum_finish(name):
        sum_copy(name, 1).wait_recv()
        sum_copy(name, 2).wait_recv()
        pair_in, _, far_in = sum_buffers(name)
        total = part(name, rank)[...].astype(F32) + pair_in[0].astype(F32)
        return total + far_in[...].astype(F32)

    def sum_sent(name, hops=(0, 1, 2)):
        for hop in hops:
            sum_copy(name, hop).wait_send()

    shared = {
        "c": s.c,
        "ft": s.f_t,
        "fq": s.f_q,
        "gca": s.part_t,
        "gsat": s.gsa_t,
        "gsaq": s.f_q,
        "out": s.gy,
    }

    def shared_part(name, index):
        if name == "sgq":
            return s.x.at[index, pl.ds(0, query)]
        if name == "sgt":
            return s.x.at[index, pl.ds(query, text)]
        return shared[name].at[index]

    def share_copy(name, hop):
        index, device = ((rank, far), (rank, beside), (far, beside))[hop]
        return remote(
            shared_part(name, index),
            shared_part(name, index),
            (s.share_send, s.share_recv),
            (SHARES.index(name), hop),
            (place, device),
        )

    def share_start(name):
        share_copy(name, 0).start()
        share_copy(name, 1).start()

    def share_forward(name):
        share_copy(name, 0).wait_recv()
        share_copy(name, 2).start()

    def share_finish(name):
        share_copy(name, 1).wait_recv()
        share_copy(name, 2).wait_recv()

    def share_sent(name):
        for hop in range(3):
            share_copy(name, hop).wait_send()

    def vec(index):
        return s.vecs[index : index + 1, :]

    def column_total(values):
        return jnp.sum(values.astype(F32), axis=0, keepdims=True)

    def row_at(row):
        return pl.ds(pl.multiple_of(row * length, length), length)

    def put_stat(index, values, weight):
        total = jnp.sum(
            jnp.sum(values * values, axis=1, keepdims=True) * weight, axis=0, keepdims=True
        )
        s.small[10:11, :] += jnp.where(lanes(z.model) == index, total, 0.0)

    load_x = pltpu.make_async_copy(s.x_h, s.x, s.load_sem.at[0])
    load_gy = pltpu.make_async_copy(s.gy_h, s.gy, s.load_sem.at[1])
    load_x.start()
    barrier = pltpu.get_barrier_semaphore()
    partners = [along(step) for step in range(1, lines)] + [
        across,
        (place, beside),
        (place, far),
    ]
    for partner in partners:
        pl.semaphore_signal(barrier, inc=1, device_id=partner, device_id_type=MESH)
    for item in own_in:
        item.start()
    own = z.model // count
    shard["vec"][...] = jnp.zeros((16, 128), BF16)
    shard["vec"][: s.vectors.shape[0], :own] = s.vectors[...]
    pack("self", [s.self_qkv[0], s.self_qkv[1], s.self_qkv[2], turn(s.self_out[...])])
    pl.semaphore_wait(barrier, len(partners))
    gather_start("vec")
    gather_start("self")
    pack("kv", [s.cross_kv[0], s.cross_kv[1]])
    pack("cross", [s.cross_q[...], turn(s.cross_out[...])])
    gather_start("kv")
    gather_start("cross")
    for kind in range(2):
        shard["out%d" % kind][...] = s.ffn_out[kind]
        own_in[kind].wait()

    chunk_count = z.features // CHUNK
    tail = z.features - chunk_count * CHUNK

    def load_chunk(index):
        slot = lax.rem(index, CHUNKS_HELD)
        return pltpu.make_async_copy(
            s.feat_h.at[pl.ds(pl.multiple_of(index * CHUNK, CHUNK), CHUNK)],
            s.chunk.at[slot],
            s.chunk_sem.at[slot],
        )

    def load_chunks():
        for index in range(CHUNKS_HELD):
            load_chunk(index).start()

    load_tail = pltpu.make_async_copy(
        s.feat_h.at[pl.ds(chunk_count * CHUNK, tail)], s.tail, s.load_sem.at[2]
    )
    load_chunks()
    load_tail.start()
    load_gy.start()

    s.small[...] = jnp.zeros_like(s.small)
    s.bias[...] = jnp.zeros_like(s.bias)
    for row, at, index in ((0, 0, 0), (0, 2, 1), (1, 0, 2), (2, 1, 3)):
        s.bias[row : row + 1, at * WIDE : at * WIDE + width] = s.head_bias[
            index : index + 1, :
        ].astype(F32)
    s.bias[3:5, : z.hidden] = s.ffn_bias[...].astype(F32)
    slots = lanes(query).astype(F32) * (1.0 / QUERIES)
    s.code[:, :query] = jnp.broadcast_to(jnp.floor(slots), (rows, query))
    s.code[:, query:] = jnp.where(s.valid[...] == 1, s.segment[...], -1).astype(F32)
    same = lax.broadcasted_iota(jnp.int32, (text, text), 0) == lanes(text)

    def as_column(values):
        return jnp.sum(jnp.where(same, values.astype(F32), 0.0), axis=1, keepdims=True)

    for row in range(rows):
        s.text_codes[row] = as_column(s.segment[row : row + 1, :])
    s.weight[...] = as_column((s.valid[pl.ds(rank, 1), :] == 1).astype(jnp.int32))
    gather_forward("vec")
    gather_finish("vec")
    for index in range(count):
        s.vecs[:, index * own : (index + 1) * own] = s.w_vec[
            index * 16 : (index + 1) * 16, :own
        ].astype(F32)
    load_x.wait()

    @pl.loop(0, rows)
    def _(row):
        normed, _ = norm_parts(s.x[row].astype(F32))
        s.a[row_at(row), :] = (normed * vec(0) + vec(1)).astype(BF16)

    s.x_own[...] = s.x[rank]
    weight_query, weight_text = jnp.ones((query, 1), F32), s.weight[...]
    weight_own = jnp.concatenate([weight_query, weight_text], axis=0)
    s.small[10:11, :] += jnp.where(
        lanes(z.model) == 4, jnp.sum(weight_own, axis=0, keepdims=True), 0.0
    )
    put_stat(0, s.x_own[...].astype(F32), weight_own)

    gather_forward("self")
    gather_finish("self")
    widen(s.m_self, s.w_self, 4)

    def self_mask(row):
        at = lax.broadcasted_iota(jnp.int32, (query, 1), 0).astype(F32) * (1.0 / QUERIES)
        codes = jnp.concatenate([jnp.floor(at), s.text_codes[row]], axis=0)
        return codes == s.code[pl.ds(row, 1), :]

    def send_order(step):
        chip_at = chip + (1 - 2 * chip) * (1 - step // 2)
        core_at = core + (1 - 2 * core) * (1 - lax.rem(step, 2))
        return chip_at * 2 + core_at

    def send_pairs(step, names):
        @pl.when(step == 0)
        def _():
            for name in names:
                sum_copy(name, 0).start()

        @pl.when(step == 2)
        def _():
            for name in names:
                sum_copy(name, 1).start()

    def self_row(step):
        row = send_order(step)
        at = row_at(row)
        qkv = dot(s.a[at, :], s.w_self[:, : 3 * WIDE]) + s.bias[0:1, : 3 * WIDE]
        low = qkv.astype(BF16)
        s.qkv[at, :] = low
        queries = spread(low[:, :WIDE] * jnp.asarray(z.scale, BF16), heads)
        scores = dot_columns(queries, low[:, WIDE : 2 * WIDE])
        mask = self_mask(row)
        scores = jnp.concatenate(
            [
                jnp.where(mask, scores[head * length : (head + 1) * length], MASKED)
                for head in range(heads)
            ],
            axis=0,
        )
        probs = softmax(scores).astype(BF16)
        s.p_self[row] = probs
        mixed = fold(dot(probs, low[:, 2 * WIDE :]), heads, length).astype(BF16)
        s.o[at, :] = mixed
        s.part_row[row] = dot_columns(mixed, s.w_self[:, 3 * WIDE :]).astype(BF16)
        send_pairs(step, ("selfq", "selft"))

    pl.loop(0, rows // 2)(self_row)
    gather_forward("kv")
    ring_pass(first_pair, 0)
    ring_pass(last_pair, 0)
    pl.loop(rows // 2, rows)(self_row)
    sum_forward("selfq")
    sum_forward("selft")
    ring_pass(first_pair, 1)
    gather_forward("cross")
    ring_pass(last_pair, 1)
    gather_finish("kv")
    widen(s.m_kv, s.w_kv, 2)

    def project(values):
        return dot(values, s.w_kv[...]) + s.bias[2:3, : 2 * WIDE]

    def project_chunk(index):
        load_chunk(index).wait()
        result = project(s.chunk[lax.rem(index, CHUNKS_HELD)])

        @pl.when(index + CHUNKS_HELD < chunk_count)
        def _():
            load_chunk(index + CHUNKS_HELD).start()

        for tile in range(2 * WIDE // 128):
            s.stage[tile // 2, (tile % 2) * CHUNK : (tile % 2 + 1) * CHUNK, :] = result[
                :, tile * 128 : (tile + 1) * 128
            ]
        keys = CHUNK // z.images
        key_at = pl.ds(pl.multiple_of(index * keys, keys), keys)
        for image in range(z.images):
            for tile in range(2 * WIDE // 128):
                s.kv[image, key_at, tile * 128 : (tile + 1) * 128] = s.stage.at[tile // 2][
                    pl.ds((tile % 2) * CHUNK + image, keys, stride=z.images), :
                ].astype(BF16)

    third = chunk_count // 3
    pl.loop(0, third)(project_chunk)

    after = s.x_own[:query, :].astype(F32) + sum_finish("selfq") + vec(6)
    s.after_self[:query, :] = after
    normed, _ = norm_parts(after)
    s.c[rank] = (normed * vec(2) + vec(3)).astype(BF16)
    share_start("c")
    put_stat(1, after, weight_query)
    after = s.x_own[query:, :].astype(F32) + sum_finish("selft") + vec(6)
    s.after_self[query:, :] = after
    normed, _ = norm_parts(after)
    s.f_t[rank] = (normed * vec(4) + vec(5)).astype(BF16)
    share_start("ft")
    put_stat(1, after, weight_text)
    put_stat(2, after, weight_text)
    ring_pass(first_pair, 2)
    pl.loop(third, 2 * third)(project_chunk)
    ring_pass(last_pair, 2)
    pl.loop(2 * third, chunk_count)(project_chunk)
    load_tail.wait()
    last = project(s.tail[...])
    first_row = lax.broadcasted_iota(jnp.int32, (tail, 1), 0) == 0
    for image in range(z.images):
        s.kv[image, z.keys - 1 :, :] = jnp.where(
            first_row, jnp.broadcast_to(last[image : image + 1, :], last.shape), 0.0
        ).astype(BF16)
    load_chunks()
    share_forward("c")
    ring_pass(first_pair, 3)
    gather_finish("cross")
    widen(s.m_cross, s.w_cross, 2)
    share_finish("c")
    queries_total = rows * query
    cross_query = dot(s.c[...].reshape(queries_total, z.model), s.w_cross[:, :WIDE])
    s.qc[...] = (cross_query + s.bias[1:2, :WIDE]).astype(BF16).reshape(s.qc.shape)
    is_key = lanes(PADDED_KEYS) < z.keys

    def all_slots(ref):
        return ref[...].reshape(queries_total, WIDE)

    def slot_of(image):
        slot = jnp.int32(0)
        for other in range(1, z.images):
            slot = jnp.where(s.image_of[other] == image, other, slot)
        return slot

    def cross_queries(image):
        values = s.qc[slot_of(image)]
        return spread(values * jnp.asarray(z.scale, BF16), heads)

    unroll = 4
    groups = z.images // unroll

    def cross_group(group):
        for inner in range(unroll):
            image = group * unroll + inner
            scores = dot_columns(cross_queries(image), s.kv[image, :, :WIDE])
            probs = softmax(jnp.where(is_key, scores, MASKED)).astype(BF16)
            s.p_cross[image] = probs
            mixed = fold(dot(probs, s.kv[image, :, WIDE:]), heads, QUERIES)
            s.oc_image[image] = mixed.astype(BF16)

    pl.loop(0, groups // 2)(cross_group)
    ring_pass(last_pair, 3)
    pl.loop(groups // 2, groups)(cross_group)

    @pl.loop(0, z.images)
    def _(slot):
        s.oc[slot] = s.oc_image[s.image_of[slot]]

    share_forward("ft")
    ring_pass(first_pair, 4)
    sum_sent("selfq")
    sum_sent("selft")
    s.part_q[...] = (
        dot_columns(all_slots(s.oc), s.w_cross[:, WIDE:]).astype(BF16).reshape(s.part_q.shape)
    )
    sum_copy("cross", 0).start()
    sum_copy("cross", 1).start()
    sum_forward("cross")
    ring_pass(last_pair, 4)
    ring_pass(first_pair, 5)
    ring_pass(last_pair, 5)
    after_query = s.after_self[:query, :] + sum_finish("cross") + vec(7)
    s.after_query[...] = after_query
    normed, _ = norm_parts(after_query)
    s.f_q[rank] = (normed * vec(4) + vec(5)).astype(BF16)
    share_start("fq")
    put_stat(2, after_query, weight_query)
    ring_pass(first_pair, 6)
    ring_pass(last_pair, 6)
    ring_pass(first_pair, 7)
    share_forward("fq")
    share_finish("ft")
    load_gy.wait()
    gather_sent("self")
    gather_sent("kv")

    f_of = {0: s.f_q, 1: s.f_t}
    w_in = {0: s.m_in0, 1: s.m_in1}
    w_out = {0: s.m_out0, 1: s.m_out1}

    def grad_rows(kind, row):
        return s.gy[row, kind * query : (kind + 1) * query, :]

    def feed_forward(kind, target, send):
        for pair in (1 - chip, chip):
            values = f_of[kind][pl.ds(pair * 2, 2)].reshape(2 * query, z.model)
            grads = jnp.concatenate(
                [grad_rows(kind, pair * 2), grad_rows(kind, pair * 2 + 1)], axis=0
            )
            up = dot(values, w_in[kind][...]) + s.bias[3 + kind : 4 + kind, : z.hidden]
            share = 0.5 * (1.0 + lax.erf(up * (0.5**0.5)))
            hidden = (up * share).astype(BF16)
            slope = share + up * (jnp.exp(-0.5 * up * up) * ((0.5 / math.pi) ** 0.5))
            grad_up = (dot(grads, w_out[kind][...]) * slope).astype(BF16)
            at = pl.ds(pl.multiple_of(pair * 2 * query, 2 * query), 2 * query)
            if kind == 0:
                s.hid[at, :] = hidden
                s.gu[at, :] = grad_up
            else:
                s.m_self[at, :] = hidden
                cut = s.m_kv.shape[1]
                for first in range(0, z.hidden, cut):
                    below = pl.ds(pl.multiple_of(first // cut * queries_total + at.start, 16), at.size)
                    s.m_kv[below, :] = grad_up[:, first : first + cut]
            back = dot_columns(grad_up, w_in[kind][...]).astype(BF16)
            target[pl.ds(pair * 2, 2)] = back.reshape(2, query, z.model)
            send(pair)
            s.small[20 + kind : 21 + kind, :] += column_total(grad_up)
            out = dot_columns(hidden, w_out[kind][...]).astype(BF16)
            out = out.reshape(2, query, z.model)
            s.part_row[pl.ds(pair * 2, 2), kind * query : (kind + 1) * query, :] = out

    def weight_terms(kind):
        values = f_of[kind][...].reshape(queries_total, z.model)
        grads = jnp.concatenate([grad_rows(kind, row) for row in range(rows)], axis=0)
        if kind == 0:
            hidden, grad_up = s.hid[...], s.gu[...]
        else:
            hidden = s.m_self[:queries_total, :]
            grad_up = jnp.concatenate(
                [
                    s.m_kv[at : at + queries_total, :]
                    for at in range(0, z.hidden // s.m_kv.shape[1] * queries_total, queries_total)
                ],
                axis=1,
            )
        for name, left, right in (
            ("in%d" % kind, values, grad_up),
            ("out%d" % kind, grads, hidden),
        ):
            ring_gather_sent(name)
            for at in range(0, z.model, WIDE):
                whole[name][at : at + WIDE, :] = dot_rows(left[:, at : at + WIDE], right).astype(
                    BF16
                )

    hops = iter((0, 1))
    feed_forward(1, s.part_t, lambda pair: sum_copy("gft", next(hops)).start())
    ring_pass(last_pair, 7)
    sum_sent("cross")
    share_finish("fq")
    sum_forward("gft")
    sum_sent("gft", (0, 1))
    hops = iter((0, 1))
    feed_forward(0, s.part_q, lambda pair: sum_copy("gfq", next(hops)).start())
    sum_forward("gfq")
    weight_terms(1)
    scatter_pass(first_pair, 0)

    def own_back(total, after, grads, slot):
        normed, scale = norm_parts(after)
        s.small[4:5, :] += column_total(total * normed)
        s.small[5:6, :] += column_total(total)
        s.small[slot : slot + 1, :] += column_total(grads)
        return grads.astype(F32) + norm_grad(normed, scale, vec(4), total)

    grad_text = own_back(sum_finish("gft"), s.after_self[query:, :], grad_rows(1, rank), 9)
    s.g_own[query:, :] = grad_text
    grad_text_low = grad_text.astype(BF16)
    s.gsa_t[rank] = grad_text_low
    s.small[6:7, :] += column_total(grad_text_low)
    share_start("gsat")
    weight_terms(0)
    share_sent("fq")
    grad_query = own_back(sum_finish("gfq"), s.after_query[...], grad_rows(0, rank), 8)
    s.g_own[:query, :] = grad_query
    grad_query_low = grad_query.astype(BF16)
    s.part_t[rank] = grad_query_low
    s.small[7:8, :] += column_total(grad_query_low)
    share_start("gca")
    scatter_pass(("in1",), 1)
    scatter_pass(last_pair, 0)
    scatter_pass(("out1",), 1)
    sum_copy("out", 0).start()
    sum_copy("out", 1).start()
    share_forward("gsat")
    sum_forward("out")
    scatter_pass(("in1",), 2)
    scatter_pass(("in0",), 1)
    share_forward("gca")
    scatter_pass(("out0",), 1)
    share_finish("gsat")
    share_finish("gca")

    grad_mixed = dot(s.part_t[...].reshape(queries_total, z.model), s.w_cross[:, WIDE:])
    s.goc[...] = grad_mixed.astype(BF16).reshape(s.goc.shape)

    def stage_put(image, values):
        for tile in range(WIDE // 128):
            s.stage.at[tile][pl.ds(image, PADDED_KEYS, stride=z.images), :] = values[
                :, tile * 128 : (tile + 1) * 128
            ]

    def cross_back(group):
        for inner in range(unroll):
            image = group * unroll + inner
            grads = spread(s.goc[slot_of(image)], heads)
            probs = s.p_cross[image]
            wide = probs.astype(F32)
            grad_probs = dot_columns(grads, s.kv[image, :, WIDE:])
            delta = jnp.sum(wide * grad_probs, axis=-1, keepdims=True)
            grad_scores = (wide * (grad_probs - delta)).astype(BF16)
            mixed = fold(dot(grad_scores, s.kv[image, :, :WIDE]), heads, QUERIES) * z.scale
            s.kv[image, : heads * QUERIES, :PADDED_KEYS] = grad_scores
            s.oc_image[image] = mixed.astype(BF16)

    pl.loop(0, groups)(cross_back)

    @pl.loop(0, z.images)
    def _(slot):
        s.gqc[slot] = s.oc_image[s.image_of[slot]]

    sum_sent("gfq")
    sum_sent("gft", (2,))
    s.part_q[...] = (
        dot_columns(all_slots(s.gqc), s.w_cross[:, :WIDE]).astype(BF16).reshape(s.part_q.shape)
    )
    sum_copy("gc", 0).start()
    sum_copy("gc", 1).start()
    scatter_pass(("out1",), 2)
    scatter_pass(("in1",), 3)
    scatter_pass(last_pair, 2)
    s.small[18:19, :WIDE] += column_total(all_slots(s.gqc))
    low_half = lanes(128) < HEAD
    gather_sent("cross")
    grad_cq = dot_rows(s.c[...].reshape(queries_total, z.model), all_slots(s.gqc))
    grad_co = dot_rows(s.part_t[...].reshape(queries_total, z.model), all_slots(s.oc))
    s.m_cross[:, :128] = grad_cq[:, :128].astype(BF16)
    s.m_cross[:, 128:256] = grad_co[:, :128].astype(BF16)
    s.m_cross[:, 256:] = jnp.where(
        low_half, grad_cq[:, 128:], pltpu.roll(grad_co[:, 128:], HEAD, 1)
    ).astype(BF16)
    sum_forward("gc")
    scatter_start("cross")

    after_ffn_sum = sum_finish("out")
    after_query_out = s.after_query[...] + after_ffn_sum[:query] + vec(8)
    after_text_out = s.after_self[query:, :] + after_ffn_sum[query:] + vec(9)
    put_stat(3, after_query_out, weight_query)
    put_stat(3, after_text_out, weight_text)
    s.gy[rank, :query, :] = after_query_out.astype(BF16)
    s.gy[rank, query:, :] = after_text_out.astype(BF16)
    share_start("out")

    def key_grad(image):
        grad_scores = s.kv[image, : heads * QUERIES, :PADDED_KEYS]
        return dot_rows(grad_scores, cross_queries(image))

    def value_grad(image):
        return dot_rows(s.p_cross[image], spread(s.goc[slot_of(image)], heads))

    def grads_at(at):
        return jnp.concatenate(
            [s.stage[tile, at, :].astype(BF16) for tile in range(WIDE // 128)], axis=1
        )

    def features_start(grad_of):
        @pl.loop(0, groups)
        def _(group):
            for inner in range(unroll):
                image = group * unroll + inner
                stage_put(image, grad_of(image))

        grads = grads_at(pl.ds(chunk_count * CHUNK, tail))
        s.turned[...] = dot_rows(grads, s.tail[...])
        s.col_sum[...] = column_total(grads)

    def features_chunk(index):
        load_chunk(index).wait()
        grads = grads_at(pl.ds(pl.multiple_of(index * CHUNK, CHUNK), CHUNK))
        s.turned[...] += dot_rows(grads, s.chunk[lax.rem(index, CHUNKS_HELD)])
        s.col_sum[...] += column_total(grads)

        @pl.when(index + CHUNKS_HELD < chunk_count)
        def _():
            load_chunk(index + CHUNKS_HELD).start()

    features_start(key_grad)
    scatter_pass(("out1",), 3)
    scatter_pass(("in1",), 4)
    scatter_pass(("in0",), 3)
    pl.loop(0, chunk_count)(features_chunk)
    load_chunks()
    turned = s.turned[...].T
    s.m_kv[:, :128] = turned[:, :128].astype(BF16)
    s.m_kv[:, 256:] = turned[:, 128:].astype(BF16)

    cross_sum = sum_finish("gc")
    normed, scale = norm_parts(s.after_self[:query, :])
    s.small[2:3, :] += column_total(cross_sum * normed)
    s.small[3:4, :] += column_total(cross_sum)
    grad_query = s.g_own[:query, :] + norm_grad(normed, scale, vec(2), cross_sum)
    s.g_own[:query, :] = grad_query
    grad_query_low = grad_query.astype(BF16)
    s.f_q[rank] = grad_query_low
    s.small[6:7, :] += column_total(grad_query_low)
    share_start("gsaq")
    scatter_pass(("out0",), 3)
    scatter_forward("cross")
    features_start(value_grad)
    scatter_pass(("out1",), 4)
    scatter_pass(("in1",), 5)
    pl.loop(0, chunk_count)(features_chunk)
    s.small[19:20, :WIDE] += s.col_sum[...]
    turned = s.turned[...].T
    s.m_kv[:, 128:256] = turned[:, :128].astype(BF16)
    s.m_kv[:, 256:] = jnp.where(
        low_half, s.m_kv[:, 256:].astype(F32), pltpu.roll(turned[:, 128:], HEAD, 1)
    ).astype(BF16)
    share_forward("gsaq")
    scatter_pass(last_pair, 4)
    scatter_start("kv")
    share_forward("out")
    share_finish("gsaq")

    def self_back(step):
        row = send_order(step)
        at = row_at(row)
        grads = jnp.concatenate([s.f_q[row], s.gsa_t[row]], axis=0)
        low = s.qkv[at, :]
        queries = spread(low[:, :WIDE] * jnp.asarray(z.scale, BF16), heads)
        grad_mixed = dot(grads, s.w_self[:, 3 * WIDE :]).astype(BF16)
        grad_mixed = spread(grad_mixed, heads)
        probs = s.p_self[row]
        wide = probs.astype(F32)
        grad_probs = dot_columns(grad_mixed, low[:, 2 * WIDE :])
        delta = jnp.sum(wide * grad_probs, axis=-1, keepdims=True)
        grad_scores = (wide * (grad_probs - delta)).astype(BF16)
        grad_q = fold(dot(grad_scores, low[:, WIDE : 2 * WIDE]), heads, length) * z.scale
        grad_k = dot_rows(grad_scores, queries)
        grad_v = dot_rows(probs, grad_mixed)
        grad_low = jnp.concatenate([grad_q, grad_k, grad_v], axis=1).astype(BF16)
        s.qkv[at, :] = grad_low
        s.small[16:17, :WIDE] += column_total(grad_low[:, :WIDE])
        s.small[17:18, :WIDE] += column_total(grad_low[:, 2 * WIDE :])
        s.part_row[row] = dot_columns(grad_low, s.w_self[:, : 3 * WIDE]).astype(BF16)
        send_pairs(step, ("gaq", "gat"))

    scatter_pass(("out1",), 5)
    sum_sent("out")
    sum_sent("gc")
    pl.loop(0, rows // 2)(self_back)
    scatter_pass(("in1",), 6)
    scatter_pass(last_pair, 5)
    pl.loop(rows // 2, rows)(self_back)
    sum_forward("gaq")
    sum_forward("gat")

    grads_all = [dot_rows(s.a[...], s.qkv[:, i * WIDE : (i + 1) * WIDE]) for i in range(3)]
    grad_stream = jnp.concatenate(
        [ref[row] for row in range(rows) for ref in (s.f_q, s.gsa_t)], axis=0
    )
    grads_all.append(dot_rows(grad_stream, s.o[...]))
    for i, value in enumerate(grads_all):
        s.m_self[:, i * 128 : (i + 1) * 128] = value[:, :128].astype(BF16)
    for i in range(2):
        s.m_self[:, (4 + i) * 128 : (5 + i) * 128] = jnp.where(
            low_half, grads_all[2 * i][:, 128:], pltpu.roll(grads_all[2 * i + 1][:, 128:], HEAD, 1)
        ).astype(BF16)
    scatter_start("self")
    scatter_pass(("out1",), 6)
    scatter_forward("kv")
    scatter_pass(("in1",), 7)
    scatter_pass(last_pair, 6)

    def stream_back(name, at):
        total = sum_finish(name)
        normed, scale = norm_parts(s.x_own[at, :].astype(F32))
        s.small[0:1, :] += column_total(total * normed)
        s.small[1:2, :] += column_total(total)
        grad = s.g_own[at, :] + norm_grad(normed, scale, vec(0), total)
        s.x[rank, at, :] = grad.astype(BF16)

    stream_back("gaq", pl.ds(0, query))
    share_start("sgq")
    stream_back("gat", pl.ds(query, text))
    share_start("sgt")
    scatter_forward("self")
    scatter_pass(("out1",), 7)

    def small_copy(source, hop, device):
        target = s.small_in.at[hop] if source is s.small else s.small_in.at[hop, pl.ds(0, 16)]
        return remote(source, target, (s.small_send, s.small_recv), (hop,), device)

    shared_rows = s.small.at[pl.ds(0, 16)]
    for hop, device in enumerate(((place, beside), (place, far))):
        item = small_copy(shared_rows, hop, device)
        item.start()
        item.wait()
        s.small[:16, :] += s.small_in[hop, :16, :]
    item = small_copy(s.small, 2, across)
    item.start()
    share_forward("sgq")
    share_forward("sgt")
    item.wait()
    s.small[...] += s.small_in[2]
    items = [small_copy(s.small, 2 + step, along(step)) for step in range(1, lines)]
    for item in items:
        item.start()
    share_finish("out")
    store_out = pltpu.make_async_copy(s.gy, s.out_h, s.load_sem.at[3])
    store_out.start()
    share_finish("sgq")
    share_finish("sgt")
    store_sg = pltpu.make_async_copy(s.x, s.sg_h, s.load_sem.at[4])
    store_sg.start()
    total = s.small[...]
    for step in range(1, lines):
        items[step - 1].wait_recv()
        total = total + s.small_in[2 + step]
    s.small_out[...] = total
    scatter_pass(last_pair, 7)
    for name in TERMS:
        scatter_finish(name)
    for name in RINGED:
        ring_scatter_sent(name)
    for item in items:
        item.wait_send()
    gather_sent("vec")
    for name in ("gaq", "gat"):
        sum_sent(name)
    for name in SHARES:
        if name != "fq":
            share_sent(name)
    store_out.wait()
    store_sg.wait()


def finish_kernel(
    out_in,
    grad_in,
    own_self,
    own_kv,
    own_cross,
    own_ffn,
    small,
    out_stream,
    stream_grad,
    grad_qkv,
    grad_out,
    grad_cq,
    grad_ckv,
    grad_co,
    grad_in_w,
    grad_out_w,
    grad_vectors,
    grad_heads,
    grad_hidden,
    rms,
):
    out_stream[...] = out_in[...]
    stream_grad[...] = grad_in[...].astype(F32)

    def piece(packed, count, index):
        at = (count + index // 2) * 128 + index % 2 * HEAD
        return packed[:, index * 128 : (index + 1) * 128], packed[:, at : at + HEAD]

    def put(ref, pieces):
        ref[:, :128] = pieces[0]
        ref[:, 128:] = pieces[1]

    def put_turned(ref, pieces):
        ref[:128, :] = pieces[0].T
        ref[128:, :] = pieces[1].T

    for index in range(3):
        put(grad_qkv.at[index], piece(own_self, 4, index))
    put_turned(grad_out, piece(own_self, 4, 3))
    put(grad_cq, piece(own_cross, 2, 0))
    put_turned(grad_co, piece(own_cross, 2, 1))
    for index in range(2):
        put(grad_ckv.at[index], piece(own_kv, 2, index))
        fan = grad_in_w.shape[1]
        grad_in_w[index] = own_ffn[index * fan : (index + 1) * fan, :]
        grad_out_w[index] = own_ffn[(2 + index) * fan : (3 + index) * fan, :]
    place, own = lax.axis_index("dp"), grad_vectors.shape[1]
    total = jnp.zeros(grad_vectors.shape, F32)
    for index in range(small.shape[1] // own):
        mine = small[: total.shape[0], index * own : (index + 1) * own]
        total = total + jnp.where(place == index, mine, 0.0)
    grad_vectors[...] = total
    grad_heads[...] = small[16:20, : grad_heads.shape[1]]
    grad_hidden[...] = small[20:22, : grad_hidden.shape[1]]
    stats = small[10:11, :128]
    valid = jnp.sum(jnp.where(lanes(128) == 4, stats, 0.0), axis=1, keepdims=True)
    rms[...] = jnp.sqrt(stats / (valid * small.shape[1]))[:, :4]


def layer(
    stream_in,
    features,
    image_index,
    text_segment,
    text_valid,
    self_qkv,
    self_out,
    cross_q,
    cross_kv,
    cross_out,
    ffn_in,
    ffn_out,
    vectors,
    head_bias,
    ffn_bias,
    out_grad,
):
    count = lax.axis_size("dp")
    tokens, model = stream_in.shape
    width, hidden = self_qkv.shape[2], ffn_in.shape[2]
    fan, feat_fan = ffn_in.shape[1], cross_kv.shape[1]
    rows, text = text_segment.shape
    images, keys, feat = features.shape
    query = SLOTS * QUERIES
    z = types.SimpleNamespace(
        count=count,
        rows=rows,
        width=width,
        heads=width // HEAD,
        fan=fan,
        feat_fan=feat_fan,
        model=model,
        hidden=hidden,
        features=images * keys,
        images=images,
        keys=keys,
        scale=HEAD**-0.5,
    )
    lines = count // 2

    operands = {
        "image_of": image_index.reshape(-1),
        "vectors": vectors,
        "self_qkv": self_qkv,
        "self_out": self_out,
        "cross_q": cross_q,
        "cross_kv": cross_kv,
        "cross_out": cross_out,
        "ffn_out": ffn_out.transpose(0, 2, 1),
        "head_bias": head_bias,
        "ffn_bias": ffn_bias,
        "segment": text_segment,
        "valid": text_valid,
        "ffn_in": ffn_in,
        "x_h": stream_in.reshape(rows, ROW_LEN, model),
        "gy_h": out_grad.reshape(rows, ROW_LEN, model),
        "feat_h": features.transpose(1, 0, 2).reshape(keys * images, feat),
    }
    spaces = dict.fromkeys(operands, pltpu.VMEM) | {"image_of": pltpu.SMEM}
    spaces |= dict.fromkeys(("ffn_in", "x_h", "gy_h", "feat_h"), pl.ANY)
    results = {
        "out_h": ((rows, ROW_LEN, model), BF16),
        "sg_h": ((rows, ROW_LEN, model), BF16),
        "own_self": ((fan, 4 * width), F32),
        "own_kv": ((feat_fan, 2 * width), F32),
        "own_cross": ((fan, 2 * width), F32),
        "own_ffn": ((4 * fan, hidden), F32),
        "small_out": ((24, model), F32),
    }
    chunk_rows = (keys + PADDED_KEYS - keys) * images
    buffers = {
        "w_vec": ((count * 16, 128), BF16),
        "vecs": ((16, model), F32),
        "bias": ((8, max(3 * WIDE, hidden)), F32),
        "code": ((rows, ROW_LEN), F32),
        "text_codes": ((rows, text, 1), F32),
        "weight": ((text, 1), F32),
        "m_self": ((model, 4 * width), BF16),
        "m_kv": ((feat, 2 * width), BF16),
        "m_cross": ((model, 2 * width), BF16),
        "w_self": ((model, 4 * WIDE), BF16),
        "w_kv": ((feat, 2 * WIDE), BF16),
        "w_cross": ((model, 2 * WIDE), BF16),
        "x": ((rows, ROW_LEN, model), BF16),
        "x_own": ((ROW_LEN, model), BF16),
        "gy": ((rows, ROW_LEN, model), BF16),
        "a": ((tokens, model), BF16),
        "qkv": ((tokens, 3 * WIDE), BF16),
        "o": ((tokens, WIDE), BF16),
        "p_self": ((rows, z.heads * ROW_LEN, ROW_LEN), BF16),
        "c": ((rows, query, model), BF16),
        "f_q": ((rows, query, model), BF16),
        "f_t": ((rows, query, model), BF16),
        "gsa_t": ((rows, query, model), BF16),
        "qc": ((images, QUERIES, WIDE), BF16),
        "gqc": ((images, QUERIES, WIDE), BF16),
        "goc": ((images, QUERIES, WIDE), BF16),
        "oc": ((images, QUERIES, WIDE), BF16),
        "oc_image": ((images, QUERIES, WIDE), BF16),
        "kv": ((images, PADDED_KEYS, 2 * WIDE), BF16),
        "p_cross": ((images, z.heads * QUERIES, PADDED_KEYS), BF16),
        "stage": ((WIDE // 128, PADDED_KEYS * images, 128), F32),
        "turned": ((WIDE, feat), F32),
        "col_sum": ((1, WIDE), F32),
        "chunk": ((CHUNKS_HELD, CHUNK, feat), BF16),
        "tail": ((images * keys % CHUNK, feat), BF16),
        "hid": ((rows * query, hidden), BF16),
        "gu": ((rows * query, hidden), BF16),
        "part_row": ((rows, ROW_LEN, model), BF16),
        "part_q": ((rows, query, model), BF16),
        "part_t": ((rows, query, model), BF16),
        "after_self": ((ROW_LEN, model), F32),
        "after_query": ((query, model), F32),
        "g_own": ((ROW_LEN, model), F32),
        "small": ((24, model), F32),
        "small_in": ((2 + lines, 24, model), F32),
    }
    for name in ("in0", "in1", "out0", "out1"):
        buffers["m_" + name] = ((model, hidden), BF16)
        buffers["r_" + name] = ((count - 1, fan, hidden), BF16)
    for name in ("selfq", "selft", "out", "cross", "gft", "gfq"):
        block = (ROW_LEN if name == "out" else query, model)
        buffers["pin_" + name] = ((2, *block), BF16)
        buffers["fin_" + name] = (block, BF16)
    buffers["half_row"] = ((ROW_LEN, model), BF16)
    buffers["half"] = ((2, query, model), BF16)
    for name in TERMS:
        high = feat_fan if name == "kv" else fan
        across = (4 if name == "self" else 2) * width
        buffers["y_" + name] = ((lines, high, across), BF16)
        buffers["z_" + name] = ((lines - 1, high, across), BF16)
    semaphores = {
        "own_sem": (2,),
        "load_sem": (5,),
        "chunk_sem": (CHUNKS_HELD,),
    }
    for name in ("gl_send", "gl_recv", "gs_send", "gs_recv"):
        semaphores[name] = (len(PIECES), lines)
    for name in ("ss_send", "ss_recv", "sl_send", "sl_recv"):
        semaphores[name] = (len(TERMS), lines)
    for kind in ("send", "recv"):
        semaphores["rg_" + kind] = (len(RINGED), 2, count - 1)
        semaphores["rs_" + kind] = (len(RINGED), 2, count - 1)
        semaphores["sum_" + kind] = (len(SUMS), 3)
        semaphores["share_" + kind] = (len(SHARES), 3)
        semaphores["small_" + kind] = (2 + lines,)
    names = (*operands, *results, *buffers, *semaphores)
    held = ("out_h", "sg_h")
    done = pl.pallas_call(
        functools.partial(layer_kernel, names, z),
        out_shape=[jax.ShapeDtypeStruct(*item) for item in results.values()],
        in_specs=[pl.BlockSpec(memory_space=spaces[name]) for name in operands],
        out_specs=[
            pl.BlockSpec(memory_space=pl.ANY if name in held else pltpu.VMEM) for name in results
        ],
        scratch_shapes=[pltpu.VMEM(*item) for item in buffers.values()]
        + [pltpu.SemaphoreType.DMA(item) for item in semaphores.values()],
        compiler_params=pltpu.CompilerParams(
            collective_id=0, has_side_effects=True, vmem_limit_bytes=VMEM_LIMIT
        ),
    )(*operands.values())
    local = [
        ((rows, ROW_LEN, model), BF16),
        ((rows, ROW_LEN, model), F32),
        (self_qkv.shape, F32),
        (self_out.shape, F32),
        (cross_q.shape, F32),
        (cross_kv.shape, F32),
        (cross_out.shape, F32),
        (ffn_in.shape, F32),
        (ffn_in.shape, F32),
        (vectors.shape, F32),
        (head_bias.shape, F32),
        (ffn_bias.shape, F32),
        ((1, 4), F32),
    ]
    inside = pl.BlockSpec(memory_space=pltpu.VMEM)
    out_all, grad_all, *others, grad_down, grad_vectors, grad_heads, grad_hidden, rms = pl.pallas_call(
        finish_kernel,
        out_shape=[jax.ShapeDtypeStruct(*item) for item in local],
        in_specs=[inside] * len(done),
        out_specs=[inside] * len(local),
        compiler_params=pltpu.CompilerParams(vmem_limit_bytes=VMEM_LIMIT),
    )(*done)
    return (
        out_all.reshape(tokens, model),
        grad_all.reshape(tokens, model),
        *others,
        grad_down.transpose(0, 2, 1),
        grad_vectors,
        grad_heads,
        grad_hidden,
        rms.reshape(4),
    )


def layer_norm(values, gain_row, shift_row):
    row_mean = jnp.mean(values, axis=-1, keepdims=True)
    centred = values - row_mean
    row_var = jnp.mean(centred * centred, axis=-1, keepdims=True)
    return centred * lax.rsqrt(row_var + EPSILON) * gain_row + shift_row


def norm_back(values, gain_row, shift_row, grad_normed):
    pull_back = jax.vjp(layer_norm, values, gain_row, shift_row)[1]
    return pull_back(grad_normed)


def gelu_exact(values):
    return jax.nn.gelu(values, approximate=False)


def round_low(values):
    return values.astype(jnp.bfloat16)


def matmul(left_side, right_side):
    return jnp.dot(left_side, right_side, preferred_element_type=jnp.float32)


def matmul_left(left_side, right_side):
    return lax.dot_general(
        left_side, right_side, (((0,), (0,)), ((), ())), preferred_element_type=jnp.float32
    )


def matmul_right(left_side, right_side):
    return lax.dot_general(
        left_side, right_side, (((1,), (1,)), ((), ())), preferred_element_type=jnp.float32
    )


def column_sum(values):
    return jnp.sum(values.astype(jnp.float32), axis=0)


def attn_scores(queries, keys_in, key_mask):
    score_scale = queries.shape[-1] ** (-0.5)
    scores = (
        jnp.einsum("bqhe,bkhe->bhqk", queries, keys_in, preferred_element_type=jnp.float32)
        * score_scale
    )
    if key_mask is None:
        return scores
    return jnp.where(key_mask[:, None], scores, MASKED)


def attend(queries, keys_in, values_in, key_mask):
    scores = attn_scores(queries, keys_in, key_mask)
    row_max = jnp.max(scores, axis=-1, keepdims=True)
    exponent = jnp.exp(scores - row_max)
    row_total = jnp.sum(exponent, axis=-1, keepdims=True)
    attn_probs = round_low(exponent / row_total)
    mixed_out = jnp.einsum(
        "bhqk,bkhe->bqhe", attn_probs, values_in, preferred_element_type=jnp.float32
    )
    return (round_low(mixed_out), row_max + jnp.log(row_total))


def attend_back(queries, keys_in, values_in, key_mask, log_total, grad_mixed):
    score_scale = queries.shape[-1] ** (-0.5)
    attn_probs = jnp.exp(attn_scores(queries, keys_in, key_mask) - log_total)
    grad_values = jnp.einsum(
        "bhqk,bqhe->bkhe", round_low(attn_probs), grad_mixed, preferred_element_type=jnp.float32
    )
    grad_probs = jnp.einsum(
        "bqhe,bkhe->bhqk", grad_mixed, values_in, preferred_element_type=jnp.float32
    )
    row_delta = jnp.sum(attn_probs * grad_probs, axis=-1, keepdims=True)
    grad_scores = round_low(attn_probs * (grad_probs - row_delta))
    grad_queries = (
        jnp.einsum("bhqk,bkhe->bqhe", grad_scores, keys_in, preferred_element_type=jnp.float32)
        * score_scale
    )
    grad_keys = (
        jnp.einsum("bhqk,bqhe->bkhe", grad_scores, queries, preferred_element_type=jnp.float32)
        * score_scale
    )
    return (round_low(grad_queries), round_low(grad_keys), round_low(grad_values))


def heads_total(partial_terms):
    return lax.psum(partial_terms, "mp")


def inputs_total(partial_terms):
    return lax.psum(partial_terms, "mp")


def ffn_forward(normed_low, weight_up, bias_up, weight_down):
    up_value = matmul(normed_low, weight_up) + bias_up
    hidden = round_low(gelu_exact(up_value))
    return (up_value, hidden, matmul(hidden, weight_down))


def ffn_back(normed_low, up_value, hidden, weight_up, weight_down, grad_low):
    grad_down = matmul_left(hidden, grad_low)
    grad_hidden = matmul_right(grad_low, weight_down)
    grad_up = round_low(jax.vjp(gelu_exact, up_value)[1](grad_hidden)[0])
    grad_in = matmul_left(normed_low, grad_up)
    return (grad_in, grad_down, column_sum(grad_up), matmul_right(grad_up, weight_up))


def body(
    stream_in,
    features,
    image_index,
    text_segment,
    text_valid,
    self_qkv,
    self_out,
    cross_q,
    cross_kv,
    cross_out,
    ffn_in,
    ffn_out,
    vectors,
    head_bias,
    ffn_bias,
    out_grad,
):
    gathered = (
        lax.all_gather(self_qkv, "dp", axis=1, tiled=True),
        lax.all_gather(self_out, "dp", axis=1, tiled=True),
        lax.all_gather(cross_q, "dp", axis=0, tiled=True),
        lax.all_gather(cross_kv, "dp", axis=1, tiled=True),
        lax.all_gather(cross_out, "dp", axis=1, tiled=True),
        lax.all_gather(ffn_in, "dp", axis=1, tiled=True),
        lax.all_gather(ffn_out, "dp", axis=2, tiled=True),
        lax.all_gather(vectors, "dp", axis=1, tiled=True),
    )
    qkv_w, proj_w, cq_w, ckv_w, cproj_w, up_w, down_w, vector_low = gathered
    vecs = vector_low.astype(jnp.float32)
    bias_heads = head_bias.astype(jnp.float32)
    bias_hidden = ffn_bias.astype(jnp.float32)
    stream = stream_in.astype(jnp.float32)
    tokens, model_width = stream.shape
    row_count = tokens // ROW_LEN
    query_count = SLOTS * QUERIES
    text_len = ROW_LEN - query_count
    local_width = qkv_w.shape[2]
    local_heads = local_width // HEAD
    query_segment = jnp.arange(query_count, dtype=jnp.int32) // QUERIES
    segment = jnp.concatenate(
        [jnp.broadcast_to(query_segment, (row_count, query_count)), text_segment], axis=1
    )
    valid = (
        jnp.concatenate([jnp.ones((row_count, query_count), jnp.int32), text_valid], axis=1) == 1
    )
    key_mask = (segment[:, :, None] == segment[:, None, :]) & valid[:, None, :]
    heads_shape = (row_count, ROW_LEN, local_heads, HEAD)
    normed_low = round_low(layer_norm(stream, vecs[0], vecs[1]))
    self_query = round_low(matmul(normed_low, qkv_w[0]) + bias_heads[0]).reshape(heads_shape)
    self_key = round_low(matmul(normed_low, qkv_w[1])).reshape(heads_shape)
    self_value = round_low(matmul(normed_low, qkv_w[2]) + bias_heads[1]).reshape(heads_shape)
    self_mixed, self_total = attend(self_query, self_key, self_value, key_mask)
    self_mixed = self_mixed.reshape(tokens, local_width)
    self_term = matmul(self_mixed, proj_w).reshape(row_count, ROW_LEN, model_width)
    after_self = stream + heads_total(self_term.reshape(tokens, model_width)) + vecs[6]
    self_rows = after_self.reshape(row_count, ROW_LEN, model_width)
    query_part = self_rows[:, :query_count].reshape(-1, model_width)
    cross_normed = round_low(layer_norm(query_part, vecs[2], vecs[3]))
    slot_count = row_count * SLOTS
    cross_query = round_low(matmul(cross_normed, cq_w) + bias_heads[2]).reshape(
        slot_count, QUERIES, local_heads, HEAD
    )
    image_order = image_index.reshape(-1)
    pick_table = (image_order[:, None] == jnp.arange(image_order.shape[0])[None, :]).astype(
        jnp.bfloat16
    )
    keys_all = round_low(
        jnp.einsum("nkf,fc->nkc", features, ckv_w[0], preferred_element_type=jnp.float32)
    )
    values_all = round_low(
        jnp.einsum("nkf,fc->nkc", features, ckv_w[1], preferred_element_type=jnp.float32)
        + bias_heads[3]
    )
    cross_keys = round_low(
        jnp.einsum("ij,jkc->ikc", pick_table, keys_all, preferred_element_type=jnp.float32)
    )
    cross_values = round_low(
        jnp.einsum("ij,jkc->ikc", pick_table, values_all, preferred_element_type=jnp.float32)
    )
    cross_keys = cross_keys.reshape(slot_count, KEYS, local_heads, HEAD)
    cross_values = cross_values.reshape(slot_count, KEYS, local_heads, HEAD)
    cross_mixed, cross_total = attend(cross_query, cross_keys, cross_values, None)
    cross_mixed = cross_mixed.reshape(-1, local_width)
    cross_term = matmul(cross_mixed, cproj_w).reshape(row_count, query_count, model_width)
    after_query = query_part + heads_total(cross_term.reshape(-1, model_width)) + vecs[7]
    after_cross = jnp.concatenate(
        [after_query.reshape(row_count, query_count, model_width), self_rows[:, query_count:]],
        axis=1,
    ).reshape(tokens, model_width)
    ffn_normed = round_low(layer_norm(after_cross, vecs[4], vecs[5])).reshape(
        row_count, ROW_LEN, model_width
    )
    ffn_query = ffn_normed[:, :query_count].reshape(-1, model_width)
    ffn_text = ffn_normed[:, query_count:].reshape(-1, model_width)
    up_query, hidden_query, part_query = ffn_forward(ffn_query, up_w[0], bias_hidden[0], down_w[0])
    up_text, hidden_text, part_text = ffn_forward(ffn_text, up_w[1], bias_hidden[1], down_w[1])
    ffn_terms = jnp.concatenate(
        [
            part_query.reshape(row_count, query_count, model_width),
            part_text.reshape(row_count, text_len, model_width),
        ],
        axis=1,
    )
    query_flag = jnp.arange(ROW_LEN) < query_count
    bias_rows = jnp.where(query_flag[:, None], vecs[8], vecs[9])
    ffn_sum = heads_total(ffn_terms.reshape(tokens, model_width)).reshape(
        row_count, ROW_LEN, model_width
    )
    after_ffn = after_cross + (ffn_sum + bias_rows).reshape(tokens, model_width)
    token_weight = valid.reshape(-1).astype(jnp.float32)
    stream_stats = jnp.stack(
        [
            jnp.sum(token_weight * jnp.sum(section * section, axis=1))
            for section in (stream, after_self, after_cross, after_ffn)
        ]
        + [jnp.sum(token_weight)]
    )
    out_low = round_low(after_ffn)
    regathered = (
        lax.all_gather(self_qkv, "dp", axis=1, tiled=True),
        lax.all_gather(self_out, "dp", axis=1, tiled=True),
        lax.all_gather(cross_q, "dp", axis=0, tiled=True),
        lax.all_gather(cross_kv, "dp", axis=1, tiled=True),
        lax.all_gather(cross_out, "dp", axis=1, tiled=True),
        lax.all_gather(ffn_in, "dp", axis=1, tiled=True),
        lax.all_gather(ffn_out, "dp", axis=2, tiled=True),
        lax.all_gather(vectors, "dp", axis=1, tiled=True),
    )
    qkv_w, proj_w, cq_w, ckv_w, cproj_w, up_w, down_w, vector_low = regathered
    vecs = vector_low.astype(jnp.float32)
    grad_out = out_grad.astype(jnp.float32)
    grad_out_rows = grad_out.reshape(row_count, ROW_LEN, model_width)
    grad_low = round_low(grad_out_rows)
    grad_low_query = grad_low[:, :query_count].reshape(-1, model_width)
    grad_low_text = grad_low[:, query_count:].reshape(-1, model_width)
    in_query, down_query, hidden_bias_query, normed_grad_query = ffn_back(
        ffn_query, up_query, hidden_query, up_w[0], down_w[0], grad_low_query
    )
    in_text, down_text, hidden_bias_text, normed_grad_text = ffn_back(
        ffn_text, up_text, hidden_text, up_w[1], down_w[1], grad_low_text
    )
    normed_grad_q = normed_grad_query.reshape(row_count, query_count, model_width)
    normed_grad_t = normed_grad_text.reshape(row_count, text_len, model_width)
    normed_grad = jnp.concatenate([normed_grad_q, normed_grad_t], axis=1)
    normed_grad = inputs_total(normed_grad.reshape(tokens, model_width))
    cross_back, gain_three, shift_three = norm_back(after_cross, vecs[4], vecs[5], normed_grad)
    grad_cross = grad_out + cross_back
    grad_cross_rows = grad_cross.reshape(row_count, ROW_LEN, model_width)
    grad_branch_cross = round_low(grad_cross_rows[:, :query_count].reshape(-1, model_width))
    grad_cproj = matmul_left(cross_mixed, grad_branch_cross)
    grad_cross_mixed = round_low(matmul_right(grad_branch_cross, cproj_w)).reshape(
        cross_query.shape
    )
    grad_cq_part, grad_ck_part, grad_cv_part = attend_back(
        cross_query, cross_keys, cross_values, None, cross_total, grad_cross_mixed
    )
    grad_cq_part = grad_cq_part.reshape(-1, local_width)
    grad_ck_all = round_low(
        jnp.einsum(
            "ij,ikc->jkc",
            pick_table,
            grad_ck_part.reshape(-1, KEYS, local_width),
            preferred_element_type=jnp.float32,
        )
    )
    grad_cv_all = round_low(
        jnp.einsum(
            "ij,ikc->jkc",
            pick_table,
            grad_cv_part.reshape(-1, KEYS, local_width),
            preferred_element_type=jnp.float32,
        )
    )
    grad_ckv = jnp.stack(
        [
            jnp.einsum("nkf,nkc->fc", features, grad_ck_all, preferred_element_type=jnp.float32),
            jnp.einsum("nkf,nkc->fc", features, grad_cv_all, preferred_element_type=jnp.float32),
        ]
    )
    grad_cq = matmul_left(cross_normed, grad_cq_part)
    cross_grad_term = matmul_right(grad_cq_part, cq_w)
    cross_normed_grad = inputs_total(cross_grad_term)
    query_back, gain_two, shift_two = norm_back(query_part, vecs[2], vecs[3], cross_normed_grad)
    grad_self = jnp.concatenate(
        [
            grad_cross_rows[:, :query_count]
            + query_back.reshape(row_count, query_count, model_width),
            grad_cross_rows[:, query_count:],
        ],
        axis=1,
    ).reshape(tokens, model_width)
    grad_branch_self = round_low(grad_self)
    grad_proj = matmul_left(self_mixed, grad_branch_self)
    grad_self_mixed = round_low(matmul_right(grad_branch_self, proj_w)).reshape(heads_shape)
    grad_sq, grad_sk, grad_sv = attend_back(
        self_query, self_key, self_value, key_mask, self_total, grad_self_mixed
    )
    grad_sq = grad_sq.reshape(tokens, local_width)
    grad_sk = grad_sk.reshape(tokens, local_width)
    grad_sv = grad_sv.reshape(tokens, local_width)
    grad_qkv = jnp.stack(
        [
            matmul_left(normed_low, grad_sq),
            matmul_left(normed_low, grad_sk),
            matmul_left(normed_low, grad_sv),
        ]
    )
    self_grad_term = (
        matmul_right(grad_sq, qkv_w[0])
        + matmul_right(grad_sk, qkv_w[1])
        + matmul_right(grad_sv, qkv_w[2])
    )
    normed_grad_self = inputs_total(self_grad_term)
    stream_back, gain_one, shift_one = norm_back(stream, vecs[0], vecs[1], normed_grad_self)
    stream_grad = grad_self + stream_back
    norm_rows = jnp.stack([gain_one, shift_one, gain_two, shift_two, gain_three, shift_three])
    grad_vectors = jnp.concatenate(
        [
            norm_rows,
            jnp.stack(
                [
                    column_sum(grad_branch_self),
                    column_sum(grad_branch_cross),
                    column_sum(grad_low_query),
                    column_sum(grad_low_text),
                ]
            ),
        ]
    )
    grad_up = jnp.stack([in_query, in_text])
    grad_down = jnp.stack([down_query, down_text])
    owned = (
        lax.psum_scatter(grad_qkv, "dp", scatter_dimension=1, tiled=True),
        lax.psum_scatter(grad_proj, "dp", scatter_dimension=1, tiled=True),
        lax.psum_scatter(grad_cq, "dp", scatter_dimension=0, tiled=True),
        lax.psum_scatter(grad_ckv, "dp", scatter_dimension=1, tiled=True),
        lax.psum_scatter(grad_cproj, "dp", scatter_dimension=1, tiled=True),
        lax.psum_scatter(grad_up, "dp", scatter_dimension=1, tiled=True),
        lax.psum_scatter(grad_down, "dp", scatter_dimension=2, tiled=True),
        lax.psum_scatter(grad_vectors, "dp", scatter_dimension=1, tiled=True),
    )
    grad_heads = jnp.stack(
        [
            column_sum(grad_sq),
            column_sum(grad_sv),
            column_sum(grad_cq_part),
            jnp.sum(grad_cv_part.astype(jnp.float32), axis=(0, 1)).reshape(-1),
        ]
    )
    grad_hidden_bias = jnp.stack([hidden_bias_query, hidden_bias_text])
    grad_heads, grad_hidden_bias, stream_stats = lax.psum(
        (grad_heads, grad_hidden_bias, stream_stats), "dp"
    )
    stream_rms = jnp.sqrt(stream_stats[:4] / (stream_stats[4] * model_width))
    return (
        out_low,
        stream_grad,
        owned[0],
        owned[1],
        owned[2],
        owned[3],
        owned[4],
        owned[5],
        owned[6],
        owned[7],
        grad_heads,
        grad_hidden_bias,
        stream_rms,
    )


def solution(mesh):
    in_specs = (
        P("dp", None),
        P("dp", None, None),
        P("dp", None),
        P("dp", None),
        P("dp", None),
        P(None, "dp", "mp"),
        P("mp", "dp"),
        P("dp", "mp"),
        P(None, "dp", "mp"),
        P("mp", "dp"),
        P(None, "dp", "mp"),
        P(None, "mp", "dp"),
        P(None, "dp"),
        P(None, "mp"),
        P(None, "mp"),
        P("dp", None),
    )
    out_specs = (
        P("dp", None),
        P("dp", None),
        P(None, "dp", "mp"),
        P("mp", "dp"),
        P("dp", "mp"),
        P(None, "dp", "mp"),
        P("mp", "dp"),
        P(None, "dp", "mp"),
        P(None, "mp", "dp"),
        P(None, "dp"),
        P(None, "mp"),
        P(None, "mp"),
        P(),
    )

    def apply(*args):
        fan = args[5].shape[1] // mesh.shape["dp"]
        whole_tiles = fan % 16 == 0 and fan <= 128 and mesh.shape["dp"] % 2 == 0
        run = layer if whole_tiles and mesh.shape["mp"] == 4 else body
        return jax.shard_map(
            run, mesh=mesh, in_specs=in_specs, out_specs=out_specs, check_vma=False
        )(*args)

    return apply
```

```python
import functools
import math
import types

import jax
import jax.numpy as jnp
from jax import lax
from jax.experimental import pallas as pl
from jax.experimental.pallas import tpu as pltpu
from jax.sharding import PartitionSpec as P

HEAD = 64
KEYS = 257
QUERIES = 32
SLOTS = 4
ROW_LEN = 256


EPSILON = 1e-06
MASKED = -1e30
MESH = pl.DeviceIdType.MESH
VMEM_LIMIT = 63 * 2**20
BF16 = jnp.bfloat16
F32 = jnp.float32
PIECES = ("vec", "self", "kv", "cross")
TERMS = ("cross", "kv", "self")
SUMS = ("selfq", "selft", "cross", "gft", "gfq", "out", "gc", "gaq", "gat")
SHARES = ("c", "ft", "fq", "gca", "gsat", "gsaq", "out", "sgq", "sgt")
RINGED = ("in0", "out0", "in1", "out1")
WIDE = 256
CHUNK = 256
CHUNKS_HELD = 4
PADDED_KEYS = 272


def dot(left, right):
    return jnp.dot(left, right, preferred_element_type=F32)


def dot_rows(left, right):
    return lax.dot_general(left, right, (((0,), (0,)), ((), ())), preferred_element_type=F32)


def dot_columns(left, right):
    return lax.dot_general(left, right, (((1,), (1,)), ((), ())), preferred_element_type=F32)


def norm_parts(values):
    centred = values - jnp.mean(values, axis=-1, keepdims=True)
    scale = lax.rsqrt(jnp.mean(centred * centred, axis=-1, keepdims=True) + EPSILON)
    return centred * scale, scale


def norm_grad(normed, scale, gain, grad):
    scaled = grad * gain
    return scale * (
        scaled
        - jnp.mean(scaled, axis=-1, keepdims=True)
        - normed * jnp.mean(scaled * normed, axis=-1, keepdims=True)
    )


def lanes(width):
    return lax.broadcasted_iota(jnp.int32, (1, width), 1)


def of_head(head):
    lane = lanes(WIDE)
    return (lane >= head * HEAD) & (lane < (head + 1) * HEAD)


def spread(values, heads):
    return jnp.concatenate(
        [jnp.where(of_head(head), values, jnp.zeros_like(values)) for head in range(heads)], axis=0
    )


def fold(values, heads, tokens):
    total = jnp.where(of_head(0), values[:tokens], 0.0)
    for head in range(1, heads):
        total = total + jnp.where(of_head(head), values[head * tokens : (head + 1) * tokens], 0.0)
    return total


def softmax(scores):
    exponent = jnp.exp(scores - jnp.max(scores, axis=-1, keepdims=True))
    return exponent * (1.0 / jnp.sum(exponent, axis=-1, keepdims=True))


def widen(packed, wide, count):
    low = lanes(128) < HEAD
    for i in range(count):
        at = (count + i // 2) * 128
        tail = packed[:, at : at + 128]
        if i % 2:
            tail = pltpu.roll(tail, HEAD, 1)
        wide[:, i * WIDE : i * WIDE + 128] = packed[:, i * 128 : (i + 1) * 128]
        wide[:, i * WIDE + 128 : (i + 1) * WIDE] = jnp.where(low, tail, jnp.zeros_like(tail))


def layer_kernel(names, sizes, *refs):
    s = types.SimpleNamespace(**dict(zip(names, refs)))
    z = sizes
    count, lines, rows, length, query, width, heads = (
        z.count,
        z.count // 2,
        z.rows,
        ROW_LEN,
        SLOTS * QUERIES,
        z.width,
        z.heads,
    )
    text = length - query
    place, rank = lax.axis_index("dp"), lax.axis_index("mp")
    line, side = place // 2, lax.rem(place, 2)
    chip, core = rank // 2, lax.rem(rank, 2)
    beside = chip * 2 + 1 - core
    far = (1 - chip) * 2 + core
    diagonal = (1 - chip) * 2 + 1 - core

    def remote(source, target, sems, index, device):
        return pltpu.make_async_remote_copy(
            src_ref=source,
            dst_ref=target,
            send_sem=sems[0].at[index],
            recv_sem=sems[1].at[index],
            device_id=device,
            device_id_type=MESH,
        )

    def other_line(step):
        at, weight = 0, 1
        while weight < lines:
            bit = lax.rem(line // weight, 2)
            at = at + weight * (1 - bit if step // weight % 2 else bit)
            weight *= 2
        return at

    def along(step):
        return (other_line(step) * 2 + side, rank)

    across = (line * 2 + 1 - side, rank)

    def block(ref, index, size):
        return ref.at[pl.ds(pl.multiple_of(index * size, 16), size)]

    fan, feat_fan = z.fan, z.feat_fan
    whole = {
        "vec": s.w_vec,
        "self": s.m_self,
        "kv": s.m_kv,
        "cross": s.m_cross,
        "in0": s.m_in0,
        "in1": s.m_in1,
        "out0": s.m_out0,
        "out1": s.m_out1,
    }
    size = {name: fan for name in PIECES + RINGED} | {"vec": 16, "kv": feat_fan}
    shard = {name: block(whole[name], place, size[name]) for name in PIECES + RINGED}
    own_in = [
        pltpu.make_async_copy(s.ffn_in.at[kind], shard["in%d" % kind], s.own_sem.at[kind])
        for kind in range(2)
    ]

    def pack(name, items):
        for i, item in enumerate(items):
            shard[name][:, i * 128 : (i + 1) * 128] = item[:, :128]
        for i in range(0, len(items), 2):
            at = (len(items) + i // 2) * 128
            shard[name][:, at : at + 128] = jnp.concatenate(
                [items[i][:, 128:], items[i + 1][:, 128:]], axis=1
            )

    def turn(values):
        return values.astype(F32).T.astype(BF16)

    def gather_line(name, step):
        return remote(
            shard[name],
            block(whole[name], place, size[name]),
            (s.gl_send, s.gl_recv),
            (PIECES.index(name), step),
            along(step),
        )

    def gather_side(name, step):
        origin = other_line(step) * 2 + side
        target = block(whole[name], origin, size[name])
        return remote(
            target,
            target,
            (s.gs_send, s.gs_recv),
            (PIECES.index(name), step),
            across,
        )

    def gather_start(name):
        for step in range(1, lines):
            gather_line(name, step).start()
        gather_side(name, 0).start()

    def gather_forward(name):
        for step in range(1, lines):
            gather_line(name, step).wait_recv()
            gather_side(name, step).start()

    def gather_finish(name):
        for step in range(lines):
            gather_side(name, step).wait_recv()

    def gather_sent(name):
        for step in range(1, lines):
            gather_line(name, step).wait_send()
        for step in range(lines):
            gather_side(name, step).wait_send()

    spot = line + side * (count - 1 - 2 * line)

    def ring_index(at):
        at = lax.rem(at + 2 * count, count)
        on = at // lines
        return (at + on * (count - 1 - 2 * at)) * 2 + on

    ring_to = ((ring_index(spot + 1), rank), (ring_index(spot - 1), rank))

    def ring_part(name, way):
        cut = -(-size[name] // 32) * 16
        return (0, cut) if way == 0 else (cut, size[name] - cut)

    def ring_block(name, at, way):
        first, high = ring_part(name, way)
        return whole[name].at[
            pl.ds(pl.multiple_of(ring_index(at) * size[name] + first, 16), high)
        ]

    def ring_gather(name, way, hop):
        target = ring_block(name, spot - hop if way == 0 else spot + hop, way)
        index = (RINGED.index(name), way, hop)
        return remote(target, target, (s.rg_send, s.rg_recv), index, ring_to[way])

    def ring_pass(names, hop):
        for name in names:
            for way in range(2):
                if hop > 0:
                    ring_gather(name, way, hop - 1).wait_recv()
                if hop < count - 1:
                    ring_gather(name, way, hop).start()

    query_pair, text_pair = RINGED[:2], RINGED[2:]

    def ring_passes(*steps):
        for *names, hop in steps:
            ring_pass(names, hop)

    def scatter_passes(*steps):
        for *names, hop in steps:
            scatter_pass(names, hop)

    def ring_gather_sent(name):
        for way in range(2):
            for hop in range(count - 1):
                ring_gather(name, way, hop).wait_send()

    def ring_scatter(name, way, hop):
        first, high = ring_part(name, way)
        return remote(
            ring_block(name, spot - 1 - hop if way == 0 else spot + 1 + hop, way),
            getattr(s, "r_" + name).at[hop, pl.ds(first, high)],
            (s.rs_send, s.rs_recv),
            (RINGED.index(name), way, hop),
            ring_to[way],
        )

    def scatter_pass(names, hop):
        for name in names:
            for way in range(2):
                first, high = ring_part(name, way)
                if hop > 0:
                    ring_scatter(name, way, hop - 1).wait_recv()
                    landed = getattr(s, "r_" + name)[hop - 1, first : first + high, :]
                    mine = ring_block(name, spot - 1 - hop if way == 0 else spot + 1 + hop, way)
                    if hop < count - 1:
                        mine[...] = mine[...] + landed
                    else:
                        total = mine[...].astype(F32) + landed.astype(F32)
                        owned[name][first : first + high, :] = total
                if hop < count - 1:
                    ring_scatter(name, way, hop).start()

    def ring_scatter_sent(name):
        for way in range(2):
            for hop in range(count - 1):
                ring_scatter(name, way, hop).wait_send()

    side_in = {name: getattr(s, "y_" + name) for name in TERMS}
    line_in = {name: getattr(s, "z_" + name) for name in TERMS}
    owned = {
        "self": s.own_self,
        "kv": s.own_kv,
        "cross": s.own_cross,
        "in0": s.own_ffn.at[pl.ds(0, fan)],
        "in1": s.own_ffn.at[pl.ds(fan, fan)],
        "out0": s.own_ffn.at[pl.ds(2 * fan, fan)],
        "out1": s.own_ffn.at[pl.ds(3 * fan, fan)],
    }
    order = [*range(1, lines), 0]

    def scatter_side(name, step):
        other = other_line(step)
        return remote(
            block(whole[name], other * 2 + 1 - side, size[name]),
            side_in[name].at[step],
            (s.ss_send, s.ss_recv),
            (TERMS.index(name), step),
            across,
        )

    def scatter_line(name, step):
        other = other_line(step)
        return remote(
            block(whole[name], other * 2 + side, size[name]),
            line_in[name].at[step - 1],
            (s.sl_send, s.sl_recv),
            (TERMS.index(name), step),
            along(step),
        )

    def scatter_start(name):
        for step in order:
            scatter_side(name, step).start()

    def scatter_forward(name):
        for step in range(1, lines):
            other = other_line(step)
            mine = block(whole[name], other * 2 + side, size[name])
            scatter_side(name, step).wait_recv()
            mine[...] = mine[...] + side_in[name][step]
            scatter_line(name, step).start()

    def scatter_finish(name):
        scatter_side(name, 0).wait_recv()
        total = block(whole[name], place, size[name])[...].astype(F32)
        total = total + side_in[name][0].astype(F32)
        for step in range(1, lines):
            scatter_line(name, step).wait_recv()
            total = total + line_in[name][step - 1].astype(F32)
        owned[name][...] = total
        for step in range(1, lines):
            scatter_line(name, step).wait_send()
        for step in range(lines):
            scatter_side(name, step).wait_send()

    halves = {"selfq": 0, "selft": 1, "cross": 0, "gft": 1, "gfq": 0, "gc": 1, "gaq": 0, "gat": 1}

    def sum_buffers(name):
        landed = {"gaq": "selfq", "gat": "selft", "gc": "cross"}.get(name, name)
        half = s.half_row if name == "out" else s.half.at[halves[name]]
        return getattr(s, "pin_" + landed), half, getattr(s, "fin_" + landed)

    def part(name, index):
        if name in ("selfq", "gaq"):
            return s.part_row.at[index, pl.ds(0, query)]
        if name in ("selft", "gat"):
            return s.part_row.at[index, pl.ds(query, text)]
        return {"out": s.part_row, "gft": s.part_t}.get(name, s.part_q).at[index]

    def sum_copy(name, hop):
        pair_in, half, far_in = sum_buffers(name)
        source, target, device = (
            (part(name, diagonal), pair_in.at[1], beside),
            (part(name, beside), pair_in.at[0], beside),
            (half, far_in, far),
        )[hop]
        index = (SUMS.index(name), hop)
        return remote(source, target, (s.sum_send, s.sum_recv), index, (place, device))

    def sum_forward(name):
        sum_copy(name, 0).wait_recv()
        pair_in, half, _ = sum_buffers(name)
        half[...] = part(name, far)[...] + pair_in[1]
        sum_copy(name, 2).start()

    def sum_finish(name):
        sum_copy(name, 1).wait_recv()
        sum_copy(name, 2).wait_recv()
        pair_in, _, far_in = sum_buffers(name)
        total = part(name, rank)[...].astype(F32) + pair_in[0].astype(F32)
        return total + far_in[...].astype(F32)

    def sum_sent(name, hops=(0, 1, 2)):
        for hop in hops:
            sum_copy(name, hop).wait_send()

    shared = {
        "c": s.c,
        "ft": s.f_t,
        "fq": s.f_q,
        "gsat": s.gsa_t,
        "gsaq": s.f_q,
        "out": s.gy,
    }

    def shared_part(name, index):
        if name in ("gca", "sgq"):
            return s.x.at[index, pl.ds(0, query)]
        if name == "sgt":
            return s.x.at[index, pl.ds(query, text)]
        return shared[name].at[index]

    def share_copy(name, hop):
        index, device = ((rank, far), (rank, beside), (far, beside))[hop]
        return remote(
            shared_part(name, index),
            shared_part(name, index),
            (s.share_send, s.share_recv),
            (SHARES.index(name), hop),
            (place, device),
        )

    def share_start(name):
        share_copy(name, 0).start()
        share_copy(name, 1).start()

    def share_forward(name):
        share_copy(name, 0).wait_recv()
        share_copy(name, 2).start()

    def share_finish(name):
        share_copy(name, 1).wait_recv()
        share_copy(name, 2).wait_recv()

    def share_sent(name):
        for hop in range(3):
            share_copy(name, hop).wait_send()

    def vec(index):
        return s.vecs[index : index + 1, :]

    def column_total(values):
        return jnp.sum(values.astype(F32), axis=0, keepdims=True)

    def row_at(row):
        return pl.ds(pl.multiple_of(row * length, length), length)

    def put_stat(index, values, weight):
        total = jnp.sum(
            jnp.sum(values * values, axis=1, keepdims=True) * weight, axis=0, keepdims=True
        )
        s.small[10:11, :] += jnp.where(lanes(z.model) == index, total, 0.0)

    load_x = pltpu.make_async_copy(s.x_h, s.x, s.load_sem.at[0])
    load_gy = pltpu.make_async_copy(s.gy_h, s.gy, s.load_sem.at[1])
    load_x.start()
    barrier = pltpu.get_barrier_semaphore()
    partners = [along(step) for step in range(1, lines)] + [
        across,
        (place, beside),
        (place, far),
    ]
    for partner in partners:
        pl.semaphore_signal(barrier, inc=1, device_id=partner, device_id_type=MESH)
    for item in own_in:
        item.start()
    own = z.model // count
    shard["vec"][...] = jnp.zeros((16, 128), BF16)
    shard["vec"][: s.vectors.shape[0], :own] = s.vectors[...]
    pack("self", [s.self_qkv[0], s.self_qkv[1], s.self_qkv[2], turn(s.self_out[...])])
    pl.semaphore_wait(barrier, len(partners))
    gather_start("vec")
    gather_start("self")
    pack("kv", [s.cross_kv[0], s.cross_kv[1]])
    pack("cross", [s.cross_q[...], turn(s.cross_out[...])])
    gather_start("kv")
    gather_start("cross")
    for kind in range(2):
        shard["out%d" % kind][...] = s.ffn_out[kind]
        own_in[kind].wait()

    chunk_count = z.features // CHUNK
    tail = z.features - chunk_count * CHUNK

    def load_chunk(index):
        slot = lax.rem(index, CHUNKS_HELD)
        return pltpu.make_async_copy(
            s.feat_h.at[pl.ds(pl.multiple_of(index * CHUNK, CHUNK), CHUNK)],
            s.chunk.at[slot],
            s.chunk_sem.at[slot],
        )

    def load_chunks():
        for index in range(CHUNKS_HELD):
            load_chunk(index).start()

    load_tail = pltpu.make_async_copy(
        s.feat_h.at[pl.ds(chunk_count * CHUNK, tail)], s.tail, s.load_sem.at[2]
    )
    load_chunks()
    load_tail.start()
    load_gy.start()

    s.small[...] = jnp.zeros_like(s.small)
    s.bias[...] = jnp.zeros_like(s.bias)
    for row, at, index in ((0, 0, 0), (0, 2, 1), (1, 0, 2), (2, 1, 3)):
        s.bias[row : row + 1, at * WIDE : at * WIDE + width] = s.head_bias[
            index : index + 1, :
        ].astype(F32)
    s.bias[3:5, : z.hidden] = s.ffn_bias[...].astype(F32)
    slots = lanes(query).astype(F32) * (1.0 / QUERIES)
    s.code[:, :query] = jnp.broadcast_to(jnp.floor(slots), (rows, query))
    s.code[:, query:] = jnp.where(s.valid[...] == 1, s.segment[...], -1).astype(F32)
    same = lax.broadcasted_iota(jnp.int32, (text, text), 0) == lanes(text)

    def as_column(values):
        return jnp.sum(jnp.where(same, values.astype(F32), 0.0), axis=1, keepdims=True)

    for row in range(rows):
        s.text_codes[row] = as_column(s.segment[row : row + 1, :])
    s.weight[...] = as_column((s.valid[pl.ds(rank, 1), :] == 1).astype(jnp.int32))
    gather_forward("vec")
    gather_finish("vec")
    for index in range(count):
        s.vecs[:, index * own : (index + 1) * own] = s.w_vec[
            index * 16 : (index + 1) * 16, :own
        ].astype(F32)
    load_x.wait()

    @pl.loop(0, rows)
    def _(row):
        normed, _ = norm_parts(s.x[row].astype(F32))
        s.a[row_at(row), :] = (normed * vec(0) + vec(1)).astype(BF16)

    ring_pass(query_pair, 0)
    s.x_own[...] = s.x[rank]
    weight_query, weight_text = jnp.ones((query, 1), F32), s.weight[...]
    weight_own = jnp.concatenate([weight_query, weight_text], axis=0)
    s.small[10:11, :] += jnp.where(
        lanes(z.model) == 4, jnp.sum(weight_own, axis=0, keepdims=True), 0.0
    )
    put_stat(0, s.x_own[...].astype(F32), weight_own)

    gather_forward("self")
    gather_finish("self")
    widen(s.m_self, s.w_self, 4)

    def self_mask(row):
        at = lax.broadcasted_iota(jnp.int32, (query, 1), 0).astype(F32) * (1.0 / QUERIES)
        codes = jnp.concatenate([jnp.floor(at), s.text_codes[row]], axis=0)
        return codes == s.code[pl.ds(row, 1), :]

    def send_order(step):
        chip_at = chip + (1 - 2 * chip) * (1 - step // 2)
        core_at = core + (1 - 2 * core) * (1 - lax.rem(step, 2))
        return chip_at * 2 + core_at

    def send_pairs(step, names):
        @pl.when(step == 0)
        def _():
            for name in names:
                sum_copy(name, 0).start()

        @pl.when(step == 2)
        def _():
            for name in names:
                sum_copy(name, 1).start()

    def self_row(step):
        row = send_order(step)
        at = row_at(row)
        qkv = dot(s.a[at, :], s.w_self[:, : 3 * WIDE]) + s.bias[0:1, : 3 * WIDE]
        low = qkv.astype(BF16)
        s.qkv[at, :] = low
        queries = spread(low[:, :WIDE] * jnp.asarray(z.scale, BF16), heads)
        scores = dot_columns(queries, low[:, WIDE : 2 * WIDE])
        mask = self_mask(row)
        scores = jnp.concatenate(
            [
                jnp.where(mask, scores[head * length : (head + 1) * length], MASKED)
                for head in range(heads)
            ],
            axis=0,
        )
        probs = softmax(scores).astype(BF16)
        s.p_self[row] = probs
        mixed = fold(dot(probs, low[:, 2 * WIDE :]), heads, length).astype(BF16)
        s.o[at, :] = mixed
        s.part_row[row] = dot_columns(mixed, s.w_self[:, 3 * WIDE :]).astype(BF16)
        send_pairs(step, ("selfq", "selft"))

    pl.loop(0, rows // 2)(self_row)
    sum_forward("selfq")
    sum_forward("selft")
    ring_pass(text_pair, 0)
    gather_forward("kv")
    pl.loop(rows // 2, rows)(self_row)
    gather_forward("cross")
    gather_finish("kv")
    widen(s.m_kv, s.w_kv, 2)

    def project(values):
        return dot(values, s.w_kv[...]) + s.bias[2:3, : 2 * WIDE]

    def project_chunk(index, first):
        load_chunk(index).wait()
        result = project(s.chunk[lax.rem(index, CHUNKS_HELD)])

        @pl.when(index + CHUNKS_HELD < chunk_count)
        def _():
            load_chunk(index + CHUNKS_HELD).start()

        for tile in range(2 * WIDE // 128):
            at = first + tile % 2 * CHUNK
            s.stage[tile // 2, at : at + CHUNK, :] = result[
                :, tile * 128 : (tile + 1) * 128
            ]
        keys = CHUNK // z.images
        key_at = pl.ds(pl.multiple_of(index * keys, keys), keys)
        for image in range(z.images):
            for tile in range(2 * WIDE // 128):
                s.kv[image, key_at, tile * 128 : (tile + 1) * 128] = s.stage.at[tile // 2][
                    pl.ds(first + tile % 2 * CHUNK + image, keys, stride=z.images), :
                ].astype(BF16)

    def project_pair(pair):
        for inner in range(2):
            project_chunk(pair * 2 + inner, inner * 2 * CHUNK)

    quarter = chunk_count // 8
    pl.loop(0, quarter)(project_pair)

    after = s.x_own[:query, :].astype(F32) + sum_finish("selfq") + vec(6)
    s.after_self[:query, :] = after
    normed, _ = norm_parts(after)
    s.c[rank] = (normed * vec(2) + vec(3)).astype(BF16)
    share_start("c")
    put_stat(1, after, weight_query)
    ring_pass(query_pair, 1)
    pl.loop(quarter, 2 * quarter)(project_pair)
    ring_pass(text_pair, 1)
    after = s.x_own[query:, :].astype(F32) + sum_finish("selft") + vec(6)
    s.after_self[query:, :] = after
    normed, _ = norm_parts(after)
    s.f_t[rank] = (normed * vec(4) + vec(5)).astype(BF16)
    share_start("ft")
    put_stat(1, after, weight_text)
    put_stat(2, after, weight_text)
    ring_passes(("in0", 2))
    pl.loop(2 * quarter, 3 * quarter)(project_pair)
    share_forward("c")
    ring_passes(("out0", 2), ("in1", 2))
    pl.loop(3 * quarter, chunk_count // 2)(project_pair)
    load_tail.wait()
    last = project(s.tail[...])
    first_row = lax.broadcasted_iota(jnp.int32, (tail, 1), 0) == 0
    for image in range(z.images):
        s.kv[image, z.keys - 1 :, :] = jnp.where(
            first_row, jnp.broadcast_to(last[image : image + 1, :], last.shape), 0.0
        ).astype(BF16)
    load_chunks()
    ring_passes(("out1", 2), ("in0", 3))
    gather_finish("cross")
    widen(s.m_cross, s.w_cross, 2)
    share_finish("c")
    queries_total = rows * query
    cross_query = dot(s.c[...].reshape(queries_total, z.model), s.w_cross[:, :WIDE])
    s.qc[...] = (cross_query + s.bias[1:2, :WIDE]).astype(BF16).reshape(s.qc.shape)
    is_key = lanes(PADDED_KEYS) < z.keys

    def all_slots(ref):
        return ref[...].reshape(queries_total, WIDE)

    def slot_of(image):
        slot = jnp.int32(0)
        for other in range(1, z.images):
            slot = jnp.where(s.image_of[other] == image, other, slot)
        return slot

    unroll = 4
    groups = z.images // unroll

    def cross_row(step):
        row = send_order(step)
        for inner in range(SLOTS):
            slot = row * SLOTS + inner
            image = s.image_of[slot]
            queries = spread(s.qc[slot] * jnp.asarray(z.scale, BF16), heads)
            scores = dot_columns(queries, s.kv[image, :, :WIDE])
            probs = softmax(jnp.where(is_key, scores, MASKED)).astype(BF16)
            s.p_cross[slot] = probs
            mixed = fold(dot(probs, s.kv[image, :, WIDE:]), heads, QUERIES)
            s.oc[slot] = mixed.astype(BF16)
        mixed = s.oc[pl.ds(row * SLOTS, SLOTS)].reshape(query, WIDE)
        s.part_q[row] = dot_columns(mixed, s.w_cross[:, WIDE:]).astype(BF16)
        send_pairs(step, ("cross",))

    pl.loop(0, rows // 2)(cross_row)
    ring_passes(("out0", 3), ("in1", 3))
    sum_sent("selfq")
    sum_sent("selft")
    sum_forward("cross")
    share_forward("ft")
    ring_passes(("out1", 3))
    pl.loop(rows // 2, rows)(cross_row)
    ring_passes(("in0", "out0", 4), ("in1", 4))
    ring_passes(("out1", 4), ("in0", "out0", 5), ("in1", "out1", 5))
    after_query = s.after_self[:query, :] + sum_finish("cross") + vec(7)
    s.after_query[...] = after_query
    normed, _ = norm_parts(after_query)
    s.f_q[rank] = (normed * vec(4) + vec(5)).astype(BF16)
    share_start("fq")
    put_stat(2, after_query, weight_query)
    ring_passes(("in0", "out0", 6), ("in1", "out1", 6), ("in0", 7))
    share_forward("fq")
    ring_passes(("out0", 7))
    load_gy.wait()
    gather_sent("self")
    gather_sent("kv")
    sum_sent("cross")
    share_finish("fq")

    f_of = {0: s.f_q, 1: s.f_t}
    w_in = {0: s.m_in0, 1: s.m_in1}
    w_out = {0: s.m_out0, 1: s.m_out1}

    def grad_rows(kind, row):
        return s.gy[row, kind * query : (kind + 1) * query, :]

    def feed_forward(kind, target, send):
        for pair in (1 - chip, chip):
            values = f_of[kind][pl.ds(pair * 2, 2)].reshape(2 * query, z.model)
            grads = jnp.concatenate(
                [grad_rows(kind, pair * 2), grad_rows(kind, pair * 2 + 1)], axis=0
            )
            up = dot(values, w_in[kind][...]) + s.bias[3 + kind : 4 + kind, : z.hidden]
            share = 0.5 * (1.0 + lax.erf(up * (0.5**0.5)))
            hidden = (up * share).astype(BF16)
            slope = share + up * (jnp.exp(-0.5 * up * up) * ((0.5 / math.pi) ** 0.5))
            grad_up = (dot(grads, w_out[kind][...]) * slope).astype(BF16)
            at = pl.ds(pl.multiple_of(pair * 2 * query, 2 * query), 2 * query)
            if kind == 0:
                slots = pl.ds(pair * 2 * SLOTS, 2 * SLOTS)
                s.hid[slots] = hidden.reshape(2 * SLOTS, QUERIES, z.hidden)
                s.gu[slots] = grad_up.reshape(2 * SLOTS, QUERIES, z.hidden)
            else:
                s.m_self[at, :] = hidden
                cut = s.m_kv.shape[1]
                for first in range(0, z.hidden, cut):
                    below = pl.ds(pl.multiple_of(first // cut * queries_total + at.start, 16), at.size)
                    s.m_kv[below, :] = grad_up[:, first : first + cut]
            back = dot_columns(grad_up, w_in[kind][...]).astype(BF16)
            target[pl.ds(pair * 2, 2)] = back.reshape(2, query, z.model)
            send(pair)
            if kind == 0 and pair is not chip:
                sum_forward("gfq")
            s.small[20 + kind : 21 + kind, :] += column_total(grad_up)
            out = dot_columns(hidden, w_out[kind][...]).astype(BF16)
            out = out.reshape(2, query, z.model)
            s.part_row[pl.ds(pair * 2, 2), kind * query : (kind + 1) * query, :] = out

    def weight_terms(kind):
        values = f_of[kind][...].reshape(queries_total, z.model)
        grads = jnp.concatenate([grad_rows(kind, row) for row in range(rows)], axis=0)
        if kind == 0:
            hidden, grad_up = (
                ref[...].reshape(queries_total, z.hidden) for ref in (s.hid, s.gu)
            )
        else:
            hidden = s.m_self[:queries_total, :]
            grad_up = jnp.concatenate(
                [
                    s.m_kv[at : at + queries_total, :]
                    for at in range(0, z.hidden // s.m_kv.shape[1] * queries_total, queries_total)
                ],
                axis=1,
            )
        for name, left, right in (
            ("in%d" % kind, values, grad_up),
            ("out%d" % kind, grads, hidden),
        ):
            ring_gather_sent(name)
            for at in range(0, z.model, WIDE):
                whole[name][at : at + WIDE, :] = dot_rows(left[:, at : at + WIDE], right).astype(
                    BF16
                )

    hops = iter((0, 1))
    feed_forward(0, s.part_q, lambda pair: sum_copy("gfq", next(hops)).start())
    ring_pass(text_pair, 7)
    share_finish("ft")
    hops = iter((0, 1))
    feed_forward(1, s.part_t, lambda pair: sum_copy("gft", next(hops)).start())
    weight_terms(0)
    share_sent("fq")
    sum_forward("gft")
    scatter_pass(query_pair, 0)
    weight_terms(1)
    scatter_pass(text_pair, 0)
    sum_copy("out", 0).start()
    sum_copy("out", 1).start()
    scatter_passes(("in0", 1))

    def own_back(total, after, grads, slot):
        normed, scale = norm_parts(after)
        s.small[4:5, :] += column_total(total * normed)
        s.small[5:6, :] += column_total(total)
        s.small[slot : slot + 1, :] += column_total(grads)
        return grads.astype(F32) + norm_grad(normed, scale, vec(4), total)

    grad_query = own_back(sum_finish("gfq"), s.after_query[...], grad_rows(0, rank), 8)
    s.g_own[:query, :] = grad_query
    grad_query_low = grad_query.astype(BF16)
    s.x[rank, :query, :] = grad_query_low
    s.small[7:8, :] += column_total(grad_query_low)
    share_start("gca")
    sum_forward("out")
    scatter_passes(("out0", 1), ("in1", "out1", 1))
    grad_text = own_back(sum_finish("gft"), s.after_self[query:, :], grad_rows(1, rank), 9)
    s.g_own[query:, :] = grad_text
    grad_text_low = grad_text.astype(BF16)
    s.gsa_t[rank] = grad_text_low
    s.small[6:7, :] += column_total(grad_text_low)
    share_start("gsat")
    scatter_passes(("in0", "out0", 2))
    share_forward("gca")
    scatter_passes(("in1", 2))
    share_finish("gca")

    grad_mixed = dot(s.x[:, :query, :].reshape(queries_total, z.model), s.w_cross[:, WIDE:])
    s.goc[...] = grad_mixed.astype(BF16).reshape(s.goc.shape)

    def stage_put(image, values):
        for tile in range(WIDE // 128):
            s.stage.at[tile][pl.ds(image, PADDED_KEYS, stride=z.images), :] = values[
                :, tile * 128 : (tile + 1) * 128
            ]

    score_places = [(s.hid, 0), (s.hid, z.hidden // 2), (s.gu, 0), (s.gu, z.hidden // 2)][:heads]

    def cross_back(step):
        row = send_order(step)
        for inner in range(SLOTS):
            slot = row * SLOTS + inner
            image = s.image_of[slot]
            grads = spread(s.goc[slot], heads)
            wide = s.p_cross[slot].astype(F32)
            grad_probs = dot_columns(grads, s.kv[image, :, WIDE:])
            delta = jnp.sum(wide * grad_probs, axis=-1, keepdims=True)
            grad_scores = (wide * (grad_probs - delta)).astype(BF16)
            for head, (ref, at) in enumerate(score_places):
                ref[slot, :, at : at + PADDED_KEYS] = grad_scores[
                    head * QUERIES : (head + 1) * QUERIES, :
                ]
            mixed = fold(dot(grad_scores, s.kv[image, :, :WIDE]), heads, QUERIES) * z.scale
            s.gqc[slot] = mixed.astype(BF16)
        mixed = s.gqc[pl.ds(row * SLOTS, SLOTS)].reshape(query, WIDE)
        s.part_q[row] = dot_columns(mixed, s.w_cross[:, :WIDE]).astype(BF16)
        send_pairs(step, ("gc",))

    sum_sent("gfq")
    pl.loop(0, rows // 2)(cross_back)
    sum_sent("gft")
    sum_forward("gc")
    scatter_passes(("out1", 2), ("in0", 3))
    pl.loop(rows // 2, rows)(cross_back)
    scatter_passes(("out0", 3), ("in1", "out1", 3))
    s.small[18:19, :WIDE] += column_total(all_slots(s.gqc))
    low_half = lanes(128) < HEAD
    gather_sent("cross")
    grad_cq = dot_rows(s.c[...].reshape(queries_total, z.model), all_slots(s.gqc))
    grad_co = dot_rows(s.x[:, :query, :].reshape(queries_total, z.model), all_slots(s.oc))
    s.m_cross[:, :128] = grad_cq[:, :128].astype(BF16)
    s.m_cross[:, 128:256] = grad_co[:, :128].astype(BF16)
    s.m_cross[:, 256:] = jnp.where(
        low_half, grad_cq[:, 128:], pltpu.roll(grad_co[:, 128:], HEAD, 1)
    ).astype(BF16)
    scatter_start("cross")

    after_ffn_sum = sum_finish("out")
    after_query_out = s.after_query[...] + after_ffn_sum[:query] + vec(8)
    after_text_out = s.after_self[query:, :] + after_ffn_sum[query:] + vec(9)
    put_stat(3, after_query_out, weight_query)
    put_stat(3, after_text_out, weight_text)
    s.gy[rank, :query, :] = after_query_out.astype(BF16)
    s.gy[rank, query:, :] = after_text_out.astype(BF16)
    share_start("out")

    def key_grad(image):
        slot = slot_of(image)
        queries = spread(s.qc[slot] * jnp.asarray(z.scale, BF16), heads)
        grad_scores = jnp.concatenate(
            [ref[slot, :, at : at + PADDED_KEYS] for ref, at in score_places], axis=0
        )
        return dot_rows(grad_scores, queries)

    def value_grad(image):
        slot = slot_of(image)
        return dot_rows(s.p_cross[slot], spread(s.goc[slot], heads))

    def grads_at(at):
        return jnp.concatenate(
            [s.stage[tile, at, :].astype(BF16) for tile in range(WIDE // 128)], axis=1
        )

    def features_start(grad_of):
        @pl.loop(0, groups)
        def _(group):
            for inner in range(unroll):
                image = group * unroll + inner
                stage_put(image, grad_of(image))

        grads = grads_at(pl.ds(chunk_count * CHUNK, tail))
        s.turned[...] = dot_rows(grads, s.tail[...])
        s.col_sum[...] = column_total(grads)

    def features_pair(pair):
        total, sums = s.turned[...], s.col_sum[...]
        for inner in range(2):
            index = pair * 2 + inner
            load_chunk(index).wait()
            grads = grads_at(pl.ds(pl.multiple_of(index * CHUNK, CHUNK), CHUNK))
            total = total + dot_rows(grads, s.chunk[lax.rem(index, CHUNKS_HELD)])
            sums = sums + column_total(grads)
        s.turned[...] = total
        s.col_sum[...] = sums

        @pl.when(pair * 2 + CHUNKS_HELD < chunk_count)
        def _():
            for inner in range(2):
                load_chunk(pair * 2 + inner + CHUNKS_HELD).start()

    scatter_passes(("in0", 4))
    features_start(key_grad)
    share_forward("gsat")
    scatter_passes(("out0", 4), ("in1", "out1", 4))
    pl.loop(0, chunk_count // 2)(features_pair)
    load_chunks()
    turned = s.turned[...].T
    s.m_kv[:, :128] = turned[:, :128].astype(BF16)
    s.m_kv[:, 256:] = turned[:, 128:].astype(BF16)

    scatter_passes(("in0", 5))
    scatter_forward("cross")
    features_start(value_grad)
    cross_sum = sum_finish("gc")
    normed, scale = norm_parts(s.after_self[:query, :])
    s.small[2:3, :] += column_total(cross_sum * normed)
    s.small[3:4, :] += column_total(cross_sum)
    grad_query = s.g_own[:query, :] + norm_grad(normed, scale, vec(2), cross_sum)
    s.g_own[:query, :] = grad_query
    grad_query_low = grad_query.astype(BF16)
    s.f_q[rank] = grad_query_low
    s.small[6:7, :] += column_total(grad_query_low)
    share_start("gsaq")
    scatter_passes(("out0", "in1", "out1", 5))
    share_forward("out")
    scatter_passes(("in0", 6))
    pl.loop(0, chunk_count // 2)(features_pair)
    s.small[19:20, :WIDE] += s.col_sum[...]
    turned = s.turned[...].T
    s.m_kv[:, 128:256] = turned[:, :128].astype(BF16)
    s.m_kv[:, 256:] = jnp.where(
        low_half, s.m_kv[:, 256:].astype(F32), pltpu.roll(turned[:, 128:], HEAD, 1)
    ).astype(BF16)
    scatter_passes(("out0", 6))
    scatter_start("kv")
    scatter_passes(("in1", 6))
    share_forward("gsaq")
    scatter_passes(("out1", 6))
    share_finish("gsat")
    share_finish("gsaq")

    def self_back(step):
        row = send_order(step)
        at = row_at(row)
        grads = jnp.concatenate([s.f_q[row], s.gsa_t[row]], axis=0)
        low = s.qkv[at, :]
        queries = spread(low[:, :WIDE] * jnp.asarray(z.scale, BF16), heads)
        grad_mixed = dot(grads, s.w_self[:, 3 * WIDE :]).astype(BF16)
        grad_mixed = spread(grad_mixed, heads)
        probs = s.p_self[row]
        wide = probs.astype(F32)
        grad_probs = dot_columns(grad_mixed, low[:, 2 * WIDE :])
        delta = jnp.sum(wide * grad_probs, axis=-1, keepdims=True)
        grad_scores = (wide * (grad_probs - delta)).astype(BF16)
        grad_q = fold(dot(grad_scores, low[:, WIDE : 2 * WIDE]), heads, length) * z.scale
        grad_k = dot_rows(grad_scores, queries)
        grad_v = dot_rows(probs, grad_mixed)
        grad_low = jnp.concatenate([grad_q, grad_k, grad_v], axis=1).astype(BF16)
        s.qkv[at, :] = grad_low
        s.small[16:17, :WIDE] += column_total(grad_low[:, :WIDE])
        s.small[17:18, :WIDE] += column_total(grad_low[:, 2 * WIDE :])
        s.part_row[row] = dot_columns(grad_low, s.w_self[:, : 3 * WIDE]).astype(BF16)
        send_pairs(step, ("gaq", "gat"))

    sum_sent("out")
    sum_sent("gc")
    share_sent("gca")
    pl.loop(0, rows // 2)(self_back)
    sum_forward("gaq")
    sum_forward("gat")
    scatter_passes(("in0", "out0", 7))
    pl.loop(rows // 2, rows)(self_back)

    grads_all = [dot_rows(s.a[...], s.qkv[:, i * WIDE : (i + 1) * WIDE]) for i in range(3)]
    grad_stream = jnp.concatenate(
        [ref[row] for row in range(rows) for ref in (s.f_q, s.gsa_t)], axis=0
    )
    grads_all.append(dot_rows(grad_stream, s.o[...]))
    for i, value in enumerate(grads_all):
        s.m_self[:, i * 128 : (i + 1) * 128] = value[:, :128].astype(BF16)
    for i in range(2):
        s.m_self[:, (4 + i) * 128 : (5 + i) * 128] = jnp.where(
            low_half, grads_all[2 * i][:, 128:], pltpu.roll(grads_all[2 * i + 1][:, 128:], HEAD, 1)
        ).astype(BF16)
    scatter_start("self")
    scatter_passes(("in1", 7))
    scatter_forward("kv")
    scatter_passes(("out1", 7))

    def stream_back(name, at):
        total = sum_finish(name)
        normed, scale = norm_parts(s.x_own[at, :].astype(F32))
        s.small[0:1, :] += column_total(total * normed)
        s.small[1:2, :] += column_total(total)
        grad = s.g_own[at, :] + norm_grad(normed, scale, vec(0), total)
        s.x[rank, at, :] = grad.astype(BF16)

    stream_back("gaq", pl.ds(0, query))
    share_start("sgq")
    stream_back("gat", pl.ds(query, text))
    share_start("sgt")
    scatter_forward("self")

    def small_copy(source, hop, device):
        target = s.small_in.at[hop] if source is s.small else s.small_in.at[hop, pl.ds(0, 16)]
        return remote(source, target, (s.small_send, s.small_recv), (hop,), device)

    shared_rows = s.small.at[pl.ds(0, 16)]
    for hop, device in enumerate(((place, beside), (place, far))):
        item = small_copy(shared_rows, hop, device)
        item.start()
        item.wait()
        s.small[:16, :] += s.small_in[hop, :16, :]
    item = small_copy(s.small, 2, across)
    item.start()
    share_forward("sgq")
    share_forward("sgt")
    item.wait()
    s.small[...] += s.small_in[2]
    items = [small_copy(s.small, 2 + step, along(step)) for step in range(1, lines)]
    for item in items:
        item.start()
    share_finish("out")
    store_out = pltpu.make_async_copy(s.gy, s.out_h, s.load_sem.at[3])
    store_out.start()
    share_finish("sgq")
    share_finish("sgt")
    store_sg = pltpu.make_async_copy(s.x, s.sg_h, s.load_sem.at[4])
    store_sg.start()
    total = s.small[...]
    for step in range(1, lines):
        items[step - 1].wait_recv()
        total = total + s.small_in[2 + step]
    s.small_out[...] = total
    for name in TERMS:
        scatter_finish(name)
    for name in RINGED:
        ring_scatter_sent(name)
    for item in items:
        item.wait_send()
    gather_sent("vec")
    for name in ("gaq", "gat"):
        sum_sent(name)
    for name in SHARES:
        if name not in ("fq", "gca"):
            share_sent(name)
    store_out.wait()
    store_sg.wait()


def finish_kernel(
    out_in,
    grad_in,
    own_self,
    own_kv,
    own_cross,
    own_ffn,
    small,
    out_stream,
    stream_grad,
    grad_qkv,
    grad_out,
    grad_cq,
    grad_ckv,
    grad_co,
    grad_in_w,
    grad_out_w,
    grad_vectors,
    grad_heads,
    grad_hidden,
    rms,
):
    out_stream[...] = out_in[...]
    stream_grad[...] = grad_in[...].astype(F32)

    def piece(packed, count, index):
        at = (count + index // 2) * 128 + index % 2 * HEAD
        return packed[:, index * 128 : (index + 1) * 128], packed[:, at : at + HEAD]

    def put(ref, pieces):
        ref[:, :128] = pieces[0]
        ref[:, 128:] = pieces[1]

    def put_turned(ref, pieces):
        ref[:128, :] = pieces[0].T
        ref[128:, :] = pieces[1].T

    for index in range(3):
        put(grad_qkv.at[index], piece(own_self, 4, index))
    put_turned(grad_out, piece(own_self, 4, 3))
    put(grad_cq, piece(own_cross, 2, 0))
    put_turned(grad_co, piece(own_cross, 2, 1))
    for index in range(2):
        put(grad_ckv.at[index], piece(own_kv, 2, index))
        fan = grad_in_w.shape[1]
        grad_in_w[index] = own_ffn[index * fan : (index + 1) * fan, :]
        grad_out_w[index] = own_ffn[(2 + index) * fan : (3 + index) * fan, :]
    place, own = lax.axis_index("dp"), grad_vectors.shape[1]
    total = jnp.zeros(grad_vectors.shape, F32)
    for index in range(small.shape[1] // own):
        mine = small[: total.shape[0], index * own : (index + 1) * own]
        total = total + jnp.where(place == index, mine, 0.0)
    grad_vectors[...] = total
    grad_heads[...] = small[16:20, : grad_heads.shape[1]]
    grad_hidden[...] = small[20:22, : grad_hidden.shape[1]]
    stats = small[10:11, :128]
    valid = jnp.sum(jnp.where(lanes(128) == 4, stats, 0.0), axis=1, keepdims=True)
    rms[...] = jnp.sqrt(stats / (valid * small.shape[1]))[:, :4]


def layer(
    stream_in,
    features,
    image_index,
    text_segment,
    text_valid,
    self_qkv,
    self_out,
    cross_q,
    cross_kv,
    cross_out,
    ffn_in,
    ffn_out,
    vectors,
    head_bias,
    ffn_bias,
    out_grad,
):
    count = lax.axis_size("dp")
    tokens, model = stream_in.shape
    width, hidden = self_qkv.shape[2], ffn_in.shape[2]
    fan, feat_fan = ffn_in.shape[1], cross_kv.shape[1]
    rows, text = text_segment.shape
    images, keys, feat = features.shape
    query = SLOTS * QUERIES
    z = types.SimpleNamespace(
        count=count,
        rows=rows,
        width=width,
        heads=width // HEAD,
        fan=fan,
        feat_fan=feat_fan,
        model=model,
        hidden=hidden,
        features=images * keys,
        images=images,
        keys=keys,
        scale=HEAD**-0.5,
    )
    lines = count // 2

    operands = {
        "image_of": image_index.reshape(-1),
        "vectors": vectors,
        "self_qkv": self_qkv,
        "self_out": self_out,
        "cross_q": cross_q,
        "cross_kv": cross_kv,
        "cross_out": cross_out,
        "ffn_out": ffn_out.transpose(0, 2, 1),
        "head_bias": head_bias,
        "ffn_bias": ffn_bias,
        "segment": text_segment,
        "valid": text_valid,
        "ffn_in": ffn_in,
        "x_h": stream_in.reshape(rows, ROW_LEN, model),
        "gy_h": out_grad.reshape(rows, ROW_LEN, model),
        "feat_h": features.transpose(1, 0, 2).reshape(keys * images, feat),
    }
    spaces = dict.fromkeys(operands, pltpu.VMEM) | {"image_of": pltpu.SMEM}
    spaces |= dict.fromkeys(("ffn_in", "x_h", "gy_h", "feat_h"), pl.ANY)
    results = {
        "out_h": ((rows, ROW_LEN, model), BF16),
        "sg_h": ((rows, ROW_LEN, model), BF16),
        "own_self": ((fan, 4 * width), F32),
        "own_kv": ((feat_fan, 2 * width), F32),
        "own_cross": ((fan, 2 * width), F32),
        "own_ffn": ((4 * fan, hidden), F32),
        "small_out": ((24, model), F32),
    }
    chunk_rows = (keys + PADDED_KEYS - keys) * images
    buffers = {
        "w_vec": ((count * 16, 128), BF16),
        "vecs": ((16, model), F32),
        "bias": ((8, max(3 * WIDE, hidden)), F32),
        "code": ((rows, ROW_LEN), F32),
        "text_codes": ((rows, text, 1), F32),
        "weight": ((text, 1), F32),
        "m_self": ((model, 4 * width), BF16),
        "m_kv": ((feat, 2 * width), BF16),
        "m_cross": ((model, 2 * width), BF16),
        "w_self": ((model, 4 * WIDE), BF16),
        "w_kv": ((feat, 2 * WIDE), BF16),
        "w_cross": ((model, 2 * WIDE), BF16),
        "x": ((rows, ROW_LEN, model), BF16),
        "x_own": ((ROW_LEN, model), BF16),
        "gy": ((rows, ROW_LEN, model), BF16),
        "a": ((tokens, model), BF16),
        "qkv": ((tokens, 3 * WIDE), BF16),
        "o": ((tokens, WIDE), BF16),
        "p_self": ((rows, z.heads * ROW_LEN, ROW_LEN), BF16),
        "c": ((rows, query, model), BF16),
        "f_q": ((rows, query, model), BF16),
        "f_t": ((rows, query, model), BF16),
        "gsa_t": ((rows, query, model), BF16),
        "qc": ((images, QUERIES, WIDE), BF16),
        "gqc": ((images, QUERIES, WIDE), BF16),
        "goc": ((images, QUERIES, WIDE), BF16),
        "oc": ((images, QUERIES, WIDE), BF16),
        "kv": ((images, PADDED_KEYS, 2 * WIDE), BF16),
        "p_cross": ((images, z.heads * QUERIES, PADDED_KEYS), BF16),
        "stage": ((WIDE // 128, PADDED_KEYS * images, 128), F32),
        "turned": ((WIDE, feat), F32),
        "col_sum": ((1, WIDE), F32),
        "chunk": ((CHUNKS_HELD, CHUNK, feat), BF16),
        "tail": ((images * keys % CHUNK, feat), BF16),
        "hid": ((images, QUERIES, hidden), BF16),
        "gu": ((images, QUERIES, hidden), BF16),
        "part_row": ((rows, ROW_LEN, model), BF16),
        "part_q": ((rows, query, model), BF16),
        "part_t": ((rows, query, model), BF16),
        "after_self": ((ROW_LEN, model), F32),
        "after_query": ((query, model), F32),
        "g_own": ((ROW_LEN, model), F32),
        "small": ((24, model), F32),
        "small_in": ((2 + lines, 24, model), F32),
    }
    for name in ("in0", "in1", "out0", "out1"):
        buffers["m_" + name] = ((model, hidden), BF16)
        buffers["r_" + name] = ((count - 1, fan, hidden), BF16)
    for name in ("selfq", "selft", "out", "cross", "gft", "gfq"):
        block = (ROW_LEN if name == "out" else query, model)
        buffers["pin_" + name] = ((2, *block), BF16)
        buffers["fin_" + name] = (block, BF16)
    buffers["half_row"] = ((ROW_LEN, model), BF16)
    buffers["half"] = ((2, query, model), BF16)
    for name in TERMS:
        high = feat_fan if name == "kv" else fan
        across = (4 if name == "self" else 2) * width
        buffers["y_" + name] = ((lines, high, across), BF16)
        buffers["z_" + name] = ((lines - 1, high, across), BF16)
    semaphores = {
        "own_sem": (2,),
        "load_sem": (5,),
        "chunk_sem": (CHUNKS_HELD,),
    }
    for name in ("gl_send", "gl_recv", "gs_send", "gs_recv"):
        semaphores[name] = (len(PIECES), lines)
    for name in ("ss_send", "ss_recv", "sl_send", "sl_recv"):
        semaphores[name] = (len(TERMS), lines)
    for kind in ("send", "recv"):
        semaphores["rg_" + kind] = (len(RINGED), 2, count - 1)
        semaphores["rs_" + kind] = (len(RINGED), 2, count - 1)
        semaphores["sum_" + kind] = (len(SUMS), 3)
        semaphores["share_" + kind] = (len(SHARES), 3)
        semaphores["small_" + kind] = (2 + lines,)
    names = (*operands, *results, *buffers, *semaphores)
    held = ("out_h", "sg_h")
    done = pl.pallas_call(
        functools.partial(layer_kernel, names, z),
        out_shape=[jax.ShapeDtypeStruct(*item) for item in results.values()],
        in_specs=[pl.BlockSpec(memory_space=spaces[name]) for name in operands],
        out_specs=[
            pl.BlockSpec(memory_space=pl.ANY if name in held else pltpu.VMEM) for name in results
        ],
        scratch_shapes=[pltpu.VMEM(*item) for item in buffers.values()]
        + [pltpu.SemaphoreType.DMA(item) for item in semaphores.values()],
        compiler_params=pltpu.CompilerParams(
            collective_id=0, has_side_effects=True, vmem_limit_bytes=VMEM_LIMIT
        ),
    )(*operands.values())
    local = [
        ((rows, ROW_LEN, model), BF16),
        ((rows, ROW_LEN, model), F32),
        (self_qkv.shape, F32),
        (self_out.shape, F32),
        (cross_q.shape, F32),
        (cross_kv.shape, F32),
        (cross_out.shape, F32),
        (ffn_in.shape, F32),
        (ffn_in.shape, F32),
        (vectors.shape, F32),
        (head_bias.shape, F32),
        (ffn_bias.shape, F32),
        ((1, 4), F32),
    ]
    inside = pl.BlockSpec(memory_space=pltpu.VMEM)
    out_all, grad_all, *others, grad_down, grad_vectors, grad_heads, grad_hidden, rms = pl.pallas_call(
        finish_kernel,
        out_shape=[jax.ShapeDtypeStruct(*item) for item in local],
        in_specs=[inside] * len(done),
        out_specs=[inside] * len(local),
        compiler_params=pltpu.CompilerParams(vmem_limit_bytes=VMEM_LIMIT),
    )(*done)
    return (
        out_all.reshape(tokens, model),
        grad_all.reshape(tokens, model),
        *others,
        grad_down.transpose(0, 2, 1),
        grad_vectors,
        grad_heads,
        grad_hidden,
        rms.reshape(4),
    )


def layer_norm(values, gain_row, shift_row):
    row_mean = jnp.mean(values, axis=-1, keepdims=True)
    centred = values - row_mean
    row_var = jnp.mean(centred * centred, axis=-1, keepdims=True)
    return centred * lax.rsqrt(row_var + EPSILON) * gain_row + shift_row


def norm_back(values, gain_row, shift_row, grad_normed):
    pull_back = jax.vjp(layer_norm, values, gain_row, shift_row)[1]
    return pull_back(grad_normed)


def gelu_exact(values):
    return jax.nn.gelu(values, approximate=False)


def round_low(values):
    return values.astype(jnp.bfloat16)


def matmul(left_side, right_side):
    return jnp.dot(left_side, right_side, preferred_element_type=jnp.float32)


def matmul_left(left_side, right_side):
    return lax.dot_general(
        left_side, right_side, (((0,), (0,)), ((), ())), preferred_element_type=jnp.float32
    )


def matmul_right(left_side, right_side):
    return lax.dot_general(
        left_side, right_side, (((1,), (1,)), ((), ())), preferred_element_type=jnp.float32
    )


def column_sum(values):
    return jnp.sum(values.astype(jnp.float32), axis=0)


def attn_scores(queries, keys_in, key_mask):
    score_scale = queries.shape[-1] ** (-0.5)
    scores = (
        jnp.einsum("bqhe,bkhe->bhqk", queries, keys_in, preferred_element_type=jnp.float32)
        * score_scale
    )
    if key_mask is None:
        return scores
    return jnp.where(key_mask[:, None], scores, MASKED)


def attend(queries, keys_in, values_in, key_mask):
    scores = attn_scores(queries, keys_in, key_mask)
    row_max = jnp.max(scores, axis=-1, keepdims=True)
    exponent = jnp.exp(scores - row_max)
    row_total = jnp.sum(exponent, axis=-1, keepdims=True)
    attn_probs = round_low(exponent / row_total)
    mixed_out = jnp.einsum(
        "bhqk,bkhe->bqhe", attn_probs, values_in, preferred_element_type=jnp.float32
    )
    return (round_low(mixed_out), row_max + jnp.log(row_total))


def attend_back(queries, keys_in, values_in, key_mask, log_total, grad_mixed):
    score_scale = queries.shape[-1] ** (-0.5)
    attn_probs = jnp.exp(attn_scores(queries, keys_in, key_mask) - log_total)
    grad_values = jnp.einsum(
        "bhqk,bqhe->bkhe", round_low(attn_probs), grad_mixed, preferred_element_type=jnp.float32
    )
    grad_probs = jnp.einsum(
        "bqhe,bkhe->bhqk", grad_mixed, values_in, preferred_element_type=jnp.float32
    )
    row_delta = jnp.sum(attn_probs * grad_probs, axis=-1, keepdims=True)
    grad_scores = round_low(attn_probs * (grad_probs - row_delta))
    grad_queries = (
        jnp.einsum("bhqk,bkhe->bqhe", grad_scores, keys_in, preferred_element_type=jnp.float32)
        * score_scale
    )
    grad_keys = (
        jnp.einsum("bhqk,bqhe->bkhe", grad_scores, queries, preferred_element_type=jnp.float32)
        * score_scale
    )
    return (round_low(grad_queries), round_low(grad_keys), round_low(grad_values))


def heads_total(partial_terms):
    return lax.psum(partial_terms, "mp")


def inputs_total(partial_terms):
    return lax.psum(partial_terms, "mp")


def ffn_forward(normed_low, weight_up, bias_up, weight_down):
    up_value = matmul(normed_low, weight_up) + bias_up
    hidden = round_low(gelu_exact(up_value))
    return (up_value, hidden, matmul(hidden, weight_down))


def ffn_back(normed_low, up_value, hidden, weight_up, weight_down, grad_low):
    grad_down = matmul_left(hidden, grad_low)
    grad_hidden = matmul_right(grad_low, weight_down)
    grad_up = round_low(jax.vjp(gelu_exact, up_value)[1](grad_hidden)[0])
    grad_in = matmul_left(normed_low, grad_up)
    return (grad_in, grad_down, column_sum(grad_up), matmul_right(grad_up, weight_up))


def body(
    stream_in,
    features,
    image_index,
    text_segment,
    text_valid,
    self_qkv,
    self_out,
    cross_q,
    cross_kv,
    cross_out,
    ffn_in,
    ffn_out,
    vectors,
    head_bias,
    ffn_bias,
    out_grad,
):
    gathered = (
        lax.all_gather(self_qkv, "dp", axis=1, tiled=True),
        lax.all_gather(self_out, "dp", axis=1, tiled=True),
        lax.all_gather(cross_q, "dp", axis=0, tiled=True),
        lax.all_gather(cross_kv, "dp", axis=1, tiled=True),
        lax.all_gather(cross_out, "dp", axis=1, tiled=True),
        lax.all_gather(ffn_in, "dp", axis=1, tiled=True),
        lax.all_gather(ffn_out, "dp", axis=2, tiled=True),
        lax.all_gather(vectors, "dp", axis=1, tiled=True),
    )
    qkv_w, proj_w, cq_w, ckv_w, cproj_w, up_w, down_w, vector_low = gathered
    vecs = vector_low.astype(jnp.float32)
    bias_heads = head_bias.astype(jnp.float32)
    bias_hidden = ffn_bias.astype(jnp.float32)
    stream = stream_in.astype(jnp.float32)
    tokens, model_width = stream.shape
    row_count = tokens // ROW_LEN
    query_count = SLOTS * QUERIES
    text_len = ROW_LEN - query_count
    local_width = qkv_w.shape[2]
    local_heads = local_width // HEAD
    query_segment = jnp.arange(query_count, dtype=jnp.int32) // QUERIES
    segment = jnp.concatenate(
        [jnp.broadcast_to(query_segment, (row_count, query_count)), text_segment], axis=1
    )
    valid = (
        jnp.concatenate([jnp.ones((row_count, query_count), jnp.int32), text_valid], axis=1) == 1
    )
    key_mask = (segment[:, :, None] == segment[:, None, :]) & valid[:, None, :]
    heads_shape = (row_count, ROW_LEN, local_heads, HEAD)
    normed_low = round_low(layer_norm(stream, vecs[0], vecs[1]))
    self_query = round_low(matmul(normed_low, qkv_w[0]) + bias_heads[0]).reshape(heads_shape)
    self_key = round_low(matmul(normed_low, qkv_w[1])).reshape(heads_shape)
    self_value = round_low(matmul(normed_low, qkv_w[2]) + bias_heads[1]).reshape(heads_shape)
    self_mixed, self_total = attend(self_query, self_key, self_value, key_mask)
    self_mixed = self_mixed.reshape(tokens, local_width)
    self_term = matmul(self_mixed, proj_w).reshape(row_count, ROW_LEN, model_width)
    after_self = stream + heads_total(self_term.reshape(tokens, model_width)) + vecs[6]
    self_rows = after_self.reshape(row_count, ROW_LEN, model_width)
    query_part = self_rows[:, :query_count].reshape(-1, model_width)
    cross_normed = round_low(layer_norm(query_part, vecs[2], vecs[3]))
    slot_count = row_count * SLOTS
    cross_query = round_low(matmul(cross_normed, cq_w) + bias_heads[2]).reshape(
        slot_count, QUERIES, local_heads, HEAD
    )
    image_order = image_index.reshape(-1)
    pick_table = (image_order[:, None] == jnp.arange(image_order.shape[0])[None, :]).astype(
        jnp.bfloat16
    )
    keys_all = round_low(
        jnp.einsum("nkf,fc->nkc", features, ckv_w[0], preferred_element_type=jnp.float32)
    )
    values_all = round_low(
        jnp.einsum("nkf,fc->nkc", features, ckv_w[1], preferred_element_type=jnp.float32)
        + bias_heads[3]
    )
    cross_keys = round_low(
        jnp.einsum("ij,jkc->ikc", pick_table, keys_all, preferred_element_type=jnp.float32)
    )
    cross_values = round_low(
        jnp.einsum("ij,jkc->ikc", pick_table, values_all, preferred_element_type=jnp.float32)
    )
    cross_keys = cross_keys.reshape(slot_count, KEYS, local_heads, HEAD)
    cross_values = cross_values.reshape(slot_count, KEYS, local_heads, HEAD)
    cross_mixed, cross_total = attend(cross_query, cross_keys, cross_values, None)
    cross_mixed = cross_mixed.reshape(-1, local_width)
    cross_term = matmul(cross_mixed, cproj_w).reshape(row_count, query_count, model_width)
    after_query = query_part + heads_total(cross_term.reshape(-1, model_width)) + vecs[7]
    after_cross = jnp.concatenate(
        [after_query.reshape(row_count, query_count, model_width), self_rows[:, query_count:]],
        axis=1,
    ).reshape(tokens, model_width)
    ffn_normed = round_low(layer_norm(after_cross, vecs[4], vecs[5])).reshape(
        row_count, ROW_LEN, model_width
    )
    ffn_query = ffn_normed[:, :query_count].reshape(-1, model_width)
    ffn_text = ffn_normed[:, query_count:].reshape(-1, model_width)
    up_query, hidden_query, part_query = ffn_forward(ffn_query, up_w[0], bias_hidden[0], down_w[0])
    up_text, hidden_text, part_text = ffn_forward(ffn_text, up_w[1], bias_hidden[1], down_w[1])
    ffn_terms = jnp.concatenate(
        [
            part_query.reshape(row_count, query_count, model_width),
            part_text.reshape(row_count, text_len, model_width),
        ],
        axis=1,
    )
    query_flag = jnp.arange(ROW_LEN) < query_count
    bias_rows = jnp.where(query_flag[:, None], vecs[8], vecs[9])
    ffn_sum = heads_total(ffn_terms.reshape(tokens, model_width)).reshape(
        row_count, ROW_LEN, model_width
    )
    after_ffn = after_cross + (ffn_sum + bias_rows).reshape(tokens, model_width)
    token_weight = valid.reshape(-1).astype(jnp.float32)
    stream_stats = jnp.stack(
        [
            jnp.sum(token_weight * jnp.sum(section * section, axis=1))
            for section in (stream, after_self, after_cross, after_ffn)
        ]
        + [jnp.sum(token_weight)]
    )
    out_low = round_low(after_ffn)
    regathered = (
        lax.all_gather(self_qkv, "dp", axis=1, tiled=True),
        lax.all_gather(self_out, "dp", axis=1, tiled=True),
        lax.all_gather(cross_q, "dp", axis=0, tiled=True),
        lax.all_gather(cross_kv, "dp", axis=1, tiled=True),
        lax.all_gather(cross_out, "dp", axis=1, tiled=True),
        lax.all_gather(ffn_in, "dp", axis=1, tiled=True),
        lax.all_gather(ffn_out, "dp", axis=2, tiled=True),
        lax.all_gather(vectors, "dp", axis=1, tiled=True),
    )
    qkv_w, proj_w, cq_w, ckv_w, cproj_w, up_w, down_w, vector_low = regathered
    vecs = vector_low.astype(jnp.float32)
    grad_out = out_grad.astype(jnp.float32)
    grad_out_rows = grad_out.reshape(row_count, ROW_LEN, model_width)
    grad_low = round_low(grad_out_rows)
    grad_low_query = grad_low[:, :query_count].reshape(-1, model_width)
    grad_low_text = grad_low[:, query_count:].reshape(-1, model_width)
    in_query, down_query, hidden_bias_query, normed_grad_query = ffn_back(
        ffn_query, up_query, hidden_query, up_w[0], down_w[0], grad_low_query
    )
    in_text, down_text, hidden_bias_text, normed_grad_text = ffn_back(
        ffn_text, up_text, hidden_text, up_w[1], down_w[1], grad_low_text
    )
    normed_grad_q = normed_grad_query.reshape(row_count, query_count, model_width)
    normed_grad_t = normed_grad_text.reshape(row_count, text_len, model_width)
    normed_grad = jnp.concatenate([normed_grad_q, normed_grad_t], axis=1)
    normed_grad = inputs_total(normed_grad.reshape(tokens, model_width))
    cross_back, gain_three, shift_three = norm_back(after_cross, vecs[4], vecs[5], normed_grad)
    grad_cross = grad_out + cross_back
    grad_cross_rows = grad_cross.reshape(row_count, ROW_LEN, model_width)
    grad_branch_cross = round_low(grad_cross_rows[:, :query_count].reshape(-1, model_width))
    grad_cproj = matmul_left(cross_mixed, grad_branch_cross)
    grad_cross_mixed = round_low(matmul_right(grad_branch_cross, cproj_w)).reshape(
        cross_query.shape
    )
    grad_cq_part, grad_ck_part, grad_cv_part = attend_back(
        cross_query, cross_keys, cross_values, None, cross_total, grad_cross_mixed
    )
    grad_cq_part = grad_cq_part.reshape(-1, local_width)
    grad_ck_all = round_low(
        jnp.einsum(
            "ij,ikc->jkc",
            pick_table,
            grad_ck_part.reshape(-1, KEYS, local_width),
            preferred_element_type=jnp.float32,
        )
    )
    grad_cv_all = round_low(
        jnp.einsum(
            "ij,ikc->jkc",
            pick_table,
            grad_cv_part.reshape(-1, KEYS, local_width),
            preferred_element_type=jnp.float32,
        )
    )
    grad_ckv = jnp.stack(
        [
            jnp.einsum("nkf,nkc->fc", features, grad_ck_all, preferred_element_type=jnp.float32),
            jnp.einsum("nkf,nkc->fc", features, grad_cv_all, preferred_element_type=jnp.float32),
        ]
    )
    grad_cq = matmul_left(cross_normed, grad_cq_part)
    cross_grad_term = matmul_right(grad_cq_part, cq_w)
    cross_normed_grad = inputs_total(cross_grad_term)
    query_back, gain_two, shift_two = norm_back(query_part, vecs[2], vecs[3], cross_normed_grad)
    grad_self = jnp.concatenate(
        [
            grad_cross_rows[:, :query_count]
            + query_back.reshape(row_count, query_count, model_width),
            grad_cross_rows[:, query_count:],
        ],
        axis=1,
    ).reshape(tokens, model_width)
    grad_branch_self = round_low(grad_self)
    grad_proj = matmul_left(self_mixed, grad_branch_self)
    grad_self_mixed = round_low(matmul_right(grad_branch_self, proj_w)).reshape(heads_shape)
    grad_sq, grad_sk, grad_sv = attend_back(
        self_query, self_key, self_value, key_mask, self_total, grad_self_mixed
    )
    grad_sq = grad_sq.reshape(tokens, local_width)
    grad_sk = grad_sk.reshape(tokens, local_width)
    grad_sv = grad_sv.reshape(tokens, local_width)
    grad_qkv = jnp.stack(
        [
            matmul_left(normed_low, grad_sq),
            matmul_left(normed_low, grad_sk),
            matmul_left(normed_low, grad_sv),
        ]
    )
    self_grad_term = (
        matmul_right(grad_sq, qkv_w[0])
        + matmul_right(grad_sk, qkv_w[1])
        + matmul_right(grad_sv, qkv_w[2])
    )
    normed_grad_self = inputs_total(self_grad_term)
    stream_back, gain_one, shift_one = norm_back(stream, vecs[0], vecs[1], normed_grad_self)
    stream_grad = grad_self + stream_back
    norm_rows = jnp.stack([gain_one, shift_one, gain_two, shift_two, gain_three, shift_three])
    grad_vectors = jnp.concatenate(
        [
            norm_rows,
            jnp.stack(
                [
                    column_sum(grad_branch_self),
                    column_sum(grad_branch_cross),
                    column_sum(grad_low_query),
                    column_sum(grad_low_text),
                ]
            ),
        ]
    )
    grad_up = jnp.stack([in_query, in_text])
    grad_down = jnp.stack([down_query, down_text])
    owned = (
        lax.psum_scatter(grad_qkv, "dp", scatter_dimension=1, tiled=True),
        lax.psum_scatter(grad_proj, "dp", scatter_dimension=1, tiled=True),
        lax.psum_scatter(grad_cq, "dp", scatter_dimension=0, tiled=True),
        lax.psum_scatter(grad_ckv, "dp", scatter_dimension=1, tiled=True),
        lax.psum_scatter(grad_cproj, "dp", scatter_dimension=1, tiled=True),
        lax.psum_scatter(grad_up, "dp", scatter_dimension=1, tiled=True),
        lax.psum_scatter(grad_down, "dp", scatter_dimension=2, tiled=True),
        lax.psum_scatter(grad_vectors, "dp", scatter_dimension=1, tiled=True),
    )
    grad_heads = jnp.stack(
        [
            column_sum(grad_sq),
            column_sum(grad_sv),
            column_sum(grad_cq_part),
            jnp.sum(grad_cv_part.astype(jnp.float32), axis=(0, 1)).reshape(-1),
        ]
    )
    grad_hidden_bias = jnp.stack([hidden_bias_query, hidden_bias_text])
    grad_heads, grad_hidden_bias, stream_stats = lax.psum(
        (grad_heads, grad_hidden_bias, stream_stats), "dp"
    )
    stream_rms = jnp.sqrt(stream_stats[:4] / (stream_stats[4] * model_width))
    return (
        out_low,
        stream_grad,
        owned[0],
        owned[1],
        owned[2],
        owned[3],
        owned[4],
        owned[5],
        owned[6],
        owned[7],
        grad_heads,
        grad_hidden_bias,
        stream_rms,
    )


def solution(mesh):
    in_specs = (
        P("dp", None),
        P("dp", None, None),
        P("dp", None),
        P("dp", None),
        P("dp", None),
        P(None, "dp", "mp"),
        P("mp", "dp"),
        P("dp", "mp"),
        P(None, "dp", "mp"),
        P("mp", "dp"),
        P(None, "dp", "mp"),
        P(None, "mp", "dp"),
        P(None, "dp"),
        P(None, "mp"),
        P(None, "mp"),
        P("dp", None),
    )
    out_specs = (
        P("dp", None),
        P("dp", None),
        P(None, "dp", "mp"),
        P("mp", "dp"),
        P("dp", "mp"),
        P(None, "dp", "mp"),
        P("mp", "dp"),
        P(None, "dp", "mp"),
        P(None, "mp", "dp"),
        P(None, "dp"),
        P(None, "mp"),
        P(None, "mp"),
        P(),
    )

    def apply(*args):
        fan = args[5].shape[1] // mesh.shape["dp"]
        whole_tiles = fan % 16 == 0 and fan <= 128 and mesh.shape["dp"] % 2 == 0
        run = layer if whole_tiles and mesh.shape["mp"] == 4 else body
        return jax.shard_map(
            run, mesh=mesh, in_specs=in_specs, out_specs=out_specs, check_vma=False
        )(*args)

    return apply
```

```python
import functools
import math
import types

import jax
import jax.numpy as jnp
from jax import lax
from jax.experimental import pallas as pl
from jax.experimental.pallas import tpu as pltpu
from jax.sharding import PartitionSpec as P

HEAD = 64
KEYS = 257
QUERIES = 32
SLOTS = 4
ROW_LEN = 256


N_C = "c"
N_CROSS = "cross"
N_DP = "dp"
N_FIN = "fin_"
N_FQ = "fq"
N_FT = "ft"
N_GAQ = "gaq"
N_GAT = "gat"
N_GC = "gc"
N_GCA = "gca"
N_GFQ = "gfq"
N_GFT = "gft"
N_GSAQ = "gsaq"
N_GSAT = "gsat"
N_IN0 = "in0"
N_IN1 = "in1"
N_KV = "kv"
N_MP = "mp"
N_OUT = "out"
N_OUT0 = "out0"
N_OUT1 = "out1"
N_PIN = "pin_"
N_R = "r_"
N_SELF = "self"
N_SELFQ = "selfq"
N_SELFT = "selft"
N_SGQ = "sgq"
N_SGT = "sgt"
N_VEC = "vec"
N_Y = "y_"
N_Z = "z_"
EPSILON = 1e-06
MASKED = -1e30
MESH = pl.DeviceIdType.MESH
VMEM_LIMIT = 63 * 2**20
BF16 = jnp.bfloat16
F32 = jnp.float32
PIECES = (N_VEC, N_SELF, N_KV, N_CROSS)
TERMS = (N_CROSS, N_KV, N_SELF)
SUMS = (N_SELFQ, N_SELFT, N_CROSS, N_GFT, N_GFQ, N_OUT, N_GC, N_GAQ, N_GAT)
SHARES = (N_C, N_FT, N_FQ, N_GCA, N_GSAT, N_GSAQ, N_OUT, N_SGQ, N_SGT)
RINGED = (N_IN0, N_OUT0, N_IN1, N_OUT1)
WIDE = 256
CHUNK = 256
CHUNKS_HELD = 4
PADDED_KEYS = 272


def dot(left, right):
    return jnp.dot(left, right, preferred_element_type=F32)


def dot_rows(left, right):
    return lax.dot_general(left, right, (((0,), (0,)), ((), ())), preferred_element_type=F32)


def dot_columns(left, right):
    return lax.dot_general(left, right, (((1,), (1,)), ((), ())), preferred_element_type=F32)


def norm_parts(values):
    centred = values - jnp.mean(values, axis=-1, keepdims=True)
    scale = lax.rsqrt(jnp.mean(centred * centred, axis=-1, keepdims=True) + EPSILON)
    return centred * scale, scale


def norm_grad(normed, scale, gain, grad):
    scaled = grad * gain
    return scale * (
        scaled
        - jnp.mean(scaled, axis=-1, keepdims=True)
        - normed * jnp.mean(scaled * normed, axis=-1, keepdims=True)
    )


def lanes(width):
    return lax.broadcasted_iota(jnp.int32, (1, width), 1)


def of_head(head):
    lane = lanes(WIDE)
    return (lane >= head * HEAD) & (lane < (head + 1) * HEAD)


def spread(values, heads):
    return jnp.concatenate(
        [jnp.where(of_head(head), values, jnp.zeros_like(values)) for head in range(heads)], axis=0
    )


def fold(values, heads, tokens):
    total = jnp.where(of_head(0), values[:tokens], 0.0)
    for head in range(1, heads):
        total = total + jnp.where(of_head(head), values[head * tokens : (head + 1) * tokens], 0.0)
    return total


def softmax(scores):
    exponent = jnp.exp(scores - jnp.max(scores, axis=-1, keepdims=True))
    return exponent * (1.0 / jnp.sum(exponent, axis=-1, keepdims=True))


def widen(packed, wide, count):
    low = lanes(128) < HEAD
    for i in range(count):
        at = (count + i // 2) * 128
        tail = packed[:, at : at + 128]
        if i % 2:
            tail = pltpu.roll(tail, HEAD, 1)
        wide[:, i * WIDE : i * WIDE + 128] = packed[:, i * 128 : (i + 1) * 128]
        wide[:, i * WIDE + 128 : (i + 1) * WIDE] = jnp.where(low, tail, jnp.zeros_like(tail))


def layer_kernel(names, sizes, *refs):
    s = types.SimpleNamespace(**dict(zip(names, refs)))
    z = sizes
    count, lines, rows, length, query, width, heads = (
        z.count,
        z.count // 2,
        z.rows,
        ROW_LEN,
        SLOTS * QUERIES,
        z.width,
        z.heads,
    )
    text = length - query
    place, rank = lax.axis_index(N_DP), lax.axis_index(N_MP)
    line, side = place // 2, lax.rem(place, 2)
    chip, core = rank // 2, lax.rem(rank, 2)
    beside = chip * 2 + 1 - core
    far = (1 - chip) * 2 + core
    diagonal = (1 - chip) * 2 + 1 - core

    def remote(source, target, sems, index, device):
        return pltpu.make_async_remote_copy(
            src_ref=source,
            dst_ref=target,
            send_sem=sems[0].at[index],
            recv_sem=sems[1].at[index],
            device_id=device,
            device_id_type=MESH,
        )

    def other_line(step):
        at, weight = 0, 1
        while weight < lines:
            bit = lax.rem(line // weight, 2)
            at = at + weight * (1 - bit if step // weight % 2 else bit)
            weight *= 2
        return at

    def along(step):
        return (other_line(step) * 2 + side, rank)

    across = (line * 2 + 1 - side, rank)

    def block(ref, index, size):
        return ref.at[pl.ds(pl.multiple_of(index * size, 16), size)]

    fan, feat_fan = z.fan, z.feat_fan
    whole = dict(
        vec=s.w_vec,
        self=s.m_self,
        kv=s.m_kv,
        cross=s.m_cross,
        in0=s.m_in0,
        in1=s.m_in1,
        out0=s.m_out0,
        out1=s.m_out1,
    )
    size = {name: fan for name in PIECES + RINGED} | {N_VEC: 16, N_KV: feat_fan}
    shard = {name: block(whole[name], place, size[name]) for name in PIECES + RINGED}
    own_in = [
        pltpu.make_async_copy(s.ffn_in.at[kind], shard["in%d" % kind], s.own_sem.at[kind])
        for kind in range(2)
    ]

    def pack(name, items):
        for i, item in enumerate(items):
            shard[name][:, i * 128 : (i + 1) * 128] = item[:, :128]
        for i in range(0, len(items), 2):
            at = (len(items) + i // 2) * 128
            shard[name][:, at : at + 128] = jnp.concatenate(
                [items[i][:, 128:], items[i + 1][:, 128:]], axis=1
            )

    def turn(values):
        return values.astype(F32).T.astype(BF16)

    def gather_line(name, step):
        return remote(
            shard[name],
            block(whole[name], place, size[name]),
            (s.gl_send, s.gl_recv),
            (PIECES.index(name), step),
            along(step),
        )

    def gather_side(name, step):
        origin = other_line(step) * 2 + side
        target = block(whole[name], origin, size[name])
        return remote(
            target,
            target,
            (s.gs_send, s.gs_recv),
            (PIECES.index(name), step),
            across,
        )

    def gather_start(name):
        for step in range(1, lines):
            gather_line(name, step).start()
        gather_side(name, 0).start()

    def gather_forward(name):
        for step in range(1, lines):
            gather_line(name, step).wait_recv()
            gather_side(name, step).start()

    def gather_finish(name):
        for step in range(lines):
            gather_side(name, step).wait_recv()

    def gather_sent(name):
        for step in range(1, lines):
            gather_line(name, step).wait_send()
        for step in range(lines):
            gather_side(name, step).wait_send()

    spot = line + side * (count - 1 - 2 * line)

    def ring_index(at):
        at = lax.rem(at + 2 * count, count)
        on = at // lines
        return (at + on * (count - 1 - 2 * at)) * 2 + on

    ring_to = ((ring_index(spot + 1), rank), (ring_index(spot - 1), rank))

    def ring_part(name, way):
        cut = -(-size[name] // 32) * 16
        return (0, cut) if way == 0 else (cut, size[name] - cut)

    def ring_block(name, at, way):
        first, high = ring_part(name, way)
        return whole[name].at[
            pl.ds(pl.multiple_of(ring_index(at) * size[name] + first, 16), high)
        ]

    def ring_gather(name, way, hop):
        target = ring_block(name, spot - hop if way == 0 else spot + hop, way)
        index = (RINGED.index(name), way, hop)
        return remote(target, target, (s.rg_send, s.rg_recv), index, ring_to[way])

    def ring_pass(names, hop):
        for name in names:
            for way in range(2):
                if hop > 0:
                    ring_gather(name, way, hop - 1).wait_recv()
                if hop < count - 1:
                    ring_gather(name, way, hop).start()

    query_pair, text_pair = RINGED[:2], RINGED[2:]

    def ring_passes(*steps):
        for *names, hop in steps:
            ring_pass(names, hop)

    def scatter_passes(*steps):
        for *names, hop in steps:
            scatter_pass(names, hop)

    def ring_gather_sent(name):
        for way in range(2):
            for hop in range(count - 1):
                ring_gather(name, way, hop).wait_send()

    def ring_scatter(name, way, hop):
        first, high = ring_part(name, way)
        return remote(
            ring_block(name, spot - 1 - hop if way == 0 else spot + 1 + hop, way),
            getattr(s, N_R + name).at[hop, pl.ds(first, high)],
            (s.rs_send, s.rs_recv),
            (RINGED.index(name), way, hop),
            ring_to[way],
        )

    def scatter_pass(names, hop):
        for name in names:
            for way in range(2):
                first, high = ring_part(name, way)
                if hop > 0:
                    ring_scatter(name, way, hop - 1).wait_recv()
                    landed = getattr(s, N_R + name)[hop - 1, first : first + high, :]
                    mine = ring_block(name, spot - 1 - hop if way == 0 else spot + 1 + hop, way)
                    if hop < count - 1:
                        mine[...] = mine[...] + landed
                    else:
                        total = mine[...].astype(F32) + landed.astype(F32)
                        owned[name][first : first + high, :] = total
                if hop < count - 1:
                    ring_scatter(name, way, hop).start()

    def ring_scatter_sent(name):
        for way in range(2):
            for hop in range(count - 1):
                ring_scatter(name, way, hop).wait_send()

    side_in = {name: getattr(s, N_Y + name) for name in TERMS}
    line_in = {name: getattr(s, N_Z + name) for name in TERMS}
    owned = dict(
        self=s.own_self,
        kv=s.own_kv,
        cross=s.own_cross,
        in0=s.own_ffn.at[pl.ds(0, fan)],
        in1=s.own_ffn.at[pl.ds(fan, fan)],
        out0=s.own_ffn.at[pl.ds(2 * fan, fan)],
        out1=s.own_ffn.at[pl.ds(3 * fan, fan)],
    )
    order = [*range(1, lines), 0]

    def scatter_side(name, step):
        other = other_line(step)
        return remote(
            block(whole[name], other * 2 + 1 - side, size[name]),
            side_in[name].at[step],
            (s.ss_send, s.ss_recv),
            (TERMS.index(name), step),
            across,
        )

    def scatter_line(name, step):
        other = other_line(step)
        return remote(
            block(whole[name], other * 2 + side, size[name]),
            line_in[name].at[step - 1],
            (s.sl_send, s.sl_recv),
            (TERMS.index(name), step),
            along(step),
        )

    def scatter_start(name):
        for step in order:
            scatter_side(name, step).start()

    def scatter_forward(name):
        for step in range(1, lines):
            other = other_line(step)
            mine = block(whole[name], other * 2 + side, size[name])
            scatter_side(name, step).wait_recv()
            mine[...] = mine[...] + side_in[name][step]
            scatter_line(name, step).start()

    def scatter_finish(name):
        scatter_side(name, 0).wait_recv()
        total = block(whole[name], place, size[name])[...].astype(F32)
        total = total + side_in[name][0].astype(F32)
        for step in range(1, lines):
            scatter_line(name, step).wait_recv()
            total = total + line_in[name][step - 1].astype(F32)
        owned[name][...] = total
        for step in range(1, lines):
            scatter_line(name, step).wait_send()
        for step in range(lines):
            scatter_side(name, step).wait_send()

    halves = {N_SELFQ: 0, N_SELFT: 1, N_CROSS: 0, N_GFT: 1, N_GFQ: 0, N_GC: 1, N_GAQ: 0, N_GAT: 1}

    def sum_buffers(name):
        landed = {N_GAQ: N_SELFQ, N_GAT: N_SELFT, N_GC: N_CROSS}.get(name, name)
        half = s.half_row if name == N_OUT else s.half.at[halves[name]]
        return getattr(s, N_PIN + landed), half, getattr(s, N_FIN + landed)

    def part(name, index):
        if name in (N_SELFQ, N_GAQ):
            return s.part_row.at[index, pl.ds(0, query)]
        if name in (N_SELFT, N_GAT):
            return s.part_row.at[index, pl.ds(query, text)]
        return {N_OUT: s.part_row, N_GFT: s.part_t}.get(name, s.part_q).at[index]

    def sum_copy(name, hop):
        pair_in, half, far_in = sum_buffers(name)
        source, target, device = (
            (part(name, diagonal), pair_in.at[1], beside),
            (part(name, beside), pair_in.at[0], beside),
            (half, far_in, far),
        )[hop]
        index = (SUMS.index(name), hop)
        return remote(source, target, (s.sum_send, s.sum_recv), index, (place, device))

    def sum_forward(name):
        sum_copy(name, 0).wait_recv()
        pair_in, half, _ = sum_buffers(name)
        half[...] = part(name, far)[...] + pair_in[1]
        sum_copy(name, 2).start()

    def sum_finish(name):
        sum_copy(name, 1).wait_recv()
        sum_copy(name, 2).wait_recv()
        pair_in, _, far_in = sum_buffers(name)
        total = part(name, rank)[...].astype(F32) + pair_in[0].astype(F32)
        return total + far_in[...].astype(F32)

    def sum_sent(name, hops=(0, 1, 2)):
        for hop in hops:
            sum_copy(name, hop).wait_send()

    shared = dict(
        c=s.c,
        ft=s.f_t,
        fq=s.f_q,
        gsat=s.gsa_t,
        gsaq=s.f_q,
        out=s.gy,
    )

    def shared_part(name, index):
        if name in (N_GCA, N_SGQ):
            return s.x.at[index, pl.ds(0, query)]
        if name == N_SGT:
            return s.x.at[index, pl.ds(query, text)]
        return shared[name].at[index]

    def share_copy(name, hop):
        index, device = ((rank, far), (rank, beside), (far, beside))[hop]
        return remote(
            shared_part(name, index),
            shared_part(name, index),
            (s.share_send, s.share_recv),
            (SHARES.index(name), hop),
            (place, device),
        )

    def share_start(name):
        share_copy(name, 0).start()
        share_copy(name, 1).start()

    def share_forward(name):
        share_copy(name, 0).wait_recv()
        share_copy(name, 2).start()

    def share_finish(name):
        share_copy(name, 1).wait_recv()
        share_copy(name, 2).wait_recv()

    def share_sent(name):
        for hop in range(3):
            share_copy(name, hop).wait_send()

    def vec(index):
        return s.vecs[index : index + 1, :]

    def column_total(values):
        return jnp.sum(values.astype(F32), axis=0, keepdims=True)

    def row_at(row):
        return pl.ds(pl.multiple_of(row * length, length), length)

    def put_stat(index, values, weight):
        total = jnp.sum(
            jnp.sum(values * values, axis=1, keepdims=True) * weight, axis=0, keepdims=True
        )
        s.small[10:11, :] += jnp.where(lanes(z.model) == index, total, 0.0)

    load_x = pltpu.make_async_copy(s.x_h, s.x, s.load_sem.at[0])
    load_gy = pltpu.make_async_copy(s.gy_h, s.gy, s.load_sem.at[1])
    load_x.start()
    barrier = pltpu.get_barrier_semaphore()
    partners = [along(step) for step in range(1, lines)] + [
        across,
        (place, beside),
        (place, far),
    ]
    for partner in partners:
        pl.semaphore_signal(barrier, inc=1, device_id=partner, device_id_type=MESH)
    for item in own_in:
        item.start()
    own = z.model // count
    shard[N_VEC][...] = jnp.zeros((16, 128), BF16)
    shard[N_VEC][: s.vectors.shape[0], :own] = s.vectors[...]
    pack(N_SELF, [s.self_qkv[0], s.self_qkv[1], s.self_qkv[2], turn(s.self_out[...])])
    pl.semaphore_wait(barrier, len(partners))
    gather_start(N_VEC)
    gather_start(N_SELF)
    pack(N_KV, [s.cross_kv[0], s.cross_kv[1]])
    pack(N_CROSS, [s.cross_q[...], turn(s.cross_out[...])])
    gather_start(N_KV)
    gather_start(N_CROSS)
    for kind in range(2):
        shard["out%d" % kind][...] = s.ffn_out[kind]
        own_in[kind].wait()

    chunk_count = z.features // CHUNK
    tail = z.features - chunk_count * CHUNK

    def load_chunk(index):
        slot = lax.rem(index, CHUNKS_HELD)
        return pltpu.make_async_copy(
            s.feat_h.at[pl.ds(pl.multiple_of(index * CHUNK, CHUNK), CHUNK)],
            s.chunk.at[slot],
            s.chunk_sem.at[slot],
        )

    def load_chunks():
        for index in range(CHUNKS_HELD):
            load_chunk(index).start()

    load_tail = pltpu.make_async_copy(
        s.feat_h.at[pl.ds(chunk_count * CHUNK, tail)], s.tail, s.load_sem.at[2]
    )
    load_chunks()
    load_tail.start()
    load_gy.start()

    s.small[...] = jnp.zeros_like(s.small)
    s.bias[...] = jnp.zeros_like(s.bias)
    for row, at, index in ((0, 0, 0), (0, 2, 1), (1, 0, 2), (2, 1, 3)):
        s.bias[row : row + 1, at * WIDE : at * WIDE + width] = s.head_bias[
            index : index + 1, :
        ].astype(F32)
    s.bias[3:5, : z.hidden] = s.ffn_bias[...].astype(F32)
    slots = lanes(query).astype(F32) * (1.0 / QUERIES)
    s.code[:, :query] = jnp.broadcast_to(jnp.floor(slots), (rows, query))
    s.code[:, query:] = jnp.where(s.valid[...] == 1, s.segment[...], -1).astype(F32)
    same = lax.broadcasted_iota(jnp.int32, (text, text), 0) == lanes(text)

    def as_column(values):
        return jnp.sum(jnp.where(same, values.astype(F32), 0.0), axis=1, keepdims=True)

    for row in range(rows):
        s.text_codes[row] = as_column(s.segment[row : row + 1, :])
    s.weight[...] = as_column((s.valid[pl.ds(rank, 1), :] == 1).astype(jnp.int32))
    gather_forward(N_VEC)
    gather_finish(N_VEC)
    for index in range(count):
        s.vecs[:, index * own : (index + 1) * own] = s.w_vec[
            index * 16 : (index + 1) * 16, :own
        ].astype(F32)
    load_x.wait()

    @pl.loop(0, rows)
    def _(row):
        normed, _ = norm_parts(s.x[row].astype(F32))
        s.a[row_at(row), :] = (normed * vec(0) + vec(1)).astype(BF16)

    ring_pass(query_pair, 0)
    s.x_own[...] = s.x[rank]
    weight_query, weight_text = jnp.ones((query, 1), F32), s.weight[...]
    weight_own = jnp.concatenate([weight_query, weight_text], axis=0)
    s.small[10:11, :] += jnp.where(
        lanes(z.model) == 4, jnp.sum(weight_own, axis=0, keepdims=True), 0.0
    )
    put_stat(0, s.x_own[...].astype(F32), weight_own)

    gather_forward(N_SELF)
    gather_finish(N_SELF)
    widen(s.m_self, s.w_self, 4)

    def self_mask(row):
        at = lax.broadcasted_iota(jnp.int32, (query, 1), 0).astype(F32) * (1.0 / QUERIES)
        codes = jnp.concatenate([jnp.floor(at), s.text_codes[row]], axis=0)
        return codes == s.code[pl.ds(row, 1), :]

    def send_order(step):
        chip_at = chip + (1 - 2 * chip) * (1 - step // 2)
        core_at = core + (1 - 2 * core) * (1 - lax.rem(step, 2))
        return chip_at * 2 + core_at

    def send_pairs(step, names):
        @pl.when(step == 0)
        def _():
            for name in names:
                sum_copy(name, 0).start()

        @pl.when(step == 2)
        def _():
            for name in names:
                sum_copy(name, 1).start()

    def self_row(step):
        row = send_order(step)
        at = row_at(row)
        qkv = dot(s.a[at, :], s.w_self[:, : 3 * WIDE]) + s.bias[0:1, : 3 * WIDE]
        low = qkv.astype(BF16)
        s.qkv[at, :] = low
        queries = spread(low[:, :WIDE] * jnp.asarray(z.scale, BF16), heads)
        scores = dot_columns(queries, low[:, WIDE : 2 * WIDE])
        mask = self_mask(row)
        scores = jnp.concatenate(
            [
                jnp.where(mask, scores[head * length : (head + 1) * length], MASKED)
                for head in range(heads)
            ],
            axis=0,
        )
        probs = softmax(scores).astype(BF16)
        s.p_self[row] = probs
        mixed = fold(dot(probs, low[:, 2 * WIDE :]), heads, length).astype(BF16)
        s.o[at, :] = mixed
        s.part_row[row] = dot_columns(mixed, s.w_self[:, 3 * WIDE :]).astype(BF16)
        send_pairs(step, (N_SELFQ, N_SELFT))

    pl.loop(0, rows // 2)(self_row)
    sum_forward(N_SELFQ)
    sum_forward(N_SELFT)
    ring_pass(text_pair, 0)
    gather_forward(N_KV)
    pl.loop(rows // 2, rows)(self_row)
    gather_forward(N_CROSS)
    gather_finish(N_KV)
    widen(s.m_kv, s.w_kv, 2)

    def project(values):
        return dot(values, s.w_kv[...]) + s.bias[2:3, : 2 * WIDE]

    def project_chunk(index, first):
        load_chunk(index).wait()
        result = project(s.chunk[lax.rem(index, CHUNKS_HELD)])

        @pl.when(index + CHUNKS_HELD < chunk_count)
        def _():
            load_chunk(index + CHUNKS_HELD).start()

        for tile in range(2 * WIDE // 128):
            at = first + tile % 2 * CHUNK
            s.stage[tile // 2, at : at + CHUNK, :] = result[
                :, tile * 128 : (tile + 1) * 128
            ]
        keys = CHUNK // z.images
        key_at = pl.ds(pl.multiple_of(index * keys, keys), keys)
        for image in range(z.images):
            for tile in range(2 * WIDE // 128):
                s.kv[image, key_at, tile * 128 : (tile + 1) * 128] = s.stage.at[tile // 2][
                    pl.ds(first + tile % 2 * CHUNK + image, keys, stride=z.images), :
                ].astype(BF16)

    def project_pair(pair):
        for inner in range(2):
            project_chunk(pair * 2 + inner, inner * 2 * CHUNK)

    quarter = chunk_count // 8
    pl.loop(0, quarter)(project_pair)

    after = s.x_own[:query, :].astype(F32) + sum_finish(N_SELFQ) + vec(6)
    s.after_self[:query, :] = after
    normed, _ = norm_parts(after)
    s.c[rank] = (normed * vec(2) + vec(3)).astype(BF16)
    share_start(N_C)
    put_stat(1, after, weight_query)
    ring_pass(query_pair, 1)
    pl.loop(quarter, 2 * quarter)(project_pair)
    ring_pass(text_pair, 1)
    after = s.x_own[query:, :].astype(F32) + sum_finish(N_SELFT) + vec(6)
    s.after_self[query:, :] = after
    normed, _ = norm_parts(after)
    s.f_t[rank] = (normed * vec(4) + vec(5)).astype(BF16)
    share_start(N_FT)
    put_stat(1, after, weight_text)
    put_stat(2, after, weight_text)
    ring_passes((N_IN0, 2))
    pl.loop(2 * quarter, 3 * quarter)(project_pair)
    share_forward(N_C)
    ring_passes((N_OUT0, 2), (N_IN1, 2))
    pl.loop(3 * quarter, chunk_count // 2)(project_pair)
    load_tail.wait()
    last = project(s.tail[...])
    first_row = lax.broadcasted_iota(jnp.int32, (tail, 1), 0) == 0
    for image in range(z.images):
        s.kv[image, z.keys - 1 :, :] = jnp.where(
            first_row, jnp.broadcast_to(last[image : image + 1, :], last.shape), 0.0
        ).astype(BF16)
    load_chunks()
    ring_passes((N_OUT1, 2), (N_IN0, 3))
    gather_finish(N_CROSS)
    widen(s.m_cross, s.w_cross, 2)
    share_finish(N_C)
    queries_total = rows * query
    cross_query = dot(s.c[...].reshape(queries_total, z.model), s.w_cross[:, :WIDE])
    s.qc[...] = (cross_query + s.bias[1:2, :WIDE]).astype(BF16).reshape(s.qc.shape)
    is_key = lanes(PADDED_KEYS) < z.keys

    def all_slots(ref):
        return ref[...].reshape(queries_total, WIDE)

    def slot_of(image):
        slot = jnp.int32(0)
        for other in range(1, z.images):
            slot = jnp.where(s.image_of[other] == image, other, slot)
        return slot

    unroll = 4
    groups = z.images // unroll

    def cross_row(step):
        row = send_order(step)
        for inner in range(SLOTS):
            slot = row * SLOTS + inner
            image = s.image_of[slot]
            queries = spread(s.qc[slot] * jnp.asarray(z.scale, BF16), heads)
            scores = dot_columns(queries, s.kv[image, :, :WIDE])
            probs = softmax(jnp.where(is_key, scores, MASKED)).astype(BF16)
            s.p_cross[slot] = probs
            mixed = fold(dot(probs, s.kv[image, :, WIDE:]), heads, QUERIES)
            s.oc[slot] = mixed.astype(BF16)
        mixed = s.oc[pl.ds(row * SLOTS, SLOTS)].reshape(query, WIDE)
        s.part_q[row] = dot_columns(mixed, s.w_cross[:, WIDE:]).astype(BF16)
        send_pairs(step, (N_CROSS,))

    pl.loop(0, rows // 2)(cross_row)
    ring_passes((N_OUT0, 3), (N_IN1, 3))
    sum_sent(N_SELFQ)
    sum_sent(N_SELFT)
    sum_forward(N_CROSS)
    share_forward(N_FT)
    ring_passes((N_OUT1, 3))
    pl.loop(rows // 2, rows)(cross_row)
    ring_passes((N_IN0, N_OUT0, 4), (N_IN1, 4))
    ring_passes((N_OUT1, 4), (N_IN0, N_OUT0, 5), (N_IN1, N_OUT1, 5))
    after_query = s.after_self[:query, :] + sum_finish(N_CROSS) + vec(7)
    s.after_query[...] = after_query
    normed, _ = norm_parts(after_query)
    s.f_q[rank] = (normed * vec(4) + vec(5)).astype(BF16)
    share_start(N_FQ)
    put_stat(2, after_query, weight_query)
    ring_passes((N_IN0, N_OUT0, 6), (N_IN1, N_OUT1, 6), (N_IN0, 7))
    share_forward(N_FQ)
    ring_passes((N_OUT0, 7))
    load_gy.wait()
    gather_sent(N_SELF)
    gather_sent(N_KV)
    sum_sent(N_CROSS)
    share_finish(N_FQ)

    f_of = {0: s.f_q, 1: s.f_t}
    w_in = {0: s.m_in0, 1: s.m_in1}
    w_out = {0: s.m_out0, 1: s.m_out1}

    def grad_rows(kind, row):
        return s.gy[row, kind * query : (kind + 1) * query, :]

    def feed_forward(kind, target, send):
        for pair in (1 - chip, chip):
            values = f_of[kind][pl.ds(pair * 2, 2)].reshape(2 * query, z.model)
            grads = jnp.concatenate(
                [grad_rows(kind, pair * 2), grad_rows(kind, pair * 2 + 1)], axis=0
            )
            up = dot(values, w_in[kind][...]) + s.bias[3 + kind : 4 + kind, : z.hidden]
            share = 0.5 * (1.0 + lax.erf(up * (0.5**0.5)))
            hidden = (up * share).astype(BF16)
            slope = share + up * (jnp.exp(-0.5 * up * up) * ((0.5 / math.pi) ** 0.5))
            grad_up = (dot(grads, w_out[kind][...]) * slope).astype(BF16)
            at = pl.ds(pl.multiple_of(pair * 2 * query, 2 * query), 2 * query)
            if kind == 0:
                slots = pl.ds(pair * 2 * SLOTS, 2 * SLOTS)
                s.hid[slots] = hidden.reshape(2 * SLOTS, QUERIES, z.hidden)
                s.gu[slots] = grad_up.reshape(2 * SLOTS, QUERIES, z.hidden)
            else:
                s.m_self[at, :] = hidden
                cut = s.m_kv.shape[1]
                for first in range(0, z.hidden, cut):
                    below = pl.ds(pl.multiple_of(first // cut * queries_total + at.start, 16), at.size)
                    s.m_kv[below, :] = grad_up[:, first : first + cut]
            back = dot_columns(grad_up, w_in[kind][...]).astype(BF16)
            target[pl.ds(pair * 2, 2)] = back.reshape(2, query, z.model)
            send(pair)
            if kind == 0 and pair is not chip:
                sum_forward(N_GFQ)
            s.small[20 + kind : 21 + kind, :] += column_total(grad_up)
            out = dot_columns(hidden, w_out[kind][...]).astype(BF16)
            out = out.reshape(2, query, z.model)
            s.part_row[pl.ds(pair * 2, 2), kind * query : (kind + 1) * query, :] = out

    def weight_terms(kind):
        values = f_of[kind][...].reshape(queries_total, z.model)
        grads = jnp.concatenate([grad_rows(kind, row) for row in range(rows)], axis=0)
        if kind == 0:
            hidden, grad_up = (
                ref[...].reshape(queries_total, z.hidden) for ref in (s.hid, s.gu)
            )
        else:
            hidden = s.m_self[:queries_total, :]
            grad_up = jnp.concatenate(
                [
                    s.m_kv[at : at + queries_total, :]
                    for at in range(0, z.hidden // s.m_kv.shape[1] * queries_total, queries_total)
                ],
                axis=1,
            )
        for name, left, right in (
            ("in%d" % kind, values, grad_up),
            ("out%d" % kind, grads, hidden),
        ):
            ring_gather_sent(name)
            for at in range(0, z.model, WIDE):
                whole[name][at : at + WIDE, :] = dot_rows(left[:, at : at + WIDE], right).astype(
                    BF16
                )

    hops = iter((0, 1))
    feed_forward(0, s.part_q, lambda pair: sum_copy(N_GFQ, next(hops)).start())
    ring_pass(text_pair, 7)
    share_finish(N_FT)
    hops = iter((0, 1))
    feed_forward(1, s.part_t, lambda pair: sum_copy(N_GFT, next(hops)).start())
    weight_terms(0)
    share_sent(N_FQ)
    sum_forward(N_GFT)
    scatter_pass(query_pair, 0)
    weight_terms(1)
    scatter_pass(text_pair, 0)
    sum_copy(N_OUT, 0).start()
    sum_copy(N_OUT, 1).start()
    scatter_passes((N_IN0, 1))

    def own_back(total, after, grads, slot):
        normed, scale = norm_parts(after)
        s.small[4:5, :] += column_total(total * normed)
        s.small[5:6, :] += column_total(total)
        s.small[slot : slot + 1, :] += column_total(grads)
        return grads.astype(F32) + norm_grad(normed, scale, vec(4), total)

    grad_query = own_back(sum_finish(N_GFQ), s.after_query[...], grad_rows(0, rank), 8)
    s.g_own[:query, :] = grad_query
    grad_query_low = grad_query.astype(BF16)
    s.x[rank, :query, :] = grad_query_low
    s.small[7:8, :] += column_total(grad_query_low)
    share_start(N_GCA)
    sum_forward(N_OUT)
    scatter_passes((N_OUT0, 1), (N_IN1, N_OUT1, 1))
    grad_text = own_back(sum_finish(N_GFT), s.after_self[query:, :], grad_rows(1, rank), 9)
    s.g_own[query:, :] = grad_text
    grad_text_low = grad_text.astype(BF16)
    s.gsa_t[rank] = grad_text_low
    s.small[6:7, :] += column_total(grad_text_low)
    share_start(N_GSAT)
    scatter_passes((N_IN0, N_OUT0, 2))
    share_forward(N_GCA)
    scatter_passes((N_IN1, 2))
    share_finish(N_GCA)

    grad_mixed = dot(s.x[:, :query, :].reshape(queries_total, z.model), s.w_cross[:, WIDE:])
    s.goc[...] = grad_mixed.astype(BF16).reshape(s.goc.shape)

    def stage_put(image, values):
        for tile in range(WIDE // 128):
            s.stage.at[tile][pl.ds(image, PADDED_KEYS, stride=z.images), :] = values[
                :, tile * 128 : (tile + 1) * 128
            ]

    score_places = [(s.hid, 0), (s.hid, z.hidden // 2), (s.gu, 0), (s.gu, z.hidden // 2)][:heads]

    def cross_back(step):
        row = send_order(step)
        for inner in range(SLOTS):
            slot = row * SLOTS + inner
            image = s.image_of[slot]
            grads = spread(s.goc[slot], heads)
            wide = s.p_cross[slot].astype(F32)
            grad_probs = dot_columns(grads, s.kv[image, :, WIDE:])
            delta = jnp.sum(wide * grad_probs, axis=-1, keepdims=True)
            grad_scores = (wide * (grad_probs - delta)).astype(BF16)
            for head, (ref, at) in enumerate(score_places):
                ref[slot, :, at : at + PADDED_KEYS] = grad_scores[
                    head * QUERIES : (head + 1) * QUERIES, :
                ]
            mixed = fold(dot(grad_scores, s.kv[image, :, :WIDE]), heads, QUERIES) * z.scale
            s.gqc[slot] = mixed.astype(BF16)
        mixed = s.gqc[pl.ds(row * SLOTS, SLOTS)].reshape(query, WIDE)
        s.part_q[row] = dot_columns(mixed, s.w_cross[:, :WIDE]).astype(BF16)
        send_pairs(step, (N_GC,))

    sum_sent(N_GFQ)
    pl.loop(0, rows // 2)(cross_back)
    sum_sent(N_GFT)
    sum_forward(N_GC)
    scatter_passes((N_OUT1, 2), (N_IN0, 3))
    pl.loop(rows // 2, rows)(cross_back)
    scatter_passes((N_OUT0, 3), (N_IN1, N_OUT1, 3))
    s.small[18:19, :WIDE] += column_total(all_slots(s.gqc))
    low_half = lanes(128) < HEAD
    gather_sent(N_CROSS)
    grad_cq = dot_rows(s.c[...].reshape(queries_total, z.model), all_slots(s.gqc))
    grad_co = dot_rows(s.x[:, :query, :].reshape(queries_total, z.model), all_slots(s.oc))
    s.m_cross[:, :128] = grad_cq[:, :128].astype(BF16)
    s.m_cross[:, 128:256] = grad_co[:, :128].astype(BF16)
    s.m_cross[:, 256:] = jnp.where(
        low_half, grad_cq[:, 128:], pltpu.roll(grad_co[:, 128:], HEAD, 1)
    ).astype(BF16)
    scatter_start(N_CROSS)

    after_ffn_sum = sum_finish(N_OUT)
    after_query_out = s.after_query[...] + after_ffn_sum[:query] + vec(8)
    after_text_out = s.after_self[query:, :] + after_ffn_sum[query:] + vec(9)
    put_stat(3, after_query_out, weight_query)
    put_stat(3, after_text_out, weight_text)
    s.gy[rank, :query, :] = after_query_out.astype(BF16)
    s.gy[rank, query:, :] = after_text_out.astype(BF16)
    share_start(N_OUT)

    def key_grad(image):
        slot = slot_of(image)
        queries = spread(s.qc[slot] * jnp.asarray(z.scale, BF16), heads)
        grad_scores = jnp.concatenate(
            [ref[slot, :, at : at + PADDED_KEYS] for ref, at in score_places], axis=0
        )
        return dot_rows(grad_scores, queries)

    def value_grad(image):
        slot = slot_of(image)
        return dot_rows(s.p_cross[slot], spread(s.goc[slot], heads))

    def grads_at(at):
        return jnp.concatenate(
            [s.stage[tile, at, :].astype(BF16) for tile in range(WIDE // 128)], axis=1
        )

    def features_start(grad_of):
        @pl.loop(0, groups)
        def _(group):
            for inner in range(unroll):
                image = group * unroll + inner
                stage_put(image, grad_of(image))

        grads = grads_at(pl.ds(chunk_count * CHUNK, tail))
        s.turned[...] = dot_rows(grads, s.tail[...])
        s.col_sum[...] = column_total(grads)

    def features_pair(pair):
        total, sums = s.turned[...], s.col_sum[...]
        for inner in range(2):
            index = pair * 2 + inner
            load_chunk(index).wait()
            grads = grads_at(pl.ds(pl.multiple_of(index * CHUNK, CHUNK), CHUNK))
            total = total + dot_rows(grads, s.chunk[lax.rem(index, CHUNKS_HELD)])
            sums = sums + column_total(grads)
        s.turned[...] = total
        s.col_sum[...] = sums

        @pl.when(pair * 2 + CHUNKS_HELD < chunk_count)
        def _():
            for inner in range(2):
                load_chunk(pair * 2 + inner + CHUNKS_HELD).start()

    scatter_passes((N_IN0, 4))
    features_start(key_grad)
    share_forward(N_GSAT)
    scatter_passes((N_OUT0, 4), (N_IN1, N_OUT1, 4))
    pl.loop(0, chunk_count // 2)(features_pair)
    load_chunks()
    turned = s.turned[...].T
    s.m_kv[:, :128] = turned[:, :128].astype(BF16)
    s.m_kv[:, 256:] = turned[:, 128:].astype(BF16)

    scatter_passes((N_IN0, 5))
    scatter_forward(N_CROSS)
    features_start(value_grad)
    cross_sum = sum_finish(N_GC)
    normed, scale = norm_parts(s.after_self[:query, :])
    s.small[2:3, :] += column_total(cross_sum * normed)
    s.small[3:4, :] += column_total(cross_sum)
    grad_query = s.g_own[:query, :] + norm_grad(normed, scale, vec(2), cross_sum)
    s.g_own[:query, :] = grad_query
    grad_query_low = grad_query.astype(BF16)
    s.f_q[rank] = grad_query_low
    s.small[6:7, :] += column_total(grad_query_low)
    share_start(N_GSAQ)
    scatter_passes((N_OUT0, N_IN1, N_OUT1, 5))
    share_forward(N_OUT)
    scatter_passes((N_IN0, 6))
    pl.loop(0, chunk_count // 2)(features_pair)
    s.small[19:20, :WIDE] += s.col_sum[...]
    turned = s.turned[...].T
    s.m_kv[:, 128:256] = turned[:, :128].astype(BF16)
    s.m_kv[:, 256:] = jnp.where(
        low_half, s.m_kv[:, 256:].astype(F32), pltpu.roll(turned[:, 128:], HEAD, 1)
    ).astype(BF16)
    scatter_passes((N_OUT0, 6))
    scatter_start(N_KV)
    scatter_passes((N_IN1, 6))
    share_forward(N_GSAQ)
    scatter_passes((N_OUT1, 6))
    share_finish(N_GSAT)
    share_finish(N_GSAQ)

    def self_back(step):
        row = send_order(step)
        at = row_at(row)
        grads = jnp.concatenate([s.f_q[row], s.gsa_t[row]], axis=0)
        low = s.qkv[at, :]
        queries = spread(low[:, :WIDE] * jnp.asarray(z.scale, BF16), heads)
        grad_mixed = dot(grads, s.w_self[:, 3 * WIDE :]).astype(BF16)
        grad_mixed = spread(grad_mixed, heads)
        probs = s.p_self[row]
        wide = probs.astype(F32)
        grad_probs = dot_columns(grad_mixed, low[:, 2 * WIDE :])
        delta = jnp.sum(wide * grad_probs, axis=-1, keepdims=True)
        grad_scores = (wide * (grad_probs - delta)).astype(BF16)
        grad_q = fold(dot(grad_scores, low[:, WIDE : 2 * WIDE]), heads, length) * z.scale
        grad_k = dot_rows(grad_scores, queries)
        grad_v = dot_rows(probs, grad_mixed)
        grad_low = jnp.concatenate([grad_q, grad_k, grad_v], axis=1).astype(BF16)
        s.qkv[at, :] = grad_low
        s.small[16:17, :WIDE] += column_total(grad_low[:, :WIDE])
        s.small[17:18, :WIDE] += column_total(grad_low[:, 2 * WIDE :])
        s.part_row[row] = dot_columns(grad_low, s.w_self[:, : 3 * WIDE]).astype(BF16)
        send_pairs(step, (N_GAQ, N_GAT))

    sum_sent(N_OUT)
    sum_sent(N_GC)
    share_sent(N_GCA)
    pl.loop(0, rows // 2)(self_back)
    sum_forward(N_GAQ)
    sum_forward(N_GAT)
    scatter_passes((N_IN0, N_OUT0, 7))
    pl.loop(rows // 2, rows)(self_back)

    grads_all = [dot_rows(s.a[...], s.qkv[:, i * WIDE : (i + 1) * WIDE]) for i in range(3)]
    grad_stream = jnp.concatenate(
        [ref[row] for row in range(rows) for ref in (s.f_q, s.gsa_t)], axis=0
    )
    grads_all.append(dot_rows(grad_stream, s.o[...]))
    for i, value in enumerate(grads_all):
        s.m_self[:, i * 128 : (i + 1) * 128] = value[:, :128].astype(BF16)
    for i in range(2):
        s.m_self[:, (4 + i) * 128 : (5 + i) * 128] = jnp.where(
            low_half, grads_all[2 * i][:, 128:], pltpu.roll(grads_all[2 * i + 1][:, 128:], HEAD, 1)
        ).astype(BF16)
    scatter_start(N_SELF)
    scatter_passes((N_IN1, 7))
    scatter_forward(N_KV)
    scatter_passes((N_OUT1, 7))

    def stream_back(name, at):
        total = sum_finish(name)
        normed, scale = norm_parts(s.x_own[at, :].astype(F32))
        s.small[0:1, :] += column_total(total * normed)
        s.small[1:2, :] += column_total(total)
        grad = s.g_own[at, :] + norm_grad(normed, scale, vec(0), total)
        s.x[rank, at, :] = grad.astype(BF16)

    stream_back(N_GAQ, pl.ds(0, query))
    share_start(N_SGQ)
    stream_back(N_GAT, pl.ds(query, text))
    share_start(N_SGT)
    scatter_forward(N_SELF)

    def small_copy(source, hop, device):
        target = s.small_in.at[hop] if source is s.small else s.small_in.at[hop, pl.ds(0, 16)]
        return remote(source, target, (s.small_send, s.small_recv), (hop,), device)

    shared_rows = s.small.at[pl.ds(0, 16)]
    for hop, device in enumerate(((place, beside), (place, far))):
        item = small_copy(shared_rows, hop, device)
        item.start()
        item.wait()
        s.small[:16, :] += s.small_in[hop, :16, :]
    item = small_copy(s.small, 2, across)
    item.start()
    share_forward(N_SGQ)
    share_forward(N_SGT)
    item.wait()
    s.small[...] += s.small_in[2]
    items = [small_copy(s.small, 2 + step, along(step)) for step in range(1, lines)]
    for item in items:
        item.start()
    share_finish(N_OUT)
    store_out = pltpu.make_async_copy(s.gy, s.out_h, s.load_sem.at[3])
    store_out.start()
    share_finish(N_SGQ)
    share_finish(N_SGT)
    store_sg = pltpu.make_async_copy(s.x, s.sg_h, s.load_sem.at[4])
    store_sg.start()
    total = s.small[...]
    for step in range(1, lines):
        items[step - 1].wait_recv()
        total = total + s.small_in[2 + step]
    s.small_out[...] = total
    for name in TERMS:
        scatter_finish(name)
    for name in RINGED:
        ring_scatter_sent(name)
    for item in items:
        item.wait_send()
    gather_sent(N_VEC)
    for name in (N_GAQ, N_GAT):
        sum_sent(name)
    for name in SHARES:
        if name not in (N_FQ, N_GCA):
            share_sent(name)
    store_out.wait()
    store_sg.wait()


def finish_kernel(
    out_in,
    grad_in,
    own_self,
    own_kv,
    own_cross,
    own_ffn,
    small,
    out_stream,
    stream_grad,
    grad_qkv,
    grad_out,
    grad_cq,
    grad_ckv,
    grad_co,
    grad_in_w,
    grad_out_w,
    grad_vectors,
    grad_heads,
    grad_hidden,
    rms,
):
    out_stream[...] = out_in[...]
    stream_grad[...] = grad_in[...].astype(F32)

    def piece(packed, count, index):
        at = (count + index // 2) * 128 + index % 2 * HEAD
        return packed[:, index * 128 : (index + 1) * 128], packed[:, at : at + HEAD]

    def put(ref, pieces):
        ref[:, :128] = pieces[0]
        ref[:, 128:] = pieces[1]

    def put_turned(ref, pieces):
        ref[:128, :] = pieces[0].T
        ref[128:, :] = pieces[1].T

    for index in range(3):
        put(grad_qkv.at[index], piece(own_self, 4, index))
    put_turned(grad_out, piece(own_self, 4, 3))
    put(grad_cq, piece(own_cross, 2, 0))
    put_turned(grad_co, piece(own_cross, 2, 1))
    for index in range(2):
        put(grad_ckv.at[index], piece(own_kv, 2, index))
        fan = grad_in_w.shape[1]
        grad_in_w[index] = own_ffn[index * fan : (index + 1) * fan, :]
        grad_out_w[index] = own_ffn[(2 + index) * fan : (3 + index) * fan, :]
    place, own = lax.axis_index(N_DP), grad_vectors.shape[1]
    total = jnp.zeros(grad_vectors.shape, F32)
    for index in range(small.shape[1] // own):
        mine = small[: total.shape[0], index * own : (index + 1) * own]
        total = total + jnp.where(place == index, mine, 0.0)
    grad_vectors[...] = total
    grad_heads[...] = small[16:20, : grad_heads.shape[1]]
    grad_hidden[...] = small[20:22, : grad_hidden.shape[1]]
    stats = small[10:11, :128]
    valid = jnp.sum(jnp.where(lanes(128) == 4, stats, 0.0), axis=1, keepdims=True)
    rms[...] = jnp.sqrt(stats / (valid * small.shape[1]))[:, :4]


def layer(
    stream_in,
    features,
    image_index,
    text_segment,
    text_valid,
    self_qkv,
    self_out,
    cross_q,
    cross_kv,
    cross_out,
    ffn_in,
    ffn_out,
    vectors,
    head_bias,
    ffn_bias,
    out_grad,
):
    count = lax.axis_size(N_DP)
    tokens, model = stream_in.shape
    width, hidden = self_qkv.shape[2], ffn_in.shape[2]
    fan, feat_fan = ffn_in.shape[1], cross_kv.shape[1]
    rows, text = text_segment.shape
    images, keys, feat = features.shape
    query = SLOTS * QUERIES
    z = types.SimpleNamespace(
        count=count,
        rows=rows,
        width=width,
        heads=width // HEAD,
        fan=fan,
        feat_fan=feat_fan,
        model=model,
        hidden=hidden,
        features=images * keys,
        images=images,
        keys=keys,
        scale=HEAD**-0.5,
    )
    lines = count // 2

    operands = dict(
        image_of=image_index.reshape(-1),
        vectors=vectors,
        self_qkv=self_qkv,
        self_out=self_out,
        cross_q=cross_q,
        cross_kv=cross_kv,
        cross_out=cross_out,
        ffn_out=ffn_out.transpose(0, 2, 1),
        head_bias=head_bias,
        ffn_bias=ffn_bias,
        segment=text_segment,
        valid=text_valid,
        ffn_in=ffn_in,
        x_h=stream_in.reshape(rows, ROW_LEN, model),
        gy_h=out_grad.reshape(rows, ROW_LEN, model),
        feat_h=features.transpose(1, 0, 2).reshape(keys * images, feat),
    )
    spaces = dict.fromkeys(operands, pltpu.VMEM) | {"image_of": pltpu.SMEM}
    spaces |= dict.fromkeys(("ffn_in", "x_h", "gy_h", "feat_h"), pl.ANY)
    results = dict(
        out_h=((rows, ROW_LEN, model), BF16),
        sg_h=((rows, ROW_LEN, model), BF16),
        own_self=((fan, 4 * width), F32),
        own_kv=((feat_fan, 2 * width), F32),
        own_cross=((fan, 2 * width), F32),
        own_ffn=((4 * fan, hidden), F32),
        small_out=((24, model), F32),
    )
    chunk_rows = (keys + PADDED_KEYS - keys) * images
    buffers = dict(
        w_vec=((count * 16, 128), BF16),
        vecs=((16, model), F32),
        bias=((8, max(3 * WIDE, hidden)), F32),
        code=((rows, ROW_LEN), F32),
        text_codes=((rows, text, 1), F32),
        weight=((text, 1), F32),
        m_self=((model, 4 * width), BF16),
        m_kv=((feat, 2 * width), BF16),
        m_cross=((model, 2 * width), BF16),
        w_self=((model, 4 * WIDE), BF16),
        w_kv=((feat, 2 * WIDE), BF16),
        w_cross=((model, 2 * WIDE), BF16),
        x=((rows, ROW_LEN, model), BF16),
        x_own=((ROW_LEN, model), BF16),
        gy=((rows, ROW_LEN, model), BF16),
        a=((tokens, model), BF16),
        qkv=((tokens, 3 * WIDE), BF16),
        o=((tokens, WIDE), BF16),
        p_self=((rows, z.heads * ROW_LEN, ROW_LEN), BF16),
        c=((rows, query, model), BF16),
        f_q=((rows, query, model), BF16),
        f_t=((rows, query, model), BF16),
        gsa_t=((rows, query, model), BF16),
        qc=((images, QUERIES, WIDE), BF16),
        gqc=((images, QUERIES, WIDE), BF16),
        goc=((images, QUERIES, WIDE), BF16),
        oc=((images, QUERIES, WIDE), BF16),
        kv=((images, PADDED_KEYS, 2 * WIDE), BF16),
        p_cross=((images, z.heads * QUERIES, PADDED_KEYS), BF16),
        stage=((WIDE // 128, PADDED_KEYS * images, 128), F32),
        turned=((WIDE, feat), F32),
        col_sum=((1, WIDE), F32),
        chunk=((CHUNKS_HELD, CHUNK, feat), BF16),
        tail=((images * keys % CHUNK, feat), BF16),
        hid=((images, QUERIES, hidden), BF16),
        gu=((images, QUERIES, hidden), BF16),
        part_row=((rows, ROW_LEN, model), BF16),
        part_q=((rows, query, model), BF16),
        part_t=((rows, query, model), BF16),
        after_self=((ROW_LEN, model), F32),
        after_query=((query, model), F32),
        g_own=((ROW_LEN, model), F32),
        small=((24, model), F32),
        small_in=((2 + lines, 24, model), F32),
    )
    for name in (N_IN0, N_IN1, N_OUT0, N_OUT1):
        buffers["m_" + name] = ((model, hidden), BF16)
        buffers[N_R + name] = ((count - 1, fan, hidden), BF16)
    for name in (N_SELFQ, N_SELFT, N_OUT, N_CROSS, N_GFT, N_GFQ):
        block = (ROW_LEN if name == N_OUT else query, model)
        buffers[N_PIN + name] = ((2, *block), BF16)
        buffers[N_FIN + name] = (block, BF16)
    buffers["half_row"] = ((ROW_LEN, model), BF16)
    buffers["half"] = ((2, query, model), BF16)
    for name in TERMS:
        high = feat_fan if name == N_KV else fan
        across = (4 if name == N_SELF else 2) * width
        buffers[N_Y + name] = ((lines, high, across), BF16)
        buffers[N_Z + name] = ((lines - 1, high, across), BF16)
    semaphores = dict(
        own_sem=(2,),
        load_sem=(5,),
        chunk_sem=(CHUNKS_HELD,),
    )
    for name in ("gl_send", "gl_recv", "gs_send", "gs_recv"):
        semaphores[name] = (len(PIECES), lines)
    for name in ("ss_send", "ss_recv", "sl_send", "sl_recv"):
        semaphores[name] = (len(TERMS), lines)
    for kind in ("send", "recv"):
        semaphores["rg_" + kind] = (len(RINGED), 2, count - 1)
        semaphores["rs_" + kind] = (len(RINGED), 2, count - 1)
        semaphores["sum_" + kind] = (len(SUMS), 3)
        semaphores["share_" + kind] = (len(SHARES), 3)
        semaphores["small_" + kind] = (2 + lines,)
    names = (*operands, *results, *buffers, *semaphores)
    held = ("out_h", "sg_h")
    done = pl.pallas_call(
        functools.partial(layer_kernel, names, z),
        out_shape=[jax.ShapeDtypeStruct(*item) for item in results.values()],
        in_specs=[pl.BlockSpec(memory_space=spaces[name]) for name in operands],
        out_specs=[
            pl.BlockSpec(memory_space=pl.ANY if name in held else pltpu.VMEM) for name in results
        ],
        scratch_shapes=[pltpu.VMEM(*item) for item in buffers.values()]
        + [pltpu.SemaphoreType.DMA(item) for item in semaphores.values()],
        compiler_params=pltpu.CompilerParams(
            collective_id=0, has_side_effects=True, vmem_limit_bytes=VMEM_LIMIT
        ),
    )(*operands.values())
    local = [
        ((rows, ROW_LEN, model), BF16),
        ((rows, ROW_LEN, model), F32),
        (self_qkv.shape, F32),
        (self_out.shape, F32),
        (cross_q.shape, F32),
        (cross_kv.shape, F32),
        (cross_out.shape, F32),
        (ffn_in.shape, F32),
        (ffn_in.shape, F32),
        (vectors.shape, F32),
        (head_bias.shape, F32),
        (ffn_bias.shape, F32),
        ((1, 4), F32),
    ]
    inside = pl.BlockSpec(memory_space=pltpu.VMEM)
    out_all, grad_all, *others, grad_down, grad_vectors, grad_heads, grad_hidden, rms = pl.pallas_call(
        finish_kernel,
        out_shape=[jax.ShapeDtypeStruct(*item) for item in local],
        in_specs=[inside] * len(done),
        out_specs=[inside] * len(local),
        compiler_params=pltpu.CompilerParams(vmem_limit_bytes=VMEM_LIMIT),
    )(*done)
    return (
        out_all.reshape(tokens, model),
        grad_all.reshape(tokens, model),
        *others,
        grad_down.transpose(0, 2, 1),
        grad_vectors,
        grad_heads,
        grad_hidden,
        rms.reshape(4),
    )


def layer_norm(values, gain_row, shift_row):
    row_mean = jnp.mean(values, axis=-1, keepdims=True)
    centred = values - row_mean
    row_var = jnp.mean(centred * centred, axis=-1, keepdims=True)
    return centred * lax.rsqrt(row_var + EPSILON) * gain_row + shift_row


def norm_back(values, gain_row, shift_row, grad_normed):
    pull_back = jax.vjp(layer_norm, values, gain_row, shift_row)[1]
    return pull_back(grad_normed)


def gelu_exact(values):
    return jax.nn.gelu(values, approximate=False)


def round_low(values):
    return values.astype(jnp.bfloat16)


def matmul(left_side, right_side):
    return jnp.dot(left_side, right_side, preferred_element_type=jnp.float32)


def matmul_left(left_side, right_side):
    return lax.dot_general(
        left_side, right_side, (((0,), (0,)), ((), ())), preferred_element_type=jnp.float32
    )


def matmul_right(left_side, right_side):
    return lax.dot_general(
        left_side, right_side, (((1,), (1,)), ((), ())), preferred_element_type=jnp.float32
    )


def column_sum(values):
    return jnp.sum(values.astype(jnp.float32), axis=0)


def attn_scores(queries, keys_in, key_mask):
    score_scale = queries.shape[-1] ** (-0.5)
    scores = (
        jnp.einsum("bqhe,bkhe->bhqk", queries, keys_in, preferred_element_type=jnp.float32)
        * score_scale
    )
    if key_mask is None:
        return scores
    return jnp.where(key_mask[:, None], scores, MASKED)


def attend(queries, keys_in, values_in, key_mask):
    scores = attn_scores(queries, keys_in, key_mask)
    row_max = jnp.max(scores, axis=-1, keepdims=True)
    exponent = jnp.exp(scores - row_max)
    row_total = jnp.sum(exponent, axis=-1, keepdims=True)
    attn_probs = round_low(exponent / row_total)
    mixed_out = jnp.einsum(
        "bhqk,bkhe->bqhe", attn_probs, values_in, preferred_element_type=jnp.float32
    )
    return (round_low(mixed_out), row_max + jnp.log(row_total))


def attend_back(queries, keys_in, values_in, key_mask, log_total, grad_mixed):
    score_scale = queries.shape[-1] ** (-0.5)
    attn_probs = jnp.exp(attn_scores(queries, keys_in, key_mask) - log_total)
    grad_values = jnp.einsum(
        "bhqk,bqhe->bkhe", round_low(attn_probs), grad_mixed, preferred_element_type=jnp.float32
    )
    grad_probs = jnp.einsum(
        "bqhe,bkhe->bhqk", grad_mixed, values_in, preferred_element_type=jnp.float32
    )
    row_delta = jnp.sum(attn_probs * grad_probs, axis=-1, keepdims=True)
    grad_scores = round_low(attn_probs * (grad_probs - row_delta))
    grad_queries = (
        jnp.einsum("bhqk,bkhe->bqhe", grad_scores, keys_in, preferred_element_type=jnp.float32)
        * score_scale
    )
    grad_keys = (
        jnp.einsum("bhqk,bqhe->bkhe", grad_scores, queries, preferred_element_type=jnp.float32)
        * score_scale
    )
    return (round_low(grad_queries), round_low(grad_keys), round_low(grad_values))


def heads_total(partial_terms):
    return lax.psum(partial_terms, N_MP)


def inputs_total(partial_terms):
    return lax.psum(partial_terms, N_MP)


def ffn_forward(normed_low, weight_up, bias_up, weight_down):
    up_value = matmul(normed_low, weight_up) + bias_up
    hidden = round_low(gelu_exact(up_value))
    return (up_value, hidden, matmul(hidden, weight_down))


def ffn_back(normed_low, up_value, hidden, weight_up, weight_down, grad_low):
    grad_down = matmul_left(hidden, grad_low)
    grad_hidden = matmul_right(grad_low, weight_down)
    grad_up = round_low(jax.vjp(gelu_exact, up_value)[1](grad_hidden)[0])
    grad_in = matmul_left(normed_low, grad_up)
    return (grad_in, grad_down, column_sum(grad_up), matmul_right(grad_up, weight_up))


def body(
    stream_in,
    features,
    image_index,
    text_segment,
    text_valid,
    self_qkv,
    self_out,
    cross_q,
    cross_kv,
    cross_out,
    ffn_in,
    ffn_out,
    vectors,
    head_bias,
    ffn_bias,
    out_grad,
):
    gathered = (
        lax.all_gather(self_qkv, N_DP, axis=1, tiled=True),
        lax.all_gather(self_out, N_DP, axis=1, tiled=True),
        lax.all_gather(cross_q, N_DP, axis=0, tiled=True),
        lax.all_gather(cross_kv, N_DP, axis=1, tiled=True),
        lax.all_gather(cross_out, N_DP, axis=1, tiled=True),
        lax.all_gather(ffn_in, N_DP, axis=1, tiled=True),
        lax.all_gather(ffn_out, N_DP, axis=2, tiled=True),
        lax.all_gather(vectors, N_DP, axis=1, tiled=True),
    )
    qkv_w, proj_w, cq_w, ckv_w, cproj_w, up_w, down_w, vector_low = gathered
    vecs = vector_low.astype(jnp.float32)
    bias_heads = head_bias.astype(jnp.float32)
    bias_hidden = ffn_bias.astype(jnp.float32)
    stream = stream_in.astype(jnp.float32)
    tokens, model_width = stream.shape
    row_count = tokens // ROW_LEN
    query_count = SLOTS * QUERIES
    text_len = ROW_LEN - query_count
    local_width = qkv_w.shape[2]
    local_heads = local_width // HEAD
    query_segment = jnp.arange(query_count, dtype=jnp.int32) // QUERIES
    segment = jnp.concatenate(
        [jnp.broadcast_to(query_segment, (row_count, query_count)), text_segment], axis=1
    )
    valid = (
        jnp.concatenate([jnp.ones((row_count, query_count), jnp.int32), text_valid], axis=1) == 1
    )
    key_mask = (segment[:, :, None] == segment[:, None, :]) & valid[:, None, :]
    heads_shape = (row_count, ROW_LEN, local_heads, HEAD)
    normed_low = round_low(layer_norm(stream, vecs[0], vecs[1]))
    self_query = round_low(matmul(normed_low, qkv_w[0]) + bias_heads[0]).reshape(heads_shape)
    self_key = round_low(matmul(normed_low, qkv_w[1])).reshape(heads_shape)
    self_value = round_low(matmul(normed_low, qkv_w[2]) + bias_heads[1]).reshape(heads_shape)
    self_mixed, self_total = attend(self_query, self_key, self_value, key_mask)
    self_mixed = self_mixed.reshape(tokens, local_width)
    self_term = matmul(self_mixed, proj_w).reshape(row_count, ROW_LEN, model_width)
    after_self = stream + heads_total(self_term.reshape(tokens, model_width)) + vecs[6]
    self_rows = after_self.reshape(row_count, ROW_LEN, model_width)
    query_part = self_rows[:, :query_count].reshape(-1, model_width)
    cross_normed = round_low(layer_norm(query_part, vecs[2], vecs[3]))
    slot_count = row_count * SLOTS
    cross_query = round_low(matmul(cross_normed, cq_w) + bias_heads[2]).reshape(
        slot_count, QUERIES, local_heads, HEAD
    )
    image_order = image_index.reshape(-1)
    pick_table = (image_order[:, None] == jnp.arange(image_order.shape[0])[None, :]).astype(
        jnp.bfloat16
    )
    keys_all = round_low(
        jnp.einsum("nkf,fc->nkc", features, ckv_w[0], preferred_element_type=jnp.float32)
    )
    values_all = round_low(
        jnp.einsum("nkf,fc->nkc", features, ckv_w[1], preferred_element_type=jnp.float32)
        + bias_heads[3]
    )
    cross_keys = round_low(
        jnp.einsum("ij,jkc->ikc", pick_table, keys_all, preferred_element_type=jnp.float32)
    )
    cross_values = round_low(
        jnp.einsum("ij,jkc->ikc", pick_table, values_all, preferred_element_type=jnp.float32)
    )
    cross_keys = cross_keys.reshape(slot_count, KEYS, local_heads, HEAD)
    cross_values = cross_values.reshape(slot_count, KEYS, local_heads, HEAD)
    cross_mixed, cross_total = attend(cross_query, cross_keys, cross_values, None)
    cross_mixed = cross_mixed.reshape(-1, local_width)
    cross_term = matmul(cross_mixed, cproj_w).reshape(row_count, query_count, model_width)
    after_query = query_part + heads_total(cross_term.reshape(-1, model_width)) + vecs[7]
    after_cross = jnp.concatenate(
        [after_query.reshape(row_count, query_count, model_width), self_rows[:, query_count:]],
        axis=1,
    ).reshape(tokens, model_width)
    ffn_normed = round_low(layer_norm(after_cross, vecs[4], vecs[5])).reshape(
        row_count, ROW_LEN, model_width
    )
    ffn_query = ffn_normed[:, :query_count].reshape(-1, model_width)
    ffn_text = ffn_normed[:, query_count:].reshape(-1, model_width)
    up_query, hidden_query, part_query = ffn_forward(ffn_query, up_w[0], bias_hidden[0], down_w[0])
    up_text, hidden_text, part_text = ffn_forward(ffn_text, up_w[1], bias_hidden[1], down_w[1])
    ffn_terms = jnp.concatenate(
        [
            part_query.reshape(row_count, query_count, model_width),
            part_text.reshape(row_count, text_len, model_width),
        ],
        axis=1,
    )
    query_flag = jnp.arange(ROW_LEN) < query_count
    bias_rows = jnp.where(query_flag[:, None], vecs[8], vecs[9])
    ffn_sum = heads_total(ffn_terms.reshape(tokens, model_width)).reshape(
        row_count, ROW_LEN, model_width
    )
    after_ffn = after_cross + (ffn_sum + bias_rows).reshape(tokens, model_width)
    token_weight = valid.reshape(-1).astype(jnp.float32)
    stream_stats = jnp.stack(
        [
            jnp.sum(token_weight * jnp.sum(section * section, axis=1))
            for section in (stream, after_self, after_cross, after_ffn)
        ]
        + [jnp.sum(token_weight)]
    )
    out_low = round_low(after_ffn)
    regathered = (
        lax.all_gather(self_qkv, N_DP, axis=1, tiled=True),
        lax.all_gather(self_out, N_DP, axis=1, tiled=True),
        lax.all_gather(cross_q, N_DP, axis=0, tiled=True),
        lax.all_gather(cross_kv, N_DP, axis=1, tiled=True),
        lax.all_gather(cross_out, N_DP, axis=1, tiled=True),
        lax.all_gather(ffn_in, N_DP, axis=1, tiled=True),
        lax.all_gather(ffn_out, N_DP, axis=2, tiled=True),
        lax.all_gather(vectors, N_DP, axis=1, tiled=True),
    )
    qkv_w, proj_w, cq_w, ckv_w, cproj_w, up_w, down_w, vector_low = regathered
    vecs = vector_low.astype(jnp.float32)
    grad_out = out_grad.astype(jnp.float32)
    grad_out_rows = grad_out.reshape(row_count, ROW_LEN, model_width)
    grad_low = round_low(grad_out_rows)
    grad_low_query = grad_low[:, :query_count].reshape(-1, model_width)
    grad_low_text = grad_low[:, query_count:].reshape(-1, model_width)
    in_query, down_query, hidden_bias_query, normed_grad_query = ffn_back(
        ffn_query, up_query, hidden_query, up_w[0], down_w[0], grad_low_query
    )
    in_text, down_text, hidden_bias_text, normed_grad_text = ffn_back(
        ffn_text, up_text, hidden_text, up_w[1], down_w[1], grad_low_text
    )
    normed_grad_q = normed_grad_query.reshape(row_count, query_count, model_width)
    normed_grad_t = normed_grad_text.reshape(row_count, text_len, model_width)
    normed_grad = jnp.concatenate([normed_grad_q, normed_grad_t], axis=1)
    normed_grad = inputs_total(normed_grad.reshape(tokens, model_width))
    cross_back, gain_three, shift_three = norm_back(after_cross, vecs[4], vecs[5], normed_grad)
    grad_cross = grad_out + cross_back
    grad_cross_rows = grad_cross.reshape(row_count, ROW_LEN, model_width)
    grad_branch_cross = round_low(grad_cross_rows[:, :query_count].reshape(-1, model_width))
    grad_cproj = matmul_left(cross_mixed, grad_branch_cross)
    grad_cross_mixed = round_low(matmul_right(grad_branch_cross, cproj_w)).reshape(
        cross_query.shape
    )
    grad_cq_part, grad_ck_part, grad_cv_part = attend_back(
        cross_query, cross_keys, cross_values, None, cross_total, grad_cross_mixed
    )
    grad_cq_part = grad_cq_part.reshape(-1, local_width)
    grad_ck_all = round_low(
        jnp.einsum(
            "ij,ikc->jkc",
            pick_table,
            grad_ck_part.reshape(-1, KEYS, local_width),
            preferred_element_type=jnp.float32,
        )
    )
    grad_cv_all = round_low(
        jnp.einsum(
            "ij,ikc->jkc",
            pick_table,
            grad_cv_part.reshape(-1, KEYS, local_width),
            preferred_element_type=jnp.float32,
        )
    )
    grad_ckv = jnp.stack(
        [
            jnp.einsum("nkf,nkc->fc", features, grad_ck_all, preferred_element_type=jnp.float32),
            jnp.einsum("nkf,nkc->fc", features, grad_cv_all, preferred_element_type=jnp.float32),
        ]
    )
    grad_cq = matmul_left(cross_normed, grad_cq_part)
    cross_grad_term = matmul_right(grad_cq_part, cq_w)
    cross_normed_grad = inputs_total(cross_grad_term)
    query_back, gain_two, shift_two = norm_back(query_part, vecs[2], vecs[3], cross_normed_grad)
    grad_self = jnp.concatenate(
        [
            grad_cross_rows[:, :query_count]
            + query_back.reshape(row_count, query_count, model_width),
            grad_cross_rows[:, query_count:],
        ],
        axis=1,
    ).reshape(tokens, model_width)
    grad_branch_self = round_low(grad_self)
    grad_proj = matmul_left(self_mixed, grad_branch_self)
    grad_self_mixed = round_low(matmul_right(grad_branch_self, proj_w)).reshape(heads_shape)
    grad_sq, grad_sk, grad_sv = attend_back(
        self_query, self_key, self_value, key_mask, self_total, grad_self_mixed
    )
    grad_sq = grad_sq.reshape(tokens, local_width)
    grad_sk = grad_sk.reshape(tokens, local_width)
    grad_sv = grad_sv.reshape(tokens, local_width)
    grad_qkv = jnp.stack(
        [
            matmul_left(normed_low, grad_sq),
            matmul_left(normed_low, grad_sk),
            matmul_left(normed_low, grad_sv),
        ]
    )
    self_grad_term = (
        matmul_right(grad_sq, qkv_w[0])
        + matmul_right(grad_sk, qkv_w[1])
        + matmul_right(grad_sv, qkv_w[2])
    )
    normed_grad_self = inputs_total(self_grad_term)
    stream_back, gain_one, shift_one = norm_back(stream, vecs[0], vecs[1], normed_grad_self)
    stream_grad = grad_self + stream_back
    norm_rows = jnp.stack([gain_one, shift_one, gain_two, shift_two, gain_three, shift_three])
    grad_vectors = jnp.concatenate(
        [
            norm_rows,
            jnp.stack(
                [
                    column_sum(grad_branch_self),
                    column_sum(grad_branch_cross),
                    column_sum(grad_low_query),
                    column_sum(grad_low_text),
                ]
            ),
        ]
    )
    grad_up = jnp.stack([in_query, in_text])
    grad_down = jnp.stack([down_query, down_text])
    owned = (
        lax.psum_scatter(grad_qkv, N_DP, scatter_dimension=1, tiled=True),
        lax.psum_scatter(grad_proj, N_DP, scatter_dimension=1, tiled=True),
        lax.psum_scatter(grad_cq, N_DP, scatter_dimension=0, tiled=True),
        lax.psum_scatter(grad_ckv, N_DP, scatter_dimension=1, tiled=True),
        lax.psum_scatter(grad_cproj, N_DP, scatter_dimension=1, tiled=True),
        lax.psum_scatter(grad_up, N_DP, scatter_dimension=1, tiled=True),
        lax.psum_scatter(grad_down, N_DP, scatter_dimension=2, tiled=True),
        lax.psum_scatter(grad_vectors, N_DP, scatter_dimension=1, tiled=True),
    )
    grad_heads = jnp.stack(
        [
            column_sum(grad_sq),
            column_sum(grad_sv),
            column_sum(grad_cq_part),
            jnp.sum(grad_cv_part.astype(jnp.float32), axis=(0, 1)).reshape(-1),
        ]
    )
    grad_hidden_bias = jnp.stack([hidden_bias_query, hidden_bias_text])
    grad_heads, grad_hidden_bias, stream_stats = lax.psum(
        (grad_heads, grad_hidden_bias, stream_stats), N_DP
    )
    stream_rms = jnp.sqrt(stream_stats[:4] / (stream_stats[4] * model_width))
    return (
        out_low,
        stream_grad,
        owned[0],
        owned[1],
        owned[2],
        owned[3],
        owned[4],
        owned[5],
        owned[6],
        owned[7],
        grad_heads,
        grad_hidden_bias,
        stream_rms,
    )


def solution(mesh):
    in_specs = (
        P(N_DP, None),
        P(N_DP, None, None),
        P(N_DP, None),
        P(N_DP, None),
        P(N_DP, None),
        P(None, N_DP, N_MP),
        P(N_MP, N_DP),
        P(N_DP, N_MP),
        P(None, N_DP, N_MP),
        P(N_MP, N_DP),
        P(None, N_DP, N_MP),
        P(None, N_MP, N_DP),
        P(None, N_DP),
        P(None, N_MP),
        P(None, N_MP),
        P(N_DP, None),
    )
    out_specs = (
        P(N_DP, None),
        P(N_DP, None),
        P(None, N_DP, N_MP),
        P(N_MP, N_DP),
        P(N_DP, N_MP),
        P(None, N_DP, N_MP),
        P(N_MP, N_DP),
        P(None, N_DP, N_MP),
        P(None, N_MP, N_DP),
        P(None, N_DP),
        P(None, N_MP),
        P(None, N_MP),
        P(),
    )

    def apply(*args):
        fan = args[5].shape[1] // mesh.shape[N_DP]
        whole_tiles = fan % 16 == 0 and fan <= 128 and mesh.shape[N_DP] % 2 == 0
        run = layer if whole_tiles and mesh.shape[N_MP] == 4 else body
        return jax.shard_map(
            run, mesh=mesh, in_specs=in_specs, out_specs=out_specs, check_vma=False
        )(*args)

    return apply
```
